32 devices in a mesh: fsdp: 8 (over z, y), rep: 4 (over x, core).
Axes of the slice: x: 2, y: 2, z: 4, core: 2. Of those that a mesh axis runs over, the one named last changes fastest.
Arguments:
- tokens: bfloat16 [32768, 768], P(('fsdp', 'rep')), may hold values from -6 to 6
- seq_ids: int32 [32, 1024], P(('fsdp', 'rep')), may hold values from 0 to 31, never falling along the last dimension, each value on 1 to 256 neighbouring positions
- key_mask: int32 [32, 1024], P(('fsdp', 'rep')), may hold values 0 or 1
- weight_query: bfloat16 [768, 768], P('fsdp'), may hold values from -0.21875 to 0.21875
- bias_query: bfloat16 [768], P('fsdp'), may hold values from -3 to 3
- weight_key: bfloat16 [768, 768], P('fsdp'), may hold values from -0.21875 to 0.21875
- weight_value: bfloat16 [768, 768], P('fsdp'), may hold values from -0.21875 to 0.21875
- bias_value: bfloat16 [768], P('fsdp'), may hold values from -3 to 3
- weight_out: bfloat16 [768, 768], P('fsdp'), may hold values from -0.625 to 0.625
- bias_out: bfloat16 [768], P('fsdp'), may hold values from -3 to 3
- norm1_gain: bfloat16 [768], P('fsdp'), may hold values from 0.5 to 1.5
- norm1_bias: bfloat16 [768], P('fsdp'), may hold values from -2 to 2
- weight_inner: bfloat16 [768, 3072], P('fsdp'), may hold values from -0.21875 to 0.21875
- bias_inner: bfloat16 [3072], P('fsdp'), may hold values from -3 to 3
- weight_outer: bfloat16 [3072, 768], P('fsdp'), may hold values from -0.109375 to 0.109375
- bias_outer: bfloat16 [768], P('fsdp'), may hold values from -2 to 2
- norm2_gain: bfloat16 [768], P('fsdp'), may hold values from 0.5 to 1.5
- norm2_bias: bfloat16 [768], P('fsdp'), may hold values from -2 to 2
- out_grad: bfloat16 [32768, 768], P(('fsdp', 'rep')), may hold values from -6 to 6
Outputs:
- layer_out: bfloat16 [32768, 768], P(('fsdp', 'rep'))
- grad_tokens: bfloat16 [32768, 768], P(('fsdp', 'rep'))
- grad_weight_query: float32 [768, 768], P('fsdp')
- grad_bias_query: float32 [768], P('fsdp')
- grad_weight_key: float32 [768, 768], P('fsdp')
- grad_weight_value: float32 [768, 768], P('fsdp')
- grad_bias_value: float32 [768], P('fsdp')
- grad_weight_out: float32 [768, 768], P('fsdp')
- grad_bias_out: float32 [768], P('fsdp')
- grad_norm1_gain: float32 [768], P('fsdp')
- grad_norm1_bias: float32 [768], P('fsdp')
- grad_weight_inner: float32 [768, 3072], P('fsdp')
- grad_bias_inner: float32 [3072], P('fsdp')
- grad_weight_outer: float32 [3072, 768], P('fsdp')
- grad_bias_outer: float32 [768], P('fsdp')
- grad_norm2_gain: float32 [768], P('fsdp')
- grad_norm2_bias: float32 [768], P('fsdp')
The draws below stay inside these ranges and needn't reach their ends.
Inputs may be any that keep to these rules, and one draw needn't show every extreme that they name: `seq_ids`: in each row of 1024 tokens the ids never fall, a sequence has at most min(256, 512) tokens, and one has exactly that many.
All inputs are finite; a program needn't handle non-finite values. No bound on the sum of `key_mask` on one device may be relied on, other than what follows from the above.
Results may differ from the reference program's by a relative error of at most 0.017.
Values may be sent and summed in bfloat16 or wider, within the bound.
No kernel may reach another device: no remote copies, remote signals or barrier semaphores. Data moves between devices by JAX's collectives and lax.ppermute only.
A program may use at most 320 MiB of HBM per device.

```python
import math
import jax
import jax.numpy as jnp
import numpy as np
from jax import lax

D = 768
HEADS = 12
DH = 64
FF = 3072
TOK_DEV = 1024
QBLOCK = 512
BLOCKS = 32
TOKENS = 32768


def touch_ends(drawn, stream_key, least, top_value):
    longest = drawn.shape.index(max(drawn.shape))
    spots = []
    for shift in (0, 1):
        where = [jax.random.randint(jax.random.fold_in(stream_key, axis), (), 0, length) for axis, length in enumerate(drawn.shape)]
        where[longest] = (where[longest] + shift) % drawn.shape[longest]
        spots.append(tuple(where))
    return drawn.at[spots[0]].set(least).at[spots[1]].set(top_value)


def levels(own_key, shape, pieces, smallest, top_value):
    def one(dim, blocks):
        draws = jax.random.uniform(jax.random.fold_in(jax.random.fold_in(own_key, 6), dim), (blocks,), jnp.float32, smallest / len(pieces), top_value / len(pieces))
        return jnp.repeat(jnp.exp(draws), shape[dim] // blocks).reshape((-1,) + (1,) * (len(shape) - dim - 1))

    level = one(*pieces[0])
    for cut in pieces[1:]:
        level = level * one(*cut)
    return level


def length_profile(count, total, reach, slope):
    weights = [(1 << 20) // math.isqrt(standing ** slope) + 1 for standing in range(2, count + 1)]
    rest, given = total - reach - (count - 1), [1] * (count - 1)
    while rest > 0:
        movable = [i for i in range(count - 1) if given[i] < reach]
        mass, budget = sum([weights[i] for i in movable]), rest
        for i in movable:
            extra = min(reach - given[i], max(1, budget * weights[i] // mass), rest)
            given[i] = given[i] + extra
            rest = rest - extra
    return np.array([reach] + given)


def uneven_parts(stream_key, number_of, total, bound, slope):
    if number_of == 2:
        one = jax.random.randint(stream_key, (), max(1, total - bound), min(bound, total - 1) + 1)
        return jnp.stack([one, total - one])
    tallies = jnp.asarray(length_profile(number_of, total, bound, slope), jnp.int32)
    twos = (number_of - 1) // 2
    source_of, receiver = tallies[1:1 + 2 * twos:2], tallies[2:2 + 2 * twos:2]
    margin = jnp.minimum(source_of - 1, bound - receiver)
    passed = jax.random.randint(jax.random.fold_in(stream_key, 1), (twos,), 0, 1 << 20) % (margin + 1)
    tallies = tallies.at[1:1 + 2 * twos:2].set(source_of - passed).at[2:2 + 2 * twos:2].set(receiver + passed)
    return tallies[jax.random.permutation(jax.random.fold_in(stream_key, 2), number_of)]


def noise(key, extent, deviation, most, split=(), kind=jnp.bfloat16):
    loudness = levels(key, extent, split, -0.22, 0.18) if split else 1.0
    drawn = jax.random.normal(key, extent, jnp.float32) * deviation * loudness
    return jnp.minimum(jnp.maximum(drawn, -most), most).astype(kind)


def setup_inputs(seed: int = 0) -> dict:
    key_list = jax.random.split(jax.random.key(seed), 20)
    tokens = noise(key_list[0], (TOKENS, D), 1.0, 6.0, ((0, 32),))
    seq_ids = jax.vmap(lambda own: jnp.searchsorted(jnp.cumsum(uneven_parts(own, max(4, TOK_DEV // 32), TOK_DEV, min(256, TOK_DEV // 2), 2)), jnp.arange(TOK_DEV), side="right"))(jax.random.split(key_list[1], BLOCKS)).reshape((BLOCKS, TOK_DEV)).astype(jnp.int32)
    key_mask = touch_ends((jax.random.randint(key_list[2], (BLOCKS, TOK_DEV), 0, 8) < 7).astype(jnp.int32), jax.random.fold_in(key_list[2], 1), 0, 1)
    weight_query = noise(key_list[3], (D, D), D ** -0.5, 0.21875, ((0, 8),))
    bias_query = noise(key_list[4], (D,), 0.5, 3.0, ((0, 8),))
    weight_key = noise(key_list[5], (D, D), D ** -0.5, 0.21875, ((0, 8),))
    weight_value = noise(key_list[6], (D, D), D ** -0.5, 0.21875, ((0, 8),))
    bias_value = noise(key_list[7], (D,), 0.5, 3.0, ((0, 8),))
    weight_out = noise(key_list[8], (D, D), (D // 8) ** -0.5, 0.625, ((0, 8),))
    bias_out = noise(key_list[9], (D,), 0.5, 3.0, ((0, 8),))
    norm1_gain = jnp.clip(1.0 + 0.1 * jax.random.normal(key_list[10], (D,), jnp.float32), 0.5, 1.5).astype(jnp.bfloat16)
    norm1_bias = noise(key_list[11], (D,), 0.3, 2.0, ((0, 8),))
    weight_inner = noise(key_list[12], (D, FF), D ** -0.5, 0.21875, ((0, 8),))
    bias_inner = noise(key_list[13], (FF,), 0.5, 3.0, ((0, 8),))
    weight_outer = noise(key_list[14], (FF, D), FF ** -0.5, 0.109375, ((0, 8),))
    bias_outer = noise(key_list[15], (D,), 0.3, 2.0, ((0, 8),))
    norm2_gain = jnp.clip(1.0 + 0.1 * jax.random.normal(key_list[16], (D,), jnp.float32), 0.5, 1.5).astype(jnp.bfloat16)
    norm2_bias = noise(key_list[17], (D,), 0.3, 2.0, ((0, 8),))
    out_grad = noise(key_list[18], (TOKENS, D), 1.0, 6.0, ((0, 32),))
    return dict(tokens=tokens, seq_ids=seq_ids, key_mask=key_mask, weight_query=weight_query, bias_query=bias_query, weight_key=weight_key, weight_value=weight_value, bias_value=bias_value, weight_out=weight_out, bias_out=bias_out, norm1_gain=norm1_gain, norm1_bias=norm1_bias, weight_inner=weight_inner, bias_inner=bias_inner, weight_outer=weight_outer, bias_outer=bias_outer, norm2_gain=norm2_gain, norm2_bias=norm2_bias, out_grad=out_grad)


@jax.custom_vjp
def low(v):
    return lax.optimization_barrier(v.astype(jnp.bfloat16)).astype(jnp.float32)

@jax.custom_vjp
def low_back(v):
    return v

def low_keep(v):
    return (low(v), None)

def low_pass(kept, grad):
    return (grad,)

def back_keep(v):
    return (v, None)

def back_low(kept, grad):
    return (low(grad),)
low.defvjp(low_keep, low_pass)
low_back.defvjp(back_keep, back_low)
HIGHEST_PRECISION = lax.Precision.HIGHEST
NEGATIVE = -1e+30
EPSILON = 1e-12

def matmul(left, right):
    return jnp.dot(left, right, precision=HIGHEST_PRECISION)

def normalize(hidden, gain, shift):
    center = hidden - lax.optimization_barrier(jnp.mean(hidden, axis=-1, keepdims=True))
    spread = lax.optimization_barrier(jnp.mean(center * center, axis=-1, keepdims=True))
    return center * lax.rsqrt(spread + EPSILON) * gain + shift

def layer_rows(params, rows, seq_row, mask_row):
    weight_query, bias_query, weight_key, weight_value, bias_value, weight_out, bias_out, norm1_gain, norm1_bias, weight_inner, bias_inner, weight_outer, bias_outer, norm2_gain, norm2_bias = params
    scale_factor = 1.0 / math.sqrt(DH)
    queries = low_back(low(matmul(rows, weight_query) + bias_query))
    keys_all = low_back(low(matmul(rows, weight_key)))
    values_all = low_back(low(matmul(rows, weight_value) + bias_value))
    key_heads = keys_all.reshape(TOK_DEV, HEADS, DH)
    value_heads = values_all.reshape(TOK_DEV, HEADS, DH)
    query_blocks = queries.reshape(TOK_DEV // QBLOCK, QBLOCK, HEADS, DH)
    seq_blocks = seq_row.reshape(TOK_DEV // QBLOCK, QBLOCK)
    offsets = jnp.arange(TOK_DEV // QBLOCK, dtype=jnp.int32) * QBLOCK
    positions = jnp.arange(TOK_DEV, dtype=jnp.int32)

    def attend(inputs):
        query_part, seq_part, offset = inputs
        query_pos = offset + jnp.arange(QBLOCK, dtype=jnp.int32)
        same_seq = seq_part[:, None] == seq_row[None, :]
        visible = (mask_row[None, :] == 1) | (query_pos[:, None] == positions[None, :])
        allowed = same_seq & visible
        scores = low_back(jnp.einsum('qhd,khd->hqk', query_part, key_heads, precision=HIGHEST_PRECISION) * scale_factor)
        scores = jnp.where(allowed[None], scores, NEGATIVE)
        probs = low(jax.nn.softmax(scores, axis=-1))
        mixed = jnp.einsum('hqk,khd->qhd', probs, value_heads, precision=HIGHEST_PRECISION)
        return mixed.reshape(QBLOCK, D)
    context = lax.map(jax.checkpoint(attend), (query_blocks, seq_blocks, offsets))
    context = low_back(low(context.reshape(TOK_DEV, D)))
    attended = low_back(matmul(context, weight_out) + bias_out)
    first = normalize(rows + attended, norm1_gain, norm1_bias)
    inner = low_back(matmul(low(first), weight_inner) + bias_inner)
    activated = low(jax.nn.gelu(inner, approximate=False))
    outer = low_back(matmul(activated, weight_outer) + bias_outer)
    return normalize(first + outer, norm2_gain, norm2_bias)

def reference(tokens, seq_ids, key_mask, weight_query, bias_query, weight_key, weight_value, bias_value, weight_out, bias_out, norm1_gain, norm1_bias, weight_inner, bias_inner, weight_outer, bias_outer, norm2_gain, norm2_bias, out_grad):
    params = tuple((item.astype(jnp.float32) for item in (weight_query, bias_query, weight_key, weight_value, bias_value, weight_out, bias_out, norm1_gain, norm1_bias, weight_inner, bias_inner, weight_outer, bias_outer, norm2_gain, norm2_bias)))
    rows_all = tokens.astype(jnp.float32).reshape(BLOCKS, TOK_DEV, D)

    def forward(params, rows_all):

        def advance(carry, inputs):
            rows, seq_row, mask_row = inputs
            return (carry, layer_rows(params, rows, seq_row, mask_row))
        _, outputs = lax.scan(advance, jnp.zeros((), jnp.float32), (rows_all, seq_ids, key_mask))
        return outputs
    result, pullback = jax.vjp(forward, params, rows_all)
    grad_params, grad_rows = pullback(out_grad.astype(jnp.float32).reshape(BLOCKS, TOK_DEV, D))
    layer_out = result.reshape(TOKENS, D).astype(jnp.bfloat16)
    grad_tokens = grad_rows.reshape(TOKENS, D).astype(jnp.bfloat16)
    return (layer_out, grad_tokens, grad_params[0], grad_params[1], grad_params[2], grad_params[3], grad_params[4], grad_params[5], grad_params[6], grad_params[7], grad_params[8], grad_params[9], grad_params[10], grad_params[11], grad_params[12], grad_params[13], grad_params[14])
```

```python
import functools
import math

import jax
import jax.numpy as jnp
from jax import lax
from jax.experimental import pallas as pl
from jax.experimental.pallas import tpu as pltpu
from jax.sharding import PartitionSpec as P

HEADS = 12
DH = 64
BF = jnp.bfloat16
F32 = jnp.float32
NEGATIVE = -1e30
EPSILON = 1e-12
QB = 128
KB = 128
SPAN = 5
ROWS = 256
VMEM = 60 * 1024 * 1024
ANY = pl.BlockSpec(memory_space=pl.ANY)


def dot(left, right):
    return jnp.dot(left, right, preferred_element_type=F32)


def dot_right(left, right):
    return lax.dot_general(left, right, (((1,), (1,)), ((), ())), preferred_element_type=F32)


def params(steps=1):
    return pltpu.CompilerParams(
        dimension_semantics=("arbitrary",) * steps, vmem_limit_bytes=VMEM
    )


def cost(flops, size):
    return pl.CostEstimate(flops=int(flops), bytes_accessed=int(size), transcendentals=0)


def struct(shape, dtype):
    return jax.ShapeDtypeStruct(shape, dtype)


def whole(shape):
    return pl.BlockSpec(shape, lambda i, s: (0,) * len(shape))


def rows_of(width, height=ROWS):
    return pl.BlockSpec((height, width), lambda i, s: (i, 0))


def norm(hidden):
    center = hidden - jnp.mean(hidden, axis=-1, keepdims=True)
    inverse = lax.rsqrt(jnp.mean(center * center, axis=-1, keepdims=True) + EPSILON)
    return center * inverse, inverse


def norm_back(grad, normed, inverse):
    mean = jnp.mean(grad, axis=-1, keepdims=True)
    along = jnp.mean(grad * normed, axis=-1, keepdims=True)
    return inverse * (grad - mean - normed * along)


def gelu_parts(inner):
    size = jnp.abs(inner)
    t = 1.0 / (1.0 + (0.3275911 * 0.7071067811865476) * size)
    decay = jnp.exp(-0.5 * inner * inner)
    poly = t * (
        0.254829592 + t * (-0.284496736 + t * (1.421413741 + t * (-1.453152027 + t * 1.061405429)))
    )
    tail = 0.5 * poly * decay
    phi = jnp.where(inner >= 0, 1.0 - tail, tail)
    return inner * phi, phi + inner * decay * 0.3989422804014327


def column_sum(value):
    return jnp.sum(value, axis=0, keepdims=True)


def windows(seq_row):
    tiles = seq_row.reshape(seq_row.shape[0] // QB, QB)
    below = jnp.sum((seq_row[None] < tiles[:, :1]).astype(jnp.int32), axis=1)
    upto = jnp.sum((seq_row[None] <= tiles[:, -1:]).astype(jnp.int32), axis=1)
    low = below // KB
    return jnp.concatenate([low, (upto + KB - 1) // KB - low])


def first_half(shape):
    return lax.broadcasted_iota(jnp.int32, shape, len(shape) - 1) < DH


def stack_pair(pair):
    low = first_half(pair.shape)
    zero = jnp.zeros_like(pair)
    return jnp.concatenate([jnp.where(low, pair, zero), jnp.where(low, zero, pair)], axis=0)


def fold_pair(both):
    half = both.shape[0] // 2
    return jnp.where(first_half((half, both.shape[1])), both[:half], both[half:])


def attend_kernel(win, seq_ref, mask_ref, q_ref, k_ref, v_ref, ctx_ref, p_ref, bias_ref):
    i = pl.program_id(0)
    low = win[i]
    count = win[pl.num_programs(0) + i]
    pairs = q_ref.shape[1] // (2 * DH)

    def body(n):
        w = n * KB
        base = pl.multiple_of(low * KB, KB)
        start = pl.multiple_of(i * QB, QB)
        own = jnp.broadcast_to(seq_ref[:, pl.ds(start, QB)], (QB, QB)).T
        rows = start + lax.broadcasted_iota(jnp.int32, (QB, KB), 0)
        for b in range(n):
            off = pl.multiple_of(base + b * KB, KB)
            cols = off + lax.broadcasted_iota(jnp.int32, (QB, KB), 1)
            visible = (mask_ref[:, pl.ds(off, KB)] == 1) | (rows == cols)
            allowed = (own == seq_ref[:, pl.ds(off, KB)]) & visible
            bias_ref[:, b * KB : (b + 1) * KB] = jnp.where(allowed, 0.0, NEGATIVE).astype(F32)
        for pair in range(pairs):
            lanes = slice(pair * 2 * DH, (pair + 1) * 2 * DH)
            bias = bias_ref[:, :w]
            scores = dot_right(stack_pair(q_ref[:, lanes]), k_ref[pl.ds(base, w), lanes])
            scores = scores + jnp.concatenate([bias, bias], axis=0)
            expon = jnp.exp(scores - jnp.max(scores, axis=1, keepdims=True))
            soft = expon * (1.0 / jnp.sum(expon, axis=1, keepdims=True))
            probs = soft.astype(BF)
            p_ref[0, pair, :, :w] = probs
            ctx_ref[:, lanes] = fold_pair(dot(probs, v_ref[pl.ds(base, w), lanes])).astype(BF)

    for n in range(1, SPAN + 1):
        pl.when(count == n)(functools.partial(body, n))


def attend(win, seq, mask, q, k, v):
    tok, d = q.shape
    tiles, pairs = tok // QB, d // (2 * DH)
    return pl.pallas_call(
        attend_kernel,
        grid_spec=pltpu.PrefetchScalarGridSpec(
            num_scalar_prefetch=1,
            grid=(tiles,),
            in_specs=[whole(seq.shape), whole(mask.shape), rows_of(d, QB), whole(k.shape), whole(v.shape)],
            out_specs=[
                rows_of(d, QB),
                pl.BlockSpec((1, pairs, 2 * QB, SPAN * KB), lambda i, s: (i, 0, 0, 0)),
            ],
            scratch_shapes=[pltpu.VMEM((QB, SPAN * KB), F32)],
        ),
        out_shape=[struct((tok, d), BF), struct((tiles, pairs, 2 * QB, SPAN * KB), BF)],
        compiler_params=params(),
        cost_estimate=cost(1.4e10, 2e7),
        name="attend",
    )(win, seq, mask, q, k, v)


def attend_back_kernel(
    win, q_ref, k_ref, v_ref, ctx_ref, do_ref, p_ref, dq_ref, dk_ref, dv_ref, bq_ref, bv_ref, dkt, dvt
):
    i = pl.program_id(0)
    low = win[i]
    count = win[pl.num_programs(0) + i]
    pairs = q_ref.shape[1] // (2 * DH)

    @pl.when(i == 0)
    def _():
        dkt[...] = jnp.zeros_like(dkt)
        dvt[...] = jnp.zeros_like(dvt)
        bq_ref[...] = jnp.zeros_like(bq_ref)

    def body(n):
        w = n * KB
        base = pl.multiple_of(low * KB, KB)
        for pair in range(pairs):
            lanes = slice(pair * 2 * DH, (pair + 1) * 2 * DH)
            grad = do_ref[:, lanes]
            do = stack_pair(grad)
            delta = jnp.sum(
                stack_pair(grad.astype(F32) * ctx_ref[:, lanes].astype(F32)), axis=1, keepdims=True
            )
            probs = p_ref[0, pair, :, :w]
            grad_probs = dot_right(do, v_ref[pl.ds(base, w), lanes])
            ds = (probs.astype(F32) * (grad_probs - delta)).astype(BF)
            dq = (fold_pair(dot(ds, k_ref[pl.ds(base, w), lanes])) * (1.0 / math.sqrt(DH))).astype(BF)
            dq_ref[:, lanes] = dq
            bq_ref[0:1, lanes] += column_sum(dq.astype(F32))
            dvt[lanes, pl.ds(base, w)] += dot(do.T, probs)
            dkt[lanes, pl.ds(base, w)] += dot(stack_pair(q_ref[:, lanes]).T, ds)

    for n in range(1, SPAN + 1):
        pl.when(count == n)(functools.partial(body, n))

    @pl.when(i == pl.num_programs(0) - 1)
    def _():
        bv_ref[...] = jnp.zeros_like(bv_ref)
        for o in range(0, k_ref.shape[0], QB):
            dk_ref[o : o + QB, :] = dkt[:, o : o + QB].T.astype(BF)
            dv = dvt[:, o : o + QB].T.astype(BF)
            dv_ref[o : o + QB, :] = dv
            bv_ref[0:1, :] += column_sum(dv.astype(F32))


def attend_back(win, q, k, v, ctx, do, p):
    tok, d = q.shape
    tiles, pairs = tok // QB, d // (2 * DH)
    row = rows_of(d, QB)
    return pl.pallas_call(
        attend_back_kernel,
        grid_spec=pltpu.PrefetchScalarGridSpec(
            num_scalar_prefetch=1,
            grid=(tiles,),
            in_specs=[
                row,
                whole(k.shape),
                whole(v.shape),
                row,
                row,
                pl.BlockSpec((1, pairs, 2 * QB, SPAN * KB), lambda i, s: (i, 0, 0, 0)),
            ],
            out_specs=[row, whole((tok, d)), whole((tok, d)), whole((8, d)), whole((8, d))],
            scratch_shapes=[pltpu.VMEM((d, tok), F32), pltpu.VMEM((d, tok), F32)],
        ),
        out_shape=[struct((tok, d), BF)] * 3 + [struct((8, d), F32)] * 2,
        compiler_params=params(),
        cost_estimate=cost(2e10, 2e7),
        name="attend_back",
    )(win, q, k, v, ctx, do, p)


class Weight:
    def __init__(self, shard, first):
        self.rows, self.width = shard.shape
        self.shard = shard
        self.first = first


class Group:
    def __init__(self, mesh, shards):
        self.fsdp = mesh.shape["fsdp"]
        self.fast = fast_path(mesh, shards)
        self.pieces = []
        self.weights = []
        first = 0
        for shard in shards:
            self.weights.append(Weight(shard, first))
            first += shard.size // (2 * PIECE)

    def full(self, k):
        weight = self.weights[k]
        return (weight.rows * (self.fsdp if self.fast else 1), weight.width)

    def payload(self, core):
        parts = []
        for weight in self.weights:
            half = lax.dynamic_slice_in_dim(weight.shard, core * (weight.rows // 2), weight.rows // 2, 0)
            parts += [half[:, c : c + PIECE] for c in range(0, weight.width, PIECE)]
        return jnp.concatenate(parts, axis=0)

    def operands(self, used):
        if not self.fast:
            return [self.weights[k].shard for k in used]
        return [self.weights[k].shard for k in used] + [array for array, _, _ in self.pieces]

    def load(self, used, table, refs, targets, sems):
        if not self.fast:
            for n, target in enumerate(targets):
                pltpu.make_async_copy(refs[n], target, sems.at[n]).start()
            return
        core = table[self.fsdp]
        for n, k in enumerate(used):
            weight, target, sem = self.weights[k], targets[n], sems.at[n]
            half = weight.rows // 2
            base = pl.multiple_of(table[0] * weight.rows, weight.rows)
            pltpu.make_async_copy(refs[n], target.at[pl.ds(base, weight.rows), :], sem).start()
            for piece, (_, sources, mate) in zip(refs[len(used) :], self.pieces):
                side = (1 - core) if mate else core
                height = piece.shape[0] // len(sources)
                for order, source in enumerate(sources):
                    row = pl.multiple_of(table[source] * weight.rows + side * half, 16)
                    for c in range(weight.width // PIECE):
                        start = order * height + weight.first + c * half
                        pltpu.make_async_copy(
                            piece.at[start : start + half, :],
                            target.at[pl.ds(row, half), c * PIECE : (c + 1) * PIECE],
                            sem,
                        ).start()

    def wait(self, targets, sems):
        for n, target in enumerate(targets):
            pltpu.make_async_copy(target, target, sems.at[n]).wait()

    def scratch(self, used):
        return [pltpu.VMEM(self.full(k), BF) for k in used] + [pltpu.SemaphoreType.DMA((len(used),))]


PIECE = 768


def fast_path(mesh, shards):
    return (
        mesh.shape["fsdp"] == 8
        and mesh.shape["rep"] == 4
        and all(s.shape[0] % 32 == 0 and s.shape[1] % PIECE == 0 for s in shards)
    )


RING = (0, 2, 4, 6, 7, 5, 3, 1)


def ring_table():
    size = len(RING)
    place = {v: p for p, v in enumerate(RING)}
    steps = list(range(0, -(size // 2) - 1, -1)) + list(range(1, size - size // 2))
    return [[RING[(place[f] + s) % size] for s in steps] for f in range(size)]


def ring_step(value, step):
    size = len(RING)
    return lax.ppermute(value, "fsdp", [(RING[p], RING[(p + step) % size]) for p in range(size)])


def rep_step(value, bits):
    return lax.ppermute(value, "rep", [(r, r ^ bits) for r in range(4)])


def pallas(body, name, grid, table, operands, in_specs, out_specs, outs, scratch, flops):
    size = sum(o.size * o.dtype.itemsize for o in list(operands) + list(outs))
    return pl.pallas_call(
        body,
        grid_spec=pltpu.PrefetchScalarGridSpec(
            num_scalar_prefetch=1, grid=grid, in_specs=in_specs, out_specs=out_specs, scratch_shapes=scratch
        ),
        out_shape=outs,
        compiler_params=params(len(grid)),
        cost_estimate=cost(flops, size),
        name=name,
    )(table, *operands)


def project(table, group, tokens, vectors):
    tok, d = tokens.shape
    used = (0, 1, 2)
    extra = group.operands(used)

    def body(s, x_ref, vec_ref, *refs):
        pieces, (q_ref, k_ref, v_ref, *weights, sems) = refs[: len(extra)], refs[len(extra) :]

        @pl.when(pl.program_id(0) == 0)
        def _():
            group.load(used, s, pieces, weights, sems)
            group.wait(weights, sems)

        x = x_ref[...]
        q = (dot(x, weights[0][...]) + vec_ref[0:1, :]).astype(BF)
        q_ref[...] = q * jnp.asarray(1.0 / math.sqrt(DH), BF)
        k_ref[...] = dot(x, weights[1][...]).astype(BF)
        v_ref[...] = (dot(x, weights[2][...]) + vec_ref[1:2, :]).astype(BF)

    return pallas(
        body,
        "project",
        (tok // ROWS,),
        table,
        [tokens, vectors] + extra,
        [rows_of(d), whole(vectors.shape)] + [ANY] * len(extra),
        [rows_of(d)] * 3,
        [struct((tok, d), BF)] * 3,
        group.scratch(used),
        6 * tok * d * d,
    )


def inner_block(table, group, context, tokens, vectors, bias_inner):
    tok, d = tokens.shape
    used = (0, 1)
    ff = group.full(1)[1]
    extra = group.operands(used)

    def body(s, ctx_ref, x_ref, vec_ref, bias_ref, *refs):
        pieces = refs[: len(extra)]
        hid_ref, low_ref, act_ref, slope_ref, w_out, w_in, sems = refs[len(extra) :]

        @pl.when(pl.program_id(0) == 0)
        def _():
            group.load(used, s, pieces, (w_out, w_in), sems)
            group.wait((w_out, w_in), sems)

        hidden = x_ref[...].astype(F32) + dot(ctx_ref[...], w_out[...]) + vec_ref[2:3, :]
        hid_ref[...] = hidden
        normed, _ = norm(hidden)
        low = (normed * vec_ref[3:4, :] + vec_ref[4:5, :]).astype(BF)
        low_ref[...] = low
        for c in range(0, ff, d):
            act, slope = gelu_parts(dot(low, w_in[:, c : c + d]) + bias_ref[0:1, c : c + d])
            act_ref[:, c : c + d] = act.astype(BF)
            slope_ref[:, c : c + d] = slope.astype(BF)

    return pallas(
        body,
        "inner_block",
        (tok // ROWS,),
        table,
        [context, tokens, vectors, bias_inner] + extra,
        [rows_of(d), rows_of(d), whole(vectors.shape), whole(bias_inner.shape)] + [ANY] * len(extra),
        [rows_of(d), rows_of(d), rows_of(ff), rows_of(ff)],
        [struct((tok, d), F32), struct((tok, d), BF), struct((tok, ff), BF), struct((tok, ff), BF)],
        group.scratch(used),
        2 * tok * d * (d + ff),
    )


def outer_block(table, group, activated, hidden, out_grad, vectors):
    tok, d = hidden.shape
    ff = activated.shape[1]
    used = (0,)
    extra = group.operands(used)

    def body(s, act_ref, hid_ref, g_ref, vec_ref, *refs):
        pieces = refs[: len(extra)]
        out_ref, second_ref, low_ref, sum_ref, w_outer, sems = refs[len(extra) :]

        @pl.when(pl.program_id(0) == 0)
        def _():
            group.load(used, s, pieces, (w_outer,), sems)
            sum_ref[...] = jnp.zeros_like(sum_ref)
            group.wait((w_outer,), sems)

        normed, _ = norm(hid_ref[...])
        first = normed * vec_ref[3:4, :] + vec_ref[4:5, :]
        normed, inverse = norm(first + dot(act_ref[...], w_outer[...]) + vec_ref[5:6, :])
        gain = vec_ref[6:7, :]
        out_ref[...] = (normed * gain + vec_ref[7:8, :]).astype(BF)
        grad = g_ref[...].astype(F32)
        second = norm_back(grad * gain, normed, inverse)
        second_ref[...] = second
        low = second.astype(BF)
        low_ref[...] = low
        sum_ref[0:1, :] += column_sum(grad * normed)
        sum_ref[1:2, :] += column_sum(grad)
        sum_ref[2:3, :] += column_sum(low.astype(F32))

    return pallas(
        body,
        "outer_block",
        (tok // ROWS,),
        table,
        [activated, hidden, out_grad, vectors] + extra,
        [rows_of(ff), rows_of(d), rows_of(d), whole(vectors.shape)] + [ANY] * len(extra),
        [rows_of(d), rows_of(d), rows_of(d), whole((8, d))],
        [struct((tok, d), BF), struct((tok, d), F32), struct((tok, d), BF), struct((8, d), F32)],
        group.scratch(used),
        2 * tok * d * ff,
    )


def active_back(table, group, grad_low, slope):
    tok, d = grad_low.shape
    ff = slope.shape[1]
    used = (0,)
    extra = group.operands(used)

    def body(s, g_ref, slope_ref, *refs):
        pieces = refs[: len(extra)]
        out_ref, sum_ref, w_outer, sems = refs[len(extra) :]

        @pl.when(pl.program_id(0) == 0)
        def _():
            group.load(used, s, pieces, (w_outer,), sems)
            sum_ref[...] = jnp.zeros_like(sum_ref)
            group.wait((w_outer,), sems)

        g = g_ref[...]
        for c in range(0, ff, d):
            low = (dot_right(g, w_outer[c : c + d, :]) * slope_ref[:, c : c + d].astype(F32)).astype(BF)
            out_ref[:, c : c + d] = low
            sum_ref[0:1, c : c + d] += column_sum(low.astype(F32))

    return pallas(
        body,
        "active_back",
        (tok // ROWS,),
        table,
        [grad_low, slope] + extra,
        [rows_of(d), rows_of(ff)] + [ANY] * len(extra),
        [rows_of(ff), whole((8, ff))],
        [struct((tok, ff), BF), struct((8, ff), F32)],
        group.scratch(used),
        2 * tok * d * ff,
    )


def inner_back(table, group, grad_inner, grad_second, hidden, vectors):
    tok, d = hidden.shape
    ff = grad_inner.shape[1]
    used = (0, 1)
    extra = group.operands(used)

    def body(s, g_ref, second_ref, hid_ref, vec_ref, *refs):
        pieces = refs[: len(extra)]
        out_ref, low_ref, ctx_ref, sum_ref, w_out, w_in, sems = refs[len(extra) :]

        @pl.when(pl.program_id(0) == 0)
        def _():
            group.load(used, s, pieces, (w_out, w_in), sems)
            sum_ref[...] = jnp.zeros_like(sum_ref)
            group.wait((w_out, w_in), sems)

        grad = second_ref[...] + dot_right(g_ref[...], w_in[...])
        normed, inverse = norm(hid_ref[...])
        hidden_grad = norm_back(grad * vec_ref[3:4, :], normed, inverse)
        out_ref[...] = hidden_grad
        low = hidden_grad.astype(BF)
        low_ref[...] = low
        ctx_ref[...] = dot_right(low, w_out[...]).astype(BF)
        sum_ref[0:1, :] += column_sum(grad * normed)
        sum_ref[1:2, :] += column_sum(grad)
        sum_ref[2:3, :] += column_sum(low.astype(F32))

    return pallas(
        body,
        "inner_back",
        (tok // ROWS,),
        table,
        [grad_inner, grad_second, hidden, vectors] + extra,
        [rows_of(ff), rows_of(d), rows_of(d), whole(vectors.shape)] + [ANY] * len(extra),
        [rows_of(d), rows_of(d), rows_of(d), whole((8, d))],
        [struct((tok, d), F32), struct((tok, d), BF), struct((tok, d), BF), struct((8, d), F32)],
        group.scratch(used),
        2 * tok * d * (d + ff),
    )


def tokens_back(table, group, grad_hidden, grads):
    tok, d = grad_hidden.shape
    used = (0, 1, 2)
    extra = group.operands(used)

    def body(s, hid_ref, q_ref, k_ref, v_ref, *refs):
        pieces, (out_ref, *weights, sems) = refs[: len(extra)], refs[len(extra) :]

        @pl.when(pl.program_id(0) == 0)
        def _():
            group.load(used, s, pieces, weights, sems)
            group.wait(weights, sems)

        total = hid_ref[...]
        for ref, weight in zip((q_ref, k_ref, v_ref), weights):
            total = total + dot_right(ref[...], weight[...])
        out_ref[...] = total.astype(BF)

    return pallas(
        body,
        "tokens_back",
        (tok // ROWS,),
        table,
        [grad_hidden, *grads] + extra,
        [rows_of(d)] * 4 + [ANY] * len(extra),
        [rows_of(d)],
        [struct((tok, d), BF)],
        group.scratch(used),
        6 * tok * d * d,
    )[0]


BLOCK = 384


def weight_grad(choice, side, left, rights, owner_rows, received=None, order=None):
    tok, m = left.shape
    halves = [r.shape[1] // 2 for r in rights]
    n = sum(halves)
    count = len(rights)
    per = BLOCK // owner_rows
    flops = 2 * tok * m * n

    def product(left_ref, right_refs):
        right = jnp.concatenate([r[...] for r in right_refs], axis=1)
        return dot(left_ref[...].T, right)

    in_specs = [pl.BlockSpec((tok, BLOCK), lambda i, s: (0, i))] + [
        pl.BlockSpec((tok, h), lambda i, s: (0, s[0] if side == 0 else 1 - s[0])) for h in halves
    ]
    if received is None:

        def body(s, left_ref, *refs):
            refs[count][...] = product(left_ref, refs[:count]).astype(BF)

        return pallas(
            body,
            "weight_grad",
            (m // BLOCK,),
            choice,
            [left, *rights],
            in_specs,
            [pl.BlockSpec((BLOCK, n), lambda i, s: (i, 0))],
            [struct((m, n), BF)],
            [],
            flops,
        )[0]

    paired = order == "y" and per == 1

    def body(s, left_ref, *refs):
        add_ref, keep_ref, send_ref = refs[count:]
        total = (product(left_ref, refs[:count]) + add_ref[...].astype(F32)).astype(BF)
        if paired:
            mine = (pl.program_id(0) % 2) == s[2]

            @pl.when(mine)
            def _():
                keep_ref[...] = total

            @pl.when(jnp.logical_not(mine))
            def _():
                send_ref[...] = total

            return
        shape = (per, 2, owner_rows // 2, n) if order == "x" else (per // 2, 2, owner_rows, n)
        parts = total.reshape(shape)
        bit = s[1] if order == "x" else s[2]
        low, high = parts[:, 0].reshape(BLOCK // 2, n), parts[:, 1].reshape(BLOCK // 2, n)
        keep_ref[...] = jnp.where(bit == 0, low, high)
        send_ref[...] = jnp.where(bit == 0, high, low)

    if paired:
        out_spec = pl.BlockSpec((BLOCK, n), lambda i, s: (i // 2, 0))
    else:
        out_spec = pl.BlockSpec((BLOCK // 2, n), lambda i, s: (i, 0))
    return pallas(
        body,
        "weight_grad_sum",
        (m // BLOCK,),
        choice,
        [left, *rights, received],
        in_specs + [pl.BlockSpec((BLOCK, n), lambda i, s: (i, 0))],
        [out_spec] * 2,
        [struct((m // 2, n), BF)] * 2,
        [],
        flops,
    )


def axis_step(value, axis):
    if axis == "x":
        return rep_step(value, 2)
    return lax.ppermute(value, "fsdp", [(f, f ^ 1) for f in range(8)])


def added(keep, received):
    return (keep.astype(F32) + received.astype(F32)).astype(BF)


class Reduce:
    def __init__(self, place, left, rights, owner_rows, order):
        self.place, self.left, self.rights = place, left, rights
        self.rows, self.order = owner_rows, order
        self.widths = [r.shape[1] for r in rights]
        self.n = sum(self.widths) // 2

    def core(self):
        other = weight_grad(self.place.choice, 1, self.left, self.rights, self.rows)
        self.received = rep_step(other, 1)

    def first(self):
        keep, send = weight_grad(
            self.place.choice, 0, self.left, self.rights, self.rows, self.received, self.order
        )
        self.keep, self.received = keep, axis_step(send, self.order)

    def second(self):
        total = added(self.keep, self.received)
        if self.order == "x":
            parts, bit, last = total.reshape(4, 2, self.rows // 2, self.n), self.place.y, "y"
        else:
            parts, bit, last = total.reshape(4, 2, self.rows // 2, self.n), self.place.x, "x"
        self.keep = lax.dynamic_index_in_dim(parts, bit, 1, keepdims=False)
        self.received = axis_step(lax.dynamic_index_in_dim(parts, 1 - bit, 1, keepdims=False), last)

    def third(self):
        parts = added(self.keep, self.received)
        z = self.place.z
        chunk = lambda k: lax.dynamic_index_in_dim(parts, (z + k) % 4, 0, keepdims=False)
        moved = [
            lax.ppermute(chunk(k), "fsdp", [(f, (f // 2 + k) % 4 * 2 + f % 2) for f in range(8)])
            for k in (1, 2, 3)
        ]
        total = chunk(0).astype(F32)
        for part in moved:
            total = total + part.astype(F32)
        self.own = total.astype(BF)

    def last(self):
        own = self.own
        others = [rep_step(own, bits) for bits in (1, 2, 3)]
        core, x = self.place.core, self.place.x

        def wide(mine, mate):
            outs, start = [], 0
            for width in self.widths:
                a, b = mine[:, start : start + width // 2], mate[:, start : start + width // 2]
                outs.append(jnp.where(core == 0, jnp.concatenate([a, b], 1), jnp.concatenate([b, a], 1)))
                start += width // 2
            return outs

        here, there = wide(own, others[0]), wide(others[1], others[2])
        return [
            jnp.where(x == 0, jnp.concatenate([a, b], 0), jnp.concatenate([b, a], 0)).astype(F32)
            for a, b in zip(here, there)
        ]


class Place:
    def __init__(self, mesh):
        f, r = lax.axis_index("fsdp"), lax.axis_index("rep")
        self.f, self.core, self.x = f, r % 2, r // 2
        self.y, self.z = f % 2, f // 2
        self.choice = jnp.stack([self.core, self.x, self.y]).astype(jnp.int32)
        if mesh.shape["fsdp"] == len(RING):
            row = lax.dynamic_index_in_dim(jnp.array(ring_table(), jnp.int32), f, 0, keepdims=False)
            self.table = jnp.concatenate([row, self.core[None].astype(jnp.int32)])
        else:
            self.table = jnp.zeros((1,), jnp.int32)


def plain_gather(mesh, shards):
    return Group(mesh, [lax.all_gather(s, "fsdp", axis=0, tiled=True) for s in shards])


def ring_gather(groups, core):
    half = len(RING) // 2
    for group in groups:
        up = down = group.payload(core)
        for step in range(1, half + 1):
            up = ring_step(up, 1)
            group.pieces.append((up, (step,), False))
            group.pieces.append((rep_step(up, 1), (step,), True))
            if step < half:
                down = ring_step(down, -1)
                group.pieces.append((down, (half + step,), False))
                group.pieces.append((rep_step(down, 1), (half + step,), True))


def local(mesh, *args):
    (
        tokens, seq_ids, key_mask, weight_query, bias_query, weight_key, weight_value, bias_value,
        weight_out, bias_out, norm1_gain, norm1_bias, weight_inner, bias_inner, weight_outer, bias_outer,
        norm2_gain, norm2_bias, out_grad,
    ) = args
    place = Place(mesh)
    table = place.table
    fsdp = mesh.shape["fsdp"]
    d = tokens.shape[1]
    win = windows(seq_ids[0])
    shards = [[weight_query, weight_key, weight_value], [weight_out, weight_inner], [weight_outer]]
    fast = all(fast_path(mesh, s) for s in shards)
    if fast:
        groups = [Group(mesh, s) for s in shards]
        ring_gather(groups, place.core)
    else:
        groups = [plain_gather(mesh, s) for s in shards]
    qkv, inner_group, outer_group = groups
    narrow = [bias_query, bias_value, bias_out, norm1_gain, norm1_bias, bias_outer, norm2_gain, norm2_bias]
    small = lax.all_gather(jnp.concatenate(narrow + [bias_inner]), "fsdp", axis=0, tiled=False)
    split = len(narrow) * (d // fsdp)
    vectors = small[:, :split].reshape(fsdp, len(narrow), d // fsdp).transpose(1, 0, 2).reshape(len(narrow), d)
    vectors = vectors.astype(F32)
    full_bias_inner = jnp.broadcast_to(small[:, split:].reshape(1, -1), (8, bias_inner.size * fsdp)).astype(F32)

    q, k, v = project(table, qkv, tokens, vectors)
    context, probs = attend(win, seq_ids, key_mask, q, k, v)
    hidden, first_low, activated, slope = inner_block(table, inner_group, context, tokens, vectors, full_bias_inner)
    layer_out, grad_second, grad_outer, sums2 = outer_block(
        table, outer_group, activated, hidden, out_grad, vectors
    )
    outer_sum = Reduce(place, activated, [grad_outer], weight_outer.shape[0], "x")
    if fast:
        outer_sum.core()
    grad_inner, sums_inner = active_back(table, outer_group, grad_outer, slope)
    inner_sum = Reduce(place, first_low, [grad_inner], weight_inner.shape[0], "y")
    if fast:
        outer_sum.first()
        inner_sum.core()
    grad_hidden, grad_att, grad_context, sums1 = inner_back(
        table, inner_group, grad_inner, grad_second, hidden, vectors
    )
    out_sum = Reduce(place, context, [grad_att], weight_out.shape[0], "y")
    if fast:
        inner_sum.first()
        outer_sum.second()
        out_sum.core()
        out_sum.first()
        inner_sum.second()
    dq, dk, dv, sum_q, sum_v = attend_back(win, q, k, v, context, grad_context, probs)
    query_sum = Reduce(place, tokens, [dq, dk, dv], weight_query.shape[0], "x")
    if fast:
        outer_sum.third()
        inner_sum.third()
        out_sum.second()
        query_sum.core()
    grad_tokens = tokens_back(table, qkv, grad_hidden, (dq, dk, dv))
    sums = jnp.concatenate(
        [sum_q[0], sum_v[0], sums1[2], sums1[0], sums1[1], sums_inner[0], sums2[2], sums2[0], sums2[1]]
    )
    sums = lax.psum(sums, ("fsdp", "rep"))
    if fast:
        query_sum.first()
        out_sum.third()
        query_sum.second()
        query_sum.third()
        (final_outer,), (final_inner,), (final_out,) = outer_sum.last(), inner_sum.last(), out_sum.last()
        final_query, final_key, final_value = query_sum.last()
    else:

        def plain(left, right):
            halves = [
                weight_grad(jnp.zeros((3,), jnp.int32), side, left, [right], left.shape[1] // 8)
                for side in (0, 1)
            ]
            owned = lax.psum_scatter(jnp.concatenate(halves, 1), "fsdp", scatter_dimension=0, tiled=True)
            return lax.psum(owned, "rep").astype(F32)

        final_outer = plain(activated, grad_outer)
        final_inner = plain(first_low, grad_inner)
        final_out = plain(context, grad_att)
        final_query, final_key, final_value = (plain(tokens, g) for g in (dq, dk, dv))

    starts = [0]
    for width in (d, d, d, d, d, bias_inner.size * fsdp, d, d, d):
        starts.append(starts[-1] + width)
    owned = [
        lax.dynamic_slice_in_dim(sums, a + place.f * ((b - a) // fsdp), (b - a) // fsdp, 0)
        for a, b in zip(starts[:-1], starts[1:])
    ]
    return (
        layer_out,
        grad_tokens,
        final_query,
        owned[0],
        final_key,
        final_value,
        owned[1],
        final_out,
        owned[2],
        owned[3],
        owned[4],
        final_inner,
        owned[5],
        final_outer,
        owned[6],
        owned[7],
        owned[8],
    )


def solution(mesh):
    rows, shard, part = P(("fsdp", "rep"), None), P("fsdp", None), P("fsdp")
    return jax.shard_map(
        functools.partial(local, mesh),
        mesh=mesh,
        in_specs=(
            rows, rows, rows, shard, part, shard, shard, part, shard, part, part, part, shard, part, shard,
            part, part, part, rows,
        ),
        out_specs=(
            rows, rows, shard, part, shard, shard, part, shard, part, part, part, shard, part, shard, part,
            part, part,
        ),
        check_vma=False,
    )
```

```python
import functools
import math

import jax
import jax.numpy as jnp
from jax import lax
from jax.experimental import pallas as pl
from jax.experimental.pallas import tpu as pltpu
from jax.sharding import PartitionSpec as P

HEADS = 12
DH = 64
BF = jnp.bfloat16
F32 = jnp.float32
NEGATIVE = -1e30
EPSILON = 1e-12
QB = 128
KB = 128
SPAN = 5
ROWS = 1024
VMEM = 60 * 1024 * 1024
COST = 0.05
ANY = pl.BlockSpec(memory_space=pl.ANY)


def dot(left, right):
    return jnp.dot(left, right, preferred_element_type=F32)


def dot_right(left, right):
    return lax.dot_general(left, right, (((1,), (1,)), ((), ())), preferred_element_type=F32)


def params(steps=1):
    return pltpu.CompilerParams(
        dimension_semantics=("arbitrary",) * steps, vmem_limit_bytes=VMEM
    )


def cost(flops, size):
    return pl.CostEstimate(flops=int(flops * COST), bytes_accessed=int(size * COST), transcendentals=0)


def struct(shape, dtype):
    return jax.ShapeDtypeStruct(shape, dtype)


def whole(shape):
    return pl.BlockSpec(shape, lambda i, s: (0,) * len(shape))


def rows_of(width, height=ROWS):
    return pl.BlockSpec((height, width), lambda i, s: (i, 0))


def norm(hidden):
    center = hidden - jnp.mean(hidden, axis=-1, keepdims=True)
    inverse = lax.rsqrt(jnp.mean(center * center, axis=-1, keepdims=True) + EPSILON)
    return center * inverse, inverse


def norm_back(grad, normed, inverse):
    mean = jnp.mean(grad, axis=-1, keepdims=True)
    along = jnp.mean(grad * normed, axis=-1, keepdims=True)
    return inverse * (grad - mean - normed * along)


def gelu_parts(inner):
    phi = 0.5 + 0.5 * lax.erf(inner * 0.7071067811865476)
    density = jnp.exp((-0.5 * inner) * inner) * 0.3989422804014327
    return inner * phi, phi + inner * density


def column_sum(value):
    return jnp.sum(value, axis=0, keepdims=True)


def windows(seq_row):
    tiles = seq_row.reshape(seq_row.shape[0] // QB, QB)
    below = jnp.sum((seq_row[None] < tiles[:, :1]).astype(jnp.int32), axis=1)
    upto = jnp.sum((seq_row[None] <= tiles[:, -1:]).astype(jnp.int32), axis=1)
    low = below // KB
    return jnp.concatenate([low, (upto + KB - 1) // KB - low])


def first_half(shape):
    return lax.broadcasted_iota(jnp.int32, shape, len(shape) - 1) < DH


def stack_pair(pair):
    low = first_half(pair.shape)
    zero = jnp.zeros_like(pair)
    return jnp.concatenate([jnp.where(low, pair, zero), jnp.where(low, zero, pair)], axis=0)


def fold_pair(both):
    half = both.shape[0] // 2
    return jnp.where(first_half((half, both.shape[1])), both[:half], both[half:])


def attend_kernel(win, seq_ref, mask_ref, q_ref, k_ref, v_ref, ctx_ref, p_ref, bias_ref, s_ref):
    i = pl.program_id(0)
    low = win[i]
    count = win[pl.num_programs(0) + i]
    pairs = q_ref.shape[1] // (2 * DH)

    def body(n):
        w = n * KB
        base = pl.multiple_of(low * KB, KB)
        start = pl.multiple_of(i * QB, QB)
        for pair in range(pairs):
            lanes = slice(pair * 2 * DH, (pair + 1) * 2 * DH)
            s_ref[pair, :, :w] = dot_right(stack_pair(q_ref[:, lanes]), k_ref[pl.ds(base, w), lanes])
        own = jnp.broadcast_to(seq_ref[:, pl.ds(start, QB)], (QB, QB)).T
        rows = start + lax.broadcasted_iota(jnp.int32, (QB, KB), 0)
        for b in range(n):
            off = pl.multiple_of(base + b * KB, KB)
            cols = off + lax.broadcasted_iota(jnp.int32, (QB, KB), 1)
            visible = (mask_ref[:, pl.ds(off, KB)] == 1) | (rows == cols)
            allowed = (own == seq_ref[:, pl.ds(off, KB)]) & visible
            bias_ref[:, b * KB : (b + 1) * KB] = jnp.where(allowed, 0.0, NEGATIVE).astype(F32)
        ones = jnp.ones((w, 2 * DH), BF)
        for group in range(0, pairs, GROUP):
            expons = []
            for pair in range(group, group + GROUP):
                lanes = slice(pair * 2 * DH, (pair + 1) * 2 * DH)
                bias = bias_ref[:, :w]
                scores = s_ref[pair, :, :w] + jnp.concatenate([bias, bias], axis=0)
                expons.append(jnp.exp(scores - jnp.max(scores, axis=1, keepdims=True)).astype(BF))
            for pair in range(group, group + GROUP):
                lanes = slice(pair * 2 * DH, (pair + 1) * 2 * DH)
                expon = expons[pair - group]
                mixed = dot(expon, jnp.concatenate([v_ref[pl.ds(base, w), lanes], ones], axis=1))
                scale = 1.0 / mixed[:, 2 * DH :]
                ctx_ref[:, lanes] = fold_pair(mixed[:, : 2 * DH] * scale).astype(BF)
                for b in range(n):
                    p_ref[0, pair, :, b * KB : (b + 1) * KB] = (
                        expon[:, b * KB : (b + 1) * KB].astype(F32) * scale
                    ).astype(BF)

    for n in range(1, SPAN + 1):
        pl.when(count == n)(functools.partial(body, n))


GROUP = 6


def attend(win, seq, mask, q, k, v):
    tok, d = q.shape
    tiles, pairs = tok // QB, d // (2 * DH)
    return pl.pallas_call(
        attend_kernel,
        grid_spec=pltpu.PrefetchScalarGridSpec(
            num_scalar_prefetch=1,
            grid=(tiles,),
            in_specs=[whole(seq.shape), whole(mask.shape), rows_of(d, QB), whole(k.shape), whole(v.shape)],
            out_specs=[
                rows_of(d, QB),
                pl.BlockSpec((1, pairs, 2 * QB, SPAN * KB), lambda i, s: (i, 0, 0, 0)),
            ],
            scratch_shapes=[pltpu.VMEM((QB, SPAN * KB), F32), pltpu.VMEM((pairs, 2 * QB, SPAN * KB), F32)],
        ),
        out_shape=[struct((tok, d), BF), struct((tiles, pairs, 2 * QB, SPAN * KB), BF)],
        compiler_params=params(),
        cost_estimate=cost(1.4e10, 2e7),
        name="attend",
    )(win, seq, mask, q, k, v)


def attend_back(place_win, side, q, k, v, ctx, do, p, tokens, out_grad):
    tok, d = q.shape
    half = d // 2
    tiles, pairs = tok // QB, half // (2 * DH)
    pick = (lambda s: s[0]) if side == 0 else (lambda s: 1 - s[0])
    row = pl.BlockSpec((QB, half), lambda i, s: (i, pick(s)))
    cols = pl.BlockSpec((tok, half), lambda i, s: (0, pick(s)))

    def kernel(s, q_ref, k_ref, v_ref, ctx_ref, do_ref, p_ref, x_ref, out_grad_ref, grad_ref, sum_ref, w_ref, dkt, dvt, s_ref):
        i = pl.program_id(0)
        low, count = s[3 + i], s[3 + tiles + i]
        start = pl.multiple_of(i * QB, QB)

        @pl.when(i == 0)
        def _():
            dkt[...] = jnp.zeros_like(dkt)
            dvt[...] = jnp.zeros_like(dvt)
            sum_ref[...] = jnp.zeros_like(sum_ref)

        def body(n):
            w = n * KB
            base = pl.multiple_of(low * KB, KB)
            lanes = [slice(p * 2 * DH, (p + 1) * 2 * DH) for p in range(pairs)]
            for pair, ln in enumerate(lanes):
                s_ref[pair, :, :w] = dot_right(stack_pair(do_ref[:, ln]), v_ref[pl.ds(base, w), ln])
            for pair, ln in enumerate(lanes):
                dvt[ln, pl.ds(base, w)] += dot(stack_pair(do_ref[:, ln]).T, p_ref[0, pair, :, :w])
            scores = []
            for pair, ln in enumerate(lanes):
                along = do_ref[:, ln].astype(F32) * ctx_ref[:, ln].astype(F32)
                delta = jnp.sum(stack_pair(along), axis=1, keepdims=True)
                scores.append((p_ref[0, pair, :, :w].astype(F32) * (s_ref[pair, :, :w] - delta)).astype(BF))
            for pair, ln in enumerate(lanes):
                dq = fold_pair(dot(scores[pair], k_ref[pl.ds(base, w), ln])) * (1.0 / math.sqrt(DH))
                dq = dq.astype(BF)
                grad_ref[pl.ds(start, QB), ln] = dq
                sum_ref[0:1, ln] += column_sum(dq.astype(F32))
            for pair, ln in enumerate(lanes):
                dkt[ln, pl.ds(base, w)] += dot(stack_pair(q_ref[:, ln]).T, scores[pair])

        for n in range(1, SPAN + 1):
            pl.when(count == n)(functools.partial(body, n))

        @pl.when(i == tiles - 1)
        def _():
            for o in range(0, tok, QB):
                grad_ref[o : o + QB, half : 2 * half] = dkt[:, o : o + QB].T.astype(BF)
                dv = dvt[:, o : o + QB].T.astype(BF)
                grad_ref[o : o + QB, 2 * half :] = dv
                sum_ref[1:2, :] += column_sum(dv.astype(F32))
            turned = x_ref[...].T
            rows = d // OWNERS
            for n in range(3):
                grads = dot(turned, grad_ref[:, n * half : (n + 1) * half])
                w_ref[:, n * rows : (n + 1) * rows, :] = grads.astype(BF).reshape(OWNERS, rows, half)
            w_ref[:, 3 * rows :, :] = out_grad_ref[...]

    return pl.pallas_call(
        kernel,
        grid_spec=pltpu.PrefetchScalarGridSpec(
            num_scalar_prefetch=1,
            grid=(tiles,),
            in_specs=[
                row,
                cols,
                cols,
                row,
                row,
                pl.BlockSpec((1, pairs, 2 * QB, SPAN * KB), lambda i, s: (i, pick(s), 0, 0)),
                whole((tok, d)),
                whole(out_grad.shape),
            ],
            out_specs=[whole((tok, 3 * half)), whole((SUMS, half)), whole((OWNERS, d // 2, half))],
            scratch_shapes=[
                pltpu.VMEM((half, tok), F32),
                pltpu.VMEM((half, tok), F32),
                pltpu.VMEM((pairs, 2 * QB, SPAN * KB), F32),
            ],
        ),
        out_shape=[
            struct((tok, 3 * half), BF),
            struct((SUMS, half), F32),
            struct((OWNERS, d // 2, half), BF),
        ],
        compiler_params=params(),
        cost_estimate=cost(1e10, 1e7),
        name="attend_back",
    )(place_win, q, k, v, ctx, do, p, tokens, out_grad)


class Weight:
    def __init__(self, shard, first):
        self.rows, self.width = shard.shape
        self.shard = shard
        self.first = first


class Group:
    def __init__(self, mesh, shards):
        self.fsdp = mesh.shape["fsdp"]
        self.fast = fast_path(mesh, shards)
        self.pieces = []
        self.weights = []
        first = 0
        for shard in shards:
            self.weights.append(Weight(shard, first))
            first += shard.size // (2 * PIECE)
        self.height = first

    def full(self, k):
        weight = self.weights[k]
        return (weight.rows * (self.fsdp if self.fast else 1), weight.width)

    def operands(self, used):
        if not self.fast:
            return [self.weights[k].shard for k in used]
        return [self.weights[k].shard for k in used] + [array for array, _, _ in self.pieces]

    def load(self, used, table, refs, targets, sems):
        if not self.fast:
            for n, target in enumerate(targets):
                pltpu.make_async_copy(refs[n], target, sems.at[n]).start()
            return
        core = table[self.fsdp]
        for n, k in enumerate(used):
            weight, target, sem = self.weights[k], targets[n], sems.at[n]
            half = weight.rows // 2
            base = pl.multiple_of(table[0] * weight.rows, weight.rows)
            pltpu.make_async_copy(refs[n], target.at[pl.ds(base, weight.rows), :], sem).start()
            for piece, (_, sources, mate) in zip(refs[len(used) :], self.pieces):
                side = (1 - core) if mate else core
                height = piece.shape[0] // len(sources)
                for order, source in enumerate(sources):
                    row = pl.multiple_of(table[source] * weight.rows + side * half, 16)
                    for c in range(weight.width // PIECE):
                        start = order * height + weight.first + c * half
                        pltpu.make_async_copy(
                            piece.at[start : start + half, :],
                            target.at[pl.ds(row, half), c * PIECE : (c + 1) * PIECE],
                            sem,
                        ).start()

    def wait(self, targets, sems):
        for n, target in enumerate(targets):
            pltpu.make_async_copy(target, target, sems.at[n]).wait()

    def wait_one(self, n, targets, sems):
        pltpu.make_async_copy(targets[n], targets[n], sems.at[n]).wait()

    def scratch(self, used):
        return [pltpu.VMEM(self.full(k), BF) for k in used] + [pltpu.SemaphoreType.DMA((len(used),))]


PIECE = 768
OWNERS = 8
SUMS = 16


def fast_path(mesh, shards):
    return (
        mesh.shape["fsdp"] == 8
        and mesh.shape["rep"] == 4
        and all(s.shape[0] % 32 == 0 and s.shape[1] % PIECE == 0 for s in shards)
    )


RING = (0, 2, 4, 6, 7, 5, 3, 1)


def ring_table():
    size = len(RING)
    place = {v: p for p, v in enumerate(RING)}
    steps = list(range(0, -(size // 2) - 1, -1)) + list(range(1, size - size // 2))
    return [[RING[(place[f] + s) % size] for s in steps] for f in range(size)]


def ring_step(value, step):
    size = len(RING)
    return lax.ppermute(value, "fsdp", [(RING[p], RING[(p + step) % size]) for p in range(size)])


def rep_step(value, bits):
    return lax.ppermute(value, "rep", [(r, r ^ bits) for r in range(4)])


def pallas(body, name, table, operands, outs, scratch, flops, limit=60):
    operands, outs = list(operands), list(outs)
    size = sum(o.size * o.dtype.itemsize for o in operands + outs)
    return pl.pallas_call(
        body,
        in_specs=[pl.BlockSpec(memory_space=pltpu.SMEM)] + [ANY] * len(operands),
        out_specs=[ANY] * len(outs),
        out_shape=outs,
        scratch_shapes=list(scratch) + [pltpu.SemaphoreType.DMA((COPIES,))],
        compiler_params=pltpu.CompilerParams(vmem_limit_bytes=limit << 20),
        cost_estimate=cost(flops, size),
        name=name,
    )(table, *operands)


COPIES = 48


class Copies:
    def __init__(self, sems):
        self.sems, self.started = sems, []

    def start(self, source, target):
        copy = pltpu.make_async_copy(source, target, self.sems.at[len(self.started)])
        copy.start()
        self.started.append([copy, False])
        return len(self.started) - 1

    def wait(self, *numbers):
        for n in numbers:
            if not self.started[n][1]:
                self.started[n][0].wait()
                self.started[n][1] = True

    def end(self):
        self.wait(*range(len(self.started)))


def vmem(*shape, dtype=BF):
    return pltpu.VMEM(shape, dtype)


def pack(table, groups, vectors):
    shards = [w.shard for g in groups for w in g.weights]
    core = table.shape[0] - 1
    outs = [struct((g.height + (SMALL if g is groups[0] else 0), PIECE), BF) for g in groups]

    def body(s, *refs):
        vec_refs = refs[: len(vectors)]
        shard_refs = list(refs[len(vectors) : len(vectors) + len(shards)])
        outs, refs = refs[len(vectors) + len(shards) :][: len(groups)], refs[len(vectors) + len(shards) + len(groups) :]
        staged, held, sems = refs[: len(groups)], refs[len(groups) : -1], refs[-1]
        copies = Copies(sems)
        loads = [copies.start(r, h) for r, h in zip(vec_refs, held)]
        ready = []
        for g, group in enumerate(groups):
            ready.append([])
            for weight in group.weights:
                ref, half = shard_refs.pop(0), weight.rows // 2
                rows = pl.ds(pl.multiple_of(s[core] * half, half), half)
                for c in range(weight.width // PIECE):
                    ready[g].append(
                        copies.start(
                            ref.at[rows, c * PIECE : (c + 1) * PIECE],
                            staged[g].at[weight.first + c * half : weight.first + (c + 1) * half, :],
                        )
                    )
        copies.wait(*loads)
        used = [r[...].astype(F32).reshape(1, -1) for r in held]
        row = jnp.concatenate(used[:-1], axis=1)
        last = jnp.concatenate([used[-1], jnp.zeros((1, PIECE - used[-1].shape[1]), F32)], axis=1)
        rest = jnp.zeros((SMALL - 2, PIECE), F32)
        staged[0][groups[0].height :, :] = jnp.concatenate([row, last, rest], axis=0).astype(BF)
        for g in range(len(groups)):
            copies.wait(*ready[g])
            copies.start(staged[g], outs[g])
        copies.end()

    return pallas(
        body,
        "pack",
        table,
        vectors + shards,
        outs,
        [vmem(*o.shape) for o in outs] + [vmem(*v.shape) for v in vectors],
        1,
    )


def project(table, group, tokens, small):
    tok, d = tokens.shape
    used = (0, 1, 2)
    extra = group.operands(used)
    fsdp, part = group.fsdp, d // group.fsdp
    wide = 4 * d // fsdp

    def body(s, x_hbm, small_hbm, *refs):
        pieces, outs, refs = refs[: len(extra)], refs[len(extra) : len(extra) + 8], refs[len(extra) + 8 :]
        x_ref, res_ref, vec_ref, bias_ref, all_small, small_sem, *weights, weight_sems, sems = refs
        copies = Copies(sems)
        tokens_in = copies.start(x_hbm, x_ref)
        group.load(used, s, pieces, weights, weight_sems)
        if group.fast:
            own = small_hbm.at[small_hbm.shape[0] - SMALL :, :]
            pltpu.make_async_copy(own, all_small.at[s[0]], small_sem).start()
            for piece, (_, sources, mate) in zip(pieces[len(used) :], group.pieces):
                if not mate:
                    pltpu.make_async_copy(
                        piece.at[group.height : group.height + SMALL, :], all_small.at[s[sources[0]]], small_sem
                    ).start()
        else:
            pltpu.make_async_copy(small_hbm, all_small, small_sem).start()
        pltpu.make_async_copy(all_small, all_small, small_sem).wait()
        rows = [all_small[f].astype(F32) for f in range(fsdp)]
        for v in range(8):
            vec_ref[v : v + 1, :] = jnp.concatenate([r[0:1, v * part : (v + 1) * part] for r in rows], axis=1)
        bias_ref[...] = jnp.zeros_like(bias_ref)
        bias_ref[0:1, :] = jnp.concatenate([r[1:2, :wide] for r in rows], axis=1)
        copies.start(vec_ref, outs[3])
        copies.start(bias_ref, outs[4])
        copies.wait(tokens_in)
        for n, weight in enumerate(weights):
            group.wait_one(n, weights, weight_sems)
            copies.start(weight, outs[5 + n])
            result = dot(x_ref[...], weight[...])
            if n == 0:
                result = (result + vec_ref[0:1, :]).astype(BF) * jnp.asarray(1.0 / math.sqrt(DH), BF)
            if n == 2:
                result = result + vec_ref[1:2, :]
            res_ref[n] = result.astype(BF)
            copies.start(res_ref.at[n], outs[n])
        copies.end()

    return pallas(
        body,
        "project",
        table,
        [tokens, small] + extra,
        [struct((tok, d), BF)] * 3
        + [struct((8, d), F32), struct((8, 4 * d), F32)]
        + [struct(group.full(k), BF) for k in used],
        [vmem(tok, d), vmem(3, tok, d), vmem(8, d, dtype=F32), vmem(8, 4 * d, dtype=F32)]
        + [vmem(fsdp, SMALL, d), pltpu.SemaphoreType.DMA]
        + group.scratch(used),
        6 * tok * d * d,
    )


SMALL = 16


def forward_block(table, inner, outer, context, tokens, out_grad, vectors, bias_inner):
    tok, d = tokens.shape
    ff = inner.full(1)[1]
    extra_inner, extra_outer = inner.operands((0, 1)), outer.operands((0,))
    count = len(extra_inner)
    extra = extra_inner + extra_outer
    rows, wide = struct((tok, d), BF), struct((tok, ff), BF)
    half, part = d // 2, ff // OWNERS
    outs = [rows, struct((tok, d), F32), rows, wide, struct((tok, d), F32), rows, struct((SUMS, d), F32)]
    outs += [struct((OWNERS, half, part), BF)] * 2
    outs += [struct(inner.full(0), BF), struct(inner.full(1), BF), struct(outer.full(0), BF)]

    def body(s, ctx_hbm, x_hbm, g_hbm, vec_hbm, bias_hbm, *refs):
        pieces, refs = refs[: len(extra)], refs[len(extra) :]
        out_hbm, hid_hbm, low_hbm, slope_hbm, second_hbm, grad_hbm, sum_hbm, mine_hbm, other_hbm = refs[:9]
        w_out_hbm, w_in_hbm, w_outer_hbm = refs[9:12]
        ctx_ref, x_ref, g_ref, vec_ref, bias_ref, hid_ref, low_ref, act_ref, slope_ref = refs[12:21]
        total, sum_ref, both, w_out, w_in, inner_sems, w_outer, outer_sems, sems = refs[21:]
        core = s[table.shape[0] - 1]
        copies = Copies(sems)
        loads = [copies.start(a, b) for a, b in ((ctx_hbm, ctx_ref), (x_hbm, x_ref), (vec_hbm, vec_ref))]
        inner.load((0, 1), s, pieces[:count], (w_out, w_in), inner_sems)
        outer.load((0,), s, pieces[count:], (w_outer,), outer_sems)
        later = [copies.start(bias_hbm, bias_ref), copies.start(g_hbm, g_ref)]
        sum_ref[...] = jnp.zeros_like(sum_ref)
        copies.wait(*loads)
        inner.wait_one(0, (w_out,), inner_sems)
        copies.start(w_out, w_out_hbm)
        hidden = x_ref[...].astype(F32) + dot(ctx_ref[...], w_out[...]) + vec_ref[2:3, :]
        hid_ref[...] = hidden
        hidden_out = copies.start(hid_ref, hid_hbm)
        normed, _ = norm(hidden)
        first = normed * vec_ref[3:4, :] + vec_ref[4:5, :]
        low_ref[...] = first.astype(BF)
        low_out = copies.start(low_ref, low_hbm)
        total[...] = first + vec_ref[5:6, :]
        inner.wait_one(1, (w_out, w_in), inner_sems)
        copies.start(w_in, w_in_hbm)
        outer.wait_one(0, (w_outer,), outer_sems)
        copies.start(w_outer, w_outer_hbm)
        copies.wait(*later)
        for c in range(0, ff, d):
            cols = slice(c, c + d)
            act, slope = gelu_parts(dot(low_ref[...], w_in[:, cols]) + bias_ref[0:1, cols])
            act = act.astype(BF)
            act_ref[:, cols] = act
            slope_ref[:, cols] = slope.astype(BF)
            copies.start(slope_ref.at[:, cols], slope_hbm.at[:, cols])
            total[...] += dot(act, w_outer[cols, :])
        normed, inverse = norm(total[...])
        gain = vec_ref[6:7, :]
        x_ref[...] = (normed * gain + vec_ref[7:8, :]).astype(BF)
        copies.start(x_ref, out_hbm)
        grad = g_ref[...].astype(F32)
        sum_ref[2:3, :] = column_sum(grad * normed)
        sum_ref[3:4, :] = column_sum(grad)
        second = norm_back(grad * gain, normed, inverse)
        low = second.astype(BF)
        ctx_ref[...] = low
        copies.start(ctx_ref, grad_hbm)
        copies.wait(hidden_out)
        hid_ref[...] = second
        copies.start(hid_ref, second_hbm)
        sum_ref[4:5, :] = column_sum(low.astype(F32))
        copies.start(sum_ref, sum_hbm)
        turned = low.T
        for i in range(0, OWNERS, 2):
            grads = dot(turned, act_ref[:, i * part : (i + 2) * part]).astype(BF)
            for k in (0, 1):
                columns = slice(k * part, (k + 1) * part)
                both[0, i + k], both[1, i + k] = grads[:half, columns], grads[half:, columns]
            pair = pl.ds(i, 2)
            copies.start(both.at[1 - core, pair], other_hbm.at[pair])
            copies.start(both.at[core, pair], mine_hbm.at[pair])
        copies.end()

    row = vmem(tok, d)
    return pallas(
        body,
        "forward_block",
        table,
        [context, tokens, out_grad, vectors, bias_inner] + extra,
        outs,
        [row, row, row, vmem(8, d, dtype=F32), vmem(8, ff, dtype=F32), vmem(tok, d, dtype=F32), row]
        + [vmem(tok, ff), vmem(tok, ff), vmem(tok, d, dtype=F32), vmem(SUMS, d, dtype=F32)]
        + [vmem(2, OWNERS, half, part)]
        + inner.scratch((0, 1))
        + outer.scratch((0,)),
        2 * tok * d * (d + 3 * ff),
        62,
    )


def active_back(choice, grad_low, slope, w_outer, first_low):
    tok, d = grad_low.shape
    ff = slope.shape[1]
    blocks = [slice(c, c + d) for c in range(0, ff, d)]
    half, rows, part = len(blocks) // 2, d // OWNERS, d // 2

    def body(s, g_hbm, slope_hbm, w_hbm, low_hbm, out_hbm, sum_hbm, mine_hbm, other_hbm, *refs):
        g_ref, slope_ref, w_ref, low_ref, out_ref, sum_ref, turned, held, sems = refs
        copies = Copies(sems)
        first = copies.start(g_hbm, g_ref)
        loads = [
            (copies.start(w_hbm.at[b, :], w_ref.at[b, :]), copies.start(slope_hbm.at[:, b], slope_ref.at[:, b]))
            for b in blocks
        ]
        left = copies.start(low_hbm, low_ref)
        sum_ref[...] = jnp.zeros_like(sum_ref)
        copies.wait(first)
        for n, b in enumerate(blocks):
            copies.wait(*loads[n])
            low = (dot_right(g_ref[...], w_ref[b, :]) * slope_ref[:, b].astype(F32)).astype(BF)
            out_ref[:, b] = low
            copies.start(out_ref.at[:, b], out_hbm.at[:, b])
            sum_ref[8 + n : 9 + n, :] = column_sum(low.astype(F32))
            if n == 0:
                copies.wait(left)
                turned[...] = low_ref[...].T
            grads = dot(turned[...], low).astype(BF)
            for k in range(0, d, part):
                at = (n % half * d + k) // part * rows
                held[n // half, :, at : at + rows, :] = grads[:, k : k + part].reshape(OWNERS, rows, part)
        copies.start(held.at[1 - s[0]], other_hbm)
        copies.start(held.at[s[0]], mine_hbm)
        copies.start(sum_ref, sum_hbm)
        copies.end()

    grad = struct((OWNERS, rows * ff // (2 * part), part), BF)
    return pallas(
        body,
        "active_back",
        choice,
        [grad_low, slope, w_outer, first_low],
        [struct((tok, ff), BF), struct((SUMS, d), F32), grad, grad],
        [vmem(tok, d), vmem(tok, ff), vmem(ff, d), vmem(tok, d), vmem(tok, ff), vmem(SUMS, d, dtype=F32)]
        + [vmem(d, tok), vmem(2, *grad.shape)],
        4 * tok * d * ff,
    )


def inner_back(choice, grad_inner, grad_second, hidden, vectors, w_out, w_in, context):
    tok, d = hidden.shape
    ff, half = grad_inner.shape[1], d // 2
    blocks = [slice(c, c + d) for c in range(0, ff, d)]

    def body(s, g_hbm, second_hbm, hid_hbm, vec_hbm, w_out_hbm, w_in_hbm, *refs):
        left_hbm, out_hbm, ctx_hbm, sum_hbm, mine_hbm, other_hbm = refs[:6]
        g_ref, second_ref, hid_ref, vec_ref, w_out, w_in, left_ref, ctx_ref, sum_ref, held, sems = refs[6:]
        copies = Copies(sems)
        loads = [
            (copies.start(g_hbm.at[:, b], g_ref.at[:, b]), copies.start(w_in_hbm.at[:, b], w_in.at[:, b]))
            for b in blocks[:1]
        ]
        first = copies.start(second_hbm, second_ref)
        loads += [
            (copies.start(g_hbm.at[:, b], g_ref.at[:, b]), copies.start(w_in_hbm.at[:, b], w_in.at[:, b]))
            for b in blocks[1:]
        ]
        later = [copies.start(a, b) for a, b in ((hid_hbm, hid_ref), (vec_hbm, vec_ref), (w_out_hbm, w_out))]
        later.append(copies.start(left_hbm, left_ref))
        sum_ref[...] = jnp.zeros_like(sum_ref)
        for n, b in enumerate(blocks):
            copies.wait(*loads[n])
            part = dot_right(g_ref[:, b], w_in[:, b])
            if n == 0:
                copies.wait(first)
            second_ref[...] += part
        copies.wait(*later)
        grad = second_ref[...]
        normed, inverse = norm(hid_ref[...])
        sum_ref[5:6, :] = column_sum(grad * normed)
        sum_ref[6:7, :] = column_sum(grad)
        hidden_grad = norm_back(grad * vec_ref[3:4, :], normed, inverse)
        second_ref[...] = hidden_grad
        copies.start(second_ref, out_hbm)
        low = hidden_grad.astype(BF)
        ctx_ref[...] = dot_right(low, w_out[...]).astype(BF)
        copies.start(ctx_ref, ctx_hbm)
        grads = dot(left_ref[...].T, low).astype(BF)
        for k in (0, 1):
            held[k] = grads[:, k * half : (k + 1) * half].reshape(OWNERS, d // OWNERS, half)
        copies.start(held.at[1 - s[0]], other_hbm)
        copies.start(held.at[s[0]], mine_hbm)
        sum_ref[7:8, :] = column_sum(low.astype(F32))
        copies.start(sum_ref, sum_hbm)
        copies.end()

    full, grad = vmem(tok, d, dtype=F32), struct((OWNERS, d // OWNERS, half), BF)
    return pallas(
        body,
        "inner_back",
        choice,
        [grad_inner, grad_second, hidden, vectors, w_out, w_in, context],
        [struct((tok, d), F32), struct((tok, d), BF), struct((SUMS, d), F32), grad, grad],
        [vmem(tok, ff), full, full, vmem(8, d, dtype=F32), vmem(d, d), vmem(d, ff), vmem(tok, d), vmem(tok, d)]
        + [vmem(SUMS, d, dtype=F32), vmem(2, *grad.shape)],
        2 * tok * d * (2 * d + ff),
    )


def tokens_back(choice, grad_hidden, mine, other, weights):
    tok, d = grad_hidden.shape
    half = d // 2

    def body(s, hid_hbm, mine_hbm, other_hbm, *refs):
        weights, out_hbm, hid_ref, grad_ref, w_ref, out_ref, sems = refs[:3], *refs[3:]
        copies = Copies(sems)
        loads = []
        for k, (grad, side) in enumerate(((other_hbm, 1 - s[0]), (mine_hbm, s[0]))):
            cols = pl.ds(pl.multiple_of(side * half, half), half)
            for n, weight in enumerate(weights):
                at = 3 * k + n
                loads.append(
                    (
                        copies.start(grad.at[:, n * half : (n + 1) * half], grad_ref.at[at]),
                        copies.start(weight.at[:, cols], w_ref.at[at]),
                    )
                )
            if k == 0:
                first = copies.start(hid_hbm, hid_ref)
        for at, load in enumerate(loads):
            copies.wait(*load)
            part = dot_right(grad_ref[at], w_ref[at])
            copies.wait(first)
            if at < 5:
                hid_ref[...] += part
            else:
                out_ref[...] = (hid_ref[...] + part).astype(BF)
        copies.start(out_ref, out_hbm)
        copies.end()

    return pallas(
        body,
        "tokens_back",
        choice,
        [grad_hidden, mine, other, *weights],
        [struct((tok, d), BF)],
        [vmem(tok, d, dtype=F32), vmem(6, tok, half), vmem(6, d, half), vmem(tok, d)],
        6 * tok * d * d,
    )[0]


def axis_step(value, axis):
    if axis == "x":
        return rep_step(value, 2)
    return lax.ppermute(value, "fsdp", [(f, f ^ 1) for f in range(8)])


def after(value, *events):
    return lax.optimization_barrier((value,) + events)[0] if events else value


def added(*terms):
    total = terms[0].astype(F32)
    for term in terms[1:]:
        total = total + term.astype(F32)
    return total.astype(BF)


def chosen(parts, bit, axis):
    return lax.dynamic_index_in_dim(parts, bit, axis, keepdims=False)


def halves(value, bit, axis):
    owners, rows, n = value.shape
    if axis == "y":
        return chosen(value.reshape(owners // 2, 2, rows, n), bit, 1)
    return chosen(value.reshape(owners, 2, rows // 2, n), bit, 1)


class Stream:
    def __init__(self, place, terms, order):
        self.place, self.terms, self.order = place, terms, order

    def move(self, axis, *events):
        bit = self.place.x if axis == "x" else self.place.y
        terms = self.terms[:-1] + [after(self.terms[-1], *events)]
        send = added(*(halves(v, 1 - bit, axis) for v in terms))
        self.terms = [halves(v, bit, axis) for v in terms] + [axis_step(send, axis)]
        return [send]

    def first(self, *events):
        return self.move(self.order[0], *events)

    def second(self, *events):
        return self.move(self.order[1], *events)


class Owned:
    def __init__(self, place, mine, received):
        self.place, mid = place, mine.shape[1] // 2
        self.streams = [
            Stream(place, [mine[:, :mid], received[:, :mid]], "xy"),
            Stream(place, [mine[:, mid:], received[:, mid:]], "yx"),
        ]

    def first(self, *events):
        return [s for stream in self.streams for s in stream.first(*events)]

    def second(self, *events):
        return [s for stream in self.streams for s in stream.second(*events)]

    def third(self, *events):
        sums = [added(*s.terms[:-1], after(s.terms[-1], *events)) for s in self.streams]
        parts = jnp.concatenate(sums, 1)
        z = self.place.z
        moved = [
            lax.ppermute(
                chosen(parts, (z + k) % 4, 0), "fsdp", [(f, (f // 2 + k) % 4 * 2 + f % 2) for f in range(8)]
            )
            for k in (1, 3, 2)
        ]
        self.terms = [chosen(parts, z, 0)] + moved
        return [parts]

    def fourth(self, *events):
        self.own = added(*self.terms[:-1], after(self.terms[-1], *events))
        self.other = rep_step(self.own, 2)
        return [self.own]

    def fifth(self, *events):
        other = after(self.other, *events)
        low = jnp.where(self.place.x == 0, self.own, other)
        high = jnp.where(self.place.x == 0, other, self.own)
        mid = low.shape[0] // 2
        half = jnp.concatenate([low[:mid], high[:mid], low[mid:], high[mid:]], 0)
        self.both = (half, rep_step(half, 1))
        return [half]

    def last(self):
        mine, mate = self.both
        first = self.place.core == 0
        return jnp.where(first, mine, mate), jnp.where(first, mate, mine)


class Place:
    def __init__(self, mesh):
        f, r = lax.axis_index("fsdp"), lax.axis_index("rep")
        self.f, self.core, self.x = f, r % 2, r // 2
        self.y, self.z = f % 2, f // 2
        self.choice = jnp.stack([self.core, self.x, self.y]).astype(jnp.int32)
        if mesh.shape["fsdp"] == len(RING):
            row = lax.dynamic_index_in_dim(jnp.array(ring_table(), jnp.int32), f, 0, keepdims=False)
            self.table = jnp.concatenate([row, self.core[None].astype(jnp.int32)])
        else:
            self.table = jnp.zeros((1,), jnp.int32)


class Ring:
    def __init__(self, group, payload, last):
        self.group, self.ways, self.last, self.count = group, {1: [payload], -1: [payload]}, last, 0

    def ways_of(self, count):
        return (1, -1) if count < len(RING) // 2 else (self.last,)

    def source(self, way, count):
        return count if way == 1 or count == len(RING) // 2 else len(RING) // 2 + count

    @property
    def came(self):
        return tuple(self.ways[way][self.count] for way in self.ways_of(self.count))

    def step(self, *events):
        self.count += 1
        for way in self.ways_of(self.count):
            self.ways[way].append(ring_step(after(self.ways[way][-1], *events), way))
            self.group.pieces.append((self.ways[way][-1], (self.source(way, self.count),), False))

    def share(self, count, *events):
        for way in self.ways_of(count):
            piece = rep_step(after(self.ways[way][count], *events), 1)
            self.group.pieces.append((piece, (self.source(way, count),), True))


class Travel:
    def __init__(self, rings):
        self.rings, self.past, self.seen, self.shared = rings, [], (), [0] * len(rings)

    def run(self, order, *events):
        for n in order:
            ring = self.rings[n]
            if len(self.past) > 2:
                last = self.past[-3]
                self.seen = self.came(last)
                self.share(last[0])
            ring.step(*events, *self.seen)
            self.past.append((n, ring.came))

    def came(self, entry):
        return entry[1]

    def share(self, n, *events):
        ring = self.rings[n]
        while self.shared[n] < ring.count:
            self.shared[n] += 1
            ring.share(self.shared[n], *events)

    def settle(self, n):
        self.share(n)


def local(mesh, *args):
    (
        tokens, seq_ids, key_mask, weight_query, bias_query, weight_key, weight_value, bias_value,
        weight_out, bias_out, norm1_gain, norm1_bias, weight_inner, bias_inner, weight_outer, bias_outer,
        norm2_gain, norm2_bias, out_grad,
    ) = args
    place = Place(mesh)
    choice, table = place.choice, place.table
    fsdp = mesh.shape["fsdp"]
    d = tokens.shape[1]
    win = windows(seq_ids[0])
    narrow = [bias_query, bias_value, bias_out, norm1_gain, norm1_bias, bias_outer, norm2_gain, norm2_bias]
    shards = [[weight_query, weight_key, weight_value], [weight_out, weight_inner], [weight_outer]]
    fast = all(fast_path(mesh, s) for s in shards)
    if fast:
        groups = [Group(mesh, s) for s in shards]
        packed = pack(table, groups, narrow + [bias_inner])
        rings = [Ring(g, p, way) for g, p, way in zip(groups, packed, (1, -1, 1))]
        small = packed[0]
        travel = Travel(rings)
        travel.run((0, 1, 2, 0, 1, 0, 2, 0))
        travel.settle(0)
        travel.run((1,))
    else:
        groups = [Group(mesh, [lax.all_gather(w, "fsdp", axis=0, tiled=True) for w in s]) for s in shards]
        rows = [jnp.concatenate(narrow), bias_inner]
        rows = [jnp.concatenate([r, jnp.zeros((d - r.size,), BF)])[None] for r in rows]
        small = jnp.concatenate(rows + [jnp.zeros((SMALL - 2, d), BF)], 0)
        small = lax.all_gather(small, "fsdp", axis=0, tiled=False)
    qkv, inner_group, outer_group = groups

    q, k, v, vectors, full_bias_inner, *weights = project(table, qkv, tokens, small)
    if fast:
        travel.run((2, 1), q)
        q = after(q, *travel.seen)
    context, probs = attend(win, seq_ids, key_mask, q, k, v)
    if fast:
        travel.run((2,), context)
        travel.settle(1)
        travel.settle(2)
    (
        layer_out, hidden, first_low, slope, grad_second, grad_outer, sums2, outer_mine, outer_other,
        w_out, w_in, w_outer,
    ) = forward_block(
        place_table(table, choice), inner_group, outer_group, context, tokens, out_grad, vectors, full_bias_inner
    )
    if not fast:
        choice = jnp.zeros((3,), jnp.int32)
    if fast:
        outer_sum = Owned(place, outer_mine, rep_step(outer_other, 1))
    grad_inner, sums_inner, inner_mine, inner_other = active_back(choice, grad_outer, slope, w_outer, first_low)
    if fast:
        inner_sum = Owned(place, inner_mine, rep_step(inner_other, 1))
        event = outer_sum.first(inner_mine)
        grad_inner = after(grad_inner, *event)
    grad_hidden, grad_context, sums1, out_mine, out_other = inner_back(
        choice, grad_inner, grad_second, hidden, vectors, w_out, w_in, context
    )
    if fast:
        event = outer_sum.second(out_mine)
        event += inner_sum.first(out_mine)
        grad_context = after(grad_context, *event)
    place_win = jnp.concatenate([choice, win])
    grads_other, sums_other, query_other = attend_back(
        place_win, 1, q, k, v, context, grad_context, probs, tokens, out_other
    )
    if fast:
        query_came = rep_step(query_other, 1)
        event = inner_sum.second(grads_other)
        event += outer_sum.third(grads_other)
        grad_context = after(grad_context, *event)
    grads_mine, sums_mine, query_mine = attend_back(
        place_win, 0, q, k, v, context, grad_context, probs, tokens, out_mine
    )
    if fast:
        query_sum = Owned(place, query_mine, query_came)
        event = query_sum.first(query_mine)
        event += inner_sum.third(query_mine)
        event += outer_sum.fourth(query_mine)
        grad_hidden = after(grad_hidden, *event)
    grad_tokens = tokens_back(choice, grad_hidden, grads_mine, grads_other, weights)
    sums_att = by_core(choice[0], sums_mine, sums_other, 1)
    sums = sums1 + sums2 + sums_inner + sums_att
    if fast:
        event = query_sum.second(grad_tokens)
        sums = sums + after(rep_step(sums, 1), *event)
        event += inner_sum.fourth(*event)
        event += outer_sum.fifth(*event)
        sums = sums + after(rep_step(sums, 2), *event)
        event = query_sum.third(*event)
        sums = sums + after(axis_step(sums, "y"), *event)
        event += inner_sum.fifth(sums)
        low, high = outer_sum.last()
        final_outer = jnp.concatenate([low, high], 0).T.astype(F32)
        sums = sums + after(z_step(sums, 1), *event)
        sums = sums + after(z_step(sums, 2), *event)
        low, high = inner_sum.last()
        rows = d // fsdp
        blocks = [v[c : c + rows] for v in (low, high) for c in range(0, v.shape[0], rows)]
        final_inner = jnp.concatenate(blocks, 1).astype(F32)
        event = query_sum.fourth(final_outer, final_inner, sums)
        query_sum.fifth(*event)
        low, high = query_sum.last()
        final_query, final_key, final_value, final_out = (
            jnp.concatenate([low[c : c + rows], high[c : c + rows]], 1).astype(F32)
            for c in range(0, 4 * rows, rows)
        )
    else:

        def plain(*blocks):
            total = jnp.concatenate(blocks, 2)
            total = total.reshape(-1, total.shape[2])
            owned = lax.psum_scatter(total, "fsdp", scatter_dimension=0, tiled=True)
            return lax.psum(owned, "rep").astype(F32)

        sums = lax.psum(sums, ("fsdp", "rep"))
        final_outer = plain(jnp.concatenate([outer_mine, outer_other], 1).transpose(0, 2, 1))
        part = d // OWNERS
        unstack = lambda v: [v[:, c : c + part] for c in range(0, v.shape[1], part)]
        final_inner = plain(*unstack(inner_mine), *unstack(inner_other))
        final_query, final_key, final_value, final_out = (
            plain(a, b) for a, b in zip(unstack(query_mine), unstack(query_other))
        )

    narrow_sums = lax.dynamic_slice_in_dim(sums, place.f * (d // fsdp), d // fsdp, 1)
    inner_sums = lax.dynamic_slice_in_dim(sums[8:12].reshape(-1), place.f * bias_inner.size, bias_inner.size, 0)
    return (
        layer_out,
        grad_tokens,
        final_query,
        narrow_sums[0],
        final_key,
        final_value,
        narrow_sums[1],
        final_out,
        narrow_sums[7],
        narrow_sums[5],
        narrow_sums[6],
        final_inner,
        inner_sums,
        final_outer,
        narrow_sums[4],
        narrow_sums[2],
        narrow_sums[3],
    )


def by_core(core, mine, other, axis):
    return jnp.where(core == 0, jnp.concatenate([mine, other], axis), jnp.concatenate([other, mine], axis))


def z_step(value, bits):
    return lax.ppermute(value, "fsdp", [(f, f ^ (2 * bits)) for f in range(8)])


def place_table(table, choice):
    return jnp.concatenate([table[:-1], choice[:1]]) if table.shape[0] > 1 else jnp.zeros((1,), jnp.int32)


def solution(mesh):
    rows, shard, part = P(("fsdp", "rep"), None), P("fsdp", None), P("fsdp")
    return jax.shard_map(
        functools.partial(local, mesh),
        mesh=mesh,
        in_specs=(
            rows, rows, rows, shard, part, shard, shard, part, shard, part, part, part, shard, part, shard,
            part, part, part, rows,
        ),
        out_specs=(
            rows, rows, shard, part, shard, shard, part, shard, part, part, part, shard, part, shard, part,
            part, part,
        ),
        check_vma=False,
    )
```

```python
import functools
import math

import jax
import jax.numpy as jnp
from jax import lax
from jax.experimental import pallas as pl
from jax.experimental.pallas import tpu as pltpu
from jax.sharding import PartitionSpec as P

HEADS = 12
DH = 64
BF = jnp.bfloat16
F32 = jnp.float32
NEGATIVE = -1e30
EPSILON = 1e-12
QB = 128
KB = 128
SPAN = 5
ROWS = 1024
VMEM = 60 * 1024 * 1024
COST = 0.05
ANY = pl.BlockSpec(memory_space=pl.ANY)


def dot(left, right):
    return jnp.dot(left, right, preferred_element_type=F32)


def dot_right(left, right):
    return lax.dot_general(left, right, (((1,), (1,)), ((), ())), preferred_element_type=F32)


def params(steps=1):
    return pltpu.CompilerParams(
        dimension_semantics=("arbitrary",) * steps, vmem_limit_bytes=VMEM
    )


def cost(flops, size):
    return pl.CostEstimate(flops=int(flops * COST), bytes_accessed=int(size * COST), transcendentals=0)


def struct(shape, dtype):
    return jax.ShapeDtypeStruct(shape, dtype)


def whole(shape):
    return pl.BlockSpec(shape, lambda i, s: (0,) * len(shape))


def rows_of(width, height=ROWS):
    return pl.BlockSpec((height, width), lambda i, s: (i, 0))


def norm(hidden):
    center = hidden - jnp.mean(hidden, axis=-1, keepdims=True)
    inverse = lax.rsqrt(jnp.mean(center * center, axis=-1, keepdims=True) + EPSILON)
    return center * inverse, inverse


def norm_back(grad, normed, inverse):
    mean = jnp.mean(grad, axis=-1, keepdims=True)
    along = jnp.mean(grad * normed, axis=-1, keepdims=True)
    return inverse * (grad - mean - normed * along)


def gelu_parts(inner):
    phi = 0.5 + 0.5 * lax.erf(inner * 0.7071067811865476)
    density = jnp.exp((-0.5 * inner) * inner) * 0.3989422804014327
    return inner * phi, phi + inner * density


def column_sum(value):
    return jnp.sum(value, axis=0, keepdims=True)


def windows(seq_row):
    tiles = seq_row.reshape(seq_row.shape[0] // QB, QB)
    below = jnp.sum((seq_row[None] < tiles[:, :1]).astype(jnp.int32), axis=1)
    upto = jnp.sum((seq_row[None] <= tiles[:, -1:]).astype(jnp.int32), axis=1)
    low = below // KB
    return jnp.concatenate([low, (upto + KB - 1) // KB - low])


def first_half(shape):
    return lax.broadcasted_iota(jnp.int32, shape, len(shape) - 1) < DH


def stack_pair(pair):
    low = first_half(pair.shape)
    zero = jnp.zeros_like(pair)
    return jnp.concatenate([jnp.where(low, pair, zero), jnp.where(low, zero, pair)], axis=0)


def fold_pair(both):
    half = both.shape[0] // 2
    return jnp.where(first_half((half, both.shape[1])), both[:half], both[half:])


def attend_kernel(win, seq_ref, mask_ref, q_ref, k_ref, v_ref, ctx_ref, p_ref, bias_ref, s_ref):
    i = pl.program_id(0)
    low = win[i]
    count = win[pl.num_programs(0) + i]
    pairs = q_ref.shape[1] // (2 * DH)

    def body(n):
        w = n * KB
        base = pl.multiple_of(low * KB, KB)
        start = pl.multiple_of(i * QB, QB)
        for pair in range(pairs):
            lanes = slice(pair * 2 * DH, (pair + 1) * 2 * DH)
            s_ref[pair, :, :w] = dot_right(stack_pair(q_ref[:, lanes]), k_ref[pl.ds(base, w), lanes])
        own = jnp.broadcast_to(seq_ref[:, pl.ds(start, QB)], (QB, QB)).T
        rows = start + lax.broadcasted_iota(jnp.int32, (QB, KB), 0)
        for b in range(n):
            off = pl.multiple_of(base + b * KB, KB)
            cols = off + lax.broadcasted_iota(jnp.int32, (QB, KB), 1)
            visible = (mask_ref[:, pl.ds(off, KB)] == 1) | (rows == cols)
            allowed = (own == seq_ref[:, pl.ds(off, KB)]) & visible
            bias_ref[:, b * KB : (b + 1) * KB] = jnp.where(allowed, 0.0, NEGATIVE).astype(F32)
        ones = jnp.ones((w, 2 * DH), BF)
        for group in range(0, pairs, GROUP):
            expons = []
            for pair in range(group, group + GROUP):
                lanes = slice(pair * 2 * DH, (pair + 1) * 2 * DH)
                bias = bias_ref[:, :w]
                scores = s_ref[pair, :, :w] + jnp.concatenate([bias, bias], axis=0)
                expons.append(jnp.exp(scores - jnp.max(scores, axis=1, keepdims=True)).astype(BF))
            for pair in range(group, group + GROUP):
                lanes = slice(pair * 2 * DH, (pair + 1) * 2 * DH)
                expon = expons[pair - group]
                mixed = dot(expon, jnp.concatenate([v_ref[pl.ds(base, w), lanes], ones], axis=1))
                scale = 1.0 / mixed[:, 2 * DH :]
                ctx_ref[:, lanes] = fold_pair(mixed[:, : 2 * DH] * scale).astype(BF)
                for b in range(n):
                    p_ref[0, pair, :, b * KB : (b + 1) * KB] = (
                        expon[:, b * KB : (b + 1) * KB].astype(F32) * scale
                    ).astype(BF)

    for n in range(1, SPAN + 1):
        pl.when(count == n)(functools.partial(body, n))


GROUP = 6


def attend(win, seq, mask, q, k, v):
    tok, d = q.shape
    tiles, pairs = tok // QB, d // (2 * DH)
    return pl.pallas_call(
        attend_kernel,
        grid_spec=pltpu.PrefetchScalarGridSpec(
            num_scalar_prefetch=1,
            grid=(tiles,),
            in_specs=[whole(seq.shape), whole(mask.shape), rows_of(d, QB), whole(k.shape), whole(v.shape)],
            out_specs=[
                rows_of(d, QB),
                pl.BlockSpec((1, pairs, 2 * QB, SPAN * KB), lambda i, s: (i, 0, 0, 0)),
            ],
            scratch_shapes=[pltpu.VMEM((QB, SPAN * KB), F32), pltpu.VMEM((pairs, 2 * QB, SPAN * KB), F32)],
        ),
        out_shape=[struct((tok, d), BF), struct((tiles, pairs, 2 * QB, SPAN * KB), BF)],
        compiler_params=params(),
        cost_estimate=cost(1.4e10, 2e7),
        name="attend",
    )(win, seq, mask, q, k, v)


def attend_back(place_win, side, q, k, v, ctx, do, p, tokens, out_grad):
    tok, d = q.shape
    half = d // 2
    tiles, pairs = tok // QB, half // (2 * DH)
    pick = (lambda s: s[0]) if side == 0 else (lambda s: 1 - s[0])
    row = pl.BlockSpec((QB, half), lambda i, s: (i, pick(s)))
    cols = pl.BlockSpec((tok, half), lambda i, s: (0, pick(s)))

    def kernel(s, q_ref, k_ref, v_ref, ctx_ref, do_ref, p_ref, x_ref, out_grad_ref, grad_ref, sum_ref, w_ref, dkt, dvt, s_ref):
        i = pl.program_id(0)
        low, count = s[3 + i], s[3 + tiles + i]
        start = pl.multiple_of(i * QB, QB)

        @pl.when(i == 0)
        def _():
            dkt[...] = jnp.zeros_like(dkt)
            dvt[...] = jnp.zeros_like(dvt)
            sum_ref[...] = jnp.zeros_like(sum_ref)

        def body(n):
            w = n * KB
            base = pl.multiple_of(low * KB, KB)
            lanes = [slice(p * 2 * DH, (p + 1) * 2 * DH) for p in range(pairs)]
            for pair, ln in enumerate(lanes):
                s_ref[pair, :, :w] = dot_right(stack_pair(do_ref[:, ln]), v_ref[pl.ds(base, w), ln])
            for pair, ln in enumerate(lanes):
                dvt[ln, pl.ds(base, w)] += dot(stack_pair(do_ref[:, ln]).T, p_ref[0, pair, :, :w])
            scores = []
            for pair, ln in enumerate(lanes):
                along = do_ref[:, ln].astype(F32) * ctx_ref[:, ln].astype(F32)
                delta = jnp.sum(stack_pair(along), axis=1, keepdims=True)
                scores.append((p_ref[0, pair, :, :w].astype(F32) * (s_ref[pair, :, :w] - delta)).astype(BF))
            for pair, ln in enumerate(lanes):
                dq = fold_pair(dot(scores[pair], k_ref[pl.ds(base, w), ln])) * (1.0 / math.sqrt(DH))
                dq = dq.astype(BF)
                grad_ref[pl.ds(start, QB), ln] = dq
                sum_ref[0:1, ln] += column_sum(dq.astype(F32))
            for pair, ln in enumerate(lanes):
                dkt[ln, pl.ds(base, w)] += dot(stack_pair(q_ref[:, ln]).T, scores[pair])

        for n in range(1, SPAN + 1):
            pl.when(count == n)(functools.partial(body, n))

        @pl.when(i == tiles - 1)
        def _():
            for o in range(0, tok, QB):
                grad_ref[o : o + QB, half : 2 * half] = dkt[:, o : o + QB].T.astype(BF)
                dv = dvt[:, o : o + QB].T.astype(BF)
                grad_ref[o : o + QB, 2 * half :] = dv
                sum_ref[1:2, :] += column_sum(dv.astype(F32))
            turned = x_ref[...].T
            rows = d // OWNERS
            for n in range(3):
                grads = dot(turned, grad_ref[:, n * half : (n + 1) * half])
                w_ref[:, n * rows : (n + 1) * rows, :] = grads.astype(BF).reshape(OWNERS, rows, half)
            w_ref[:, 3 * rows :, :] = out_grad_ref[...]

    return pl.pallas_call(
        kernel,
        grid_spec=pltpu.PrefetchScalarGridSpec(
            num_scalar_prefetch=1,
            grid=(tiles,),
            in_specs=[
                row,
                cols,
                cols,
                row,
                row,
                pl.BlockSpec((1, pairs, 2 * QB, SPAN * KB), lambda i, s: (i, pick(s), 0, 0)),
                whole((tok, d)),
                whole(out_grad.shape),
            ],
            out_specs=[whole((tok, 3 * half)), whole((SUMS, half)), whole((OWNERS, d // 2, half))],
            scratch_shapes=[
                pltpu.VMEM((half, tok), F32),
                pltpu.VMEM((half, tok), F32),
                pltpu.VMEM((pairs, 2 * QB, SPAN * KB), F32),
            ],
        ),
        out_shape=[
            struct((tok, 3 * half), BF),
            struct((SUMS, half), F32),
            struct((OWNERS, d // 2, half), BF),
        ],
        compiler_params=params(),
        cost_estimate=cost(1e10, 1e7),
        name="attend_back",
    )(place_win, q, k, v, ctx, do, p, tokens, out_grad)


class Weight:
    def __init__(self, shard, first):
        self.rows, self.width = shard.shape
        self.shard = shard
        self.first = first


class Group:
    def __init__(self, mesh, shards):
        self.fsdp = mesh.shape["fsdp"]
        self.fast = fast_path(mesh, shards)
        self.pieces = []
        self.weights = []
        first = 0
        for shard in shards:
            self.weights.append(Weight(shard, first))
            first += shard.size // (2 * PIECE)
        self.height = first

    def full(self, k):
        weight = self.weights[k]
        return (weight.rows * (self.fsdp if self.fast else 1), weight.width)

    def operands(self, used):
        if not self.fast:
            return [self.weights[k].shard for k in used]
        return [self.weights[k].shard for k in used] + [array for array, _, _ in self.pieces]

    def load(self, used, table, refs, targets, sems):
        if not self.fast:
            for n, target in enumerate(targets):
                pltpu.make_async_copy(refs[n], target, sems.at[n]).start()
            return
        core = table[self.fsdp]
        for n, k in enumerate(used):
            weight, target, sem = self.weights[k], targets[n], sems.at[n]
            half = weight.rows // 2
            base = pl.multiple_of(table[0] * weight.rows, weight.rows)
            pltpu.make_async_copy(refs[n], target.at[pl.ds(base, weight.rows), :], sem).start()
            for piece, (_, sources, mate) in zip(refs[len(used) :], self.pieces):
                side = (1 - core) if mate else core
                height = piece.shape[0] // len(sources)
                for order, source in enumerate(sources):
                    row = pl.multiple_of(table[source] * weight.rows + side * half, 16)
                    for c in range(weight.width // PIECE):
                        start = order * height + weight.first + c * half
                        pltpu.make_async_copy(
                            piece.at[start : start + half, :],
                            target.at[pl.ds(row, half), c * PIECE : (c + 1) * PIECE],
                            sem,
                        ).start()

    def wait(self, targets, sems):
        for n, target in enumerate(targets):
            pltpu.make_async_copy(target, target, sems.at[n]).wait()

    def wait_one(self, n, targets, sems):
        pltpu.make_async_copy(targets[n], targets[n], sems.at[n]).wait()

    def scratch(self, used):
        return [pltpu.VMEM(self.full(k), BF) for k in used] + [pltpu.SemaphoreType.DMA((len(used),))]


PIECE = 768
OWNERS = 8
SUMS = 16


def fast_path(mesh, shards):
    return (
        mesh.shape["fsdp"] == 8
        and mesh.shape["rep"] == 4
        and all(s.shape[0] % 32 == 0 and s.shape[1] % PIECE == 0 for s in shards)
    )


RING = (0, 2, 4, 6, 7, 5, 3, 1)


def ring_table():
    size = len(RING)
    place = {v: p for p, v in enumerate(RING)}
    steps = list(range(0, -(size // 2) - 1, -1)) + list(range(1, size - size // 2))
    return [[RING[(place[f] + s) % size] for s in steps] for f in range(size)]


def ring_step(value, step):
    size = len(RING)
    return lax.ppermute(value, "fsdp", [(RING[p], RING[(p + step) % size]) for p in range(size)])


def rep_step(value, bits):
    return lax.ppermute(value, "rep", [(r, r ^ bits) for r in range(4)])


def pallas(body, name, table, operands, outs, scratch, flops, limit=60):
    operands, outs = list(operands), list(outs)
    size = sum(o.size * o.dtype.itemsize for o in operands + outs)
    return pl.pallas_call(
        body,
        in_specs=[pl.BlockSpec(memory_space=pltpu.SMEM)] + [ANY] * len(operands),
        out_specs=[ANY] * len(outs),
        out_shape=outs,
        scratch_shapes=list(scratch) + [pltpu.SemaphoreType.DMA((COPIES,))],
        compiler_params=pltpu.CompilerParams(vmem_limit_bytes=limit << 20),
        cost_estimate=cost(flops, size),
        name=name,
    )(table, *operands)


COPIES = 48


class Copies:
    def __init__(self, sems):
        self.sems, self.started = sems, []

    def start(self, source, target):
        copy = pltpu.make_async_copy(source, target, self.sems.at[len(self.started)])
        copy.start()
        self.started.append([copy, False])
        return len(self.started) - 1

    def wait(self, *numbers):
        for n in numbers:
            if not self.started[n][1]:
                self.started[n][0].wait()
                self.started[n][1] = True

    def end(self):
        self.wait(*range(len(self.started)))


def vmem(*shape, dtype=BF):
    return pltpu.VMEM(shape, dtype)


def pack(table, groups, vectors):
    shards = [w.shard for g in groups for w in g.weights]
    core = table.shape[0] - 1
    outs = [struct((g.height + (SMALL if g is groups[0] else 0), PIECE), BF) for g in groups]

    def body(s, *refs):
        vec_refs = refs[: len(vectors)]
        shard_refs = list(refs[len(vectors) : len(vectors) + len(shards)])
        outs, refs = refs[len(vectors) + len(shards) :][: len(groups)], refs[len(vectors) + len(shards) + len(groups) :]
        staged, held, sems = refs[: len(groups)], refs[len(groups) : -1], refs[-1]
        copies = Copies(sems)
        loads = [copies.start(r, h) for r, h in zip(vec_refs, held)]
        ready = []
        for g, group in enumerate(groups):
            ready.append([])
            for weight in group.weights:
                ref, half = shard_refs.pop(0), weight.rows // 2
                rows = pl.ds(pl.multiple_of(s[core] * half, half), half)
                for c in range(weight.width // PIECE):
                    ready[g].append(
                        copies.start(
                            ref.at[rows, c * PIECE : (c + 1) * PIECE],
                            staged[g].at[weight.first + c * half : weight.first + (c + 1) * half, :],
                        )
                    )
        copies.wait(*loads)
        used = [r[...].astype(F32).reshape(1, -1) for r in held]
        row = jnp.concatenate(used[:-1], axis=1)
        last = jnp.concatenate([used[-1], jnp.zeros((1, PIECE - used[-1].shape[1]), F32)], axis=1)
        rest = jnp.zeros((SMALL - 2, PIECE), F32)
        staged[0][groups[0].height :, :] = jnp.concatenate([row, last, rest], axis=0).astype(BF)
        for g in range(len(groups)):
            copies.wait(*ready[g])
            copies.start(staged[g], outs[g])
        copies.end()

    return pallas(
        body,
        "pack",
        table,
        vectors + shards,
        outs,
        [vmem(*o.shape) for o in outs] + [vmem(*v.shape) for v in vectors],
        1,
    )


def project(table, group, tokens, small):
    tok, d = tokens.shape
    used = (0, 1, 2)
    extra = group.operands(used)
    fsdp, part = group.fsdp, d // group.fsdp
    wide = 4 * d // fsdp

    def body(s, x_hbm, small_hbm, *refs):
        pieces, outs, refs = refs[: len(extra)], refs[len(extra) : len(extra) + 8], refs[len(extra) + 8 :]
        x_ref, res_ref, vec_ref, bias_ref, all_small, small_sem, *weights, weight_sems, sems = refs
        copies = Copies(sems)
        tokens_in = copies.start(x_hbm, x_ref)
        group.load(used, s, pieces, weights, weight_sems)
        if group.fast:
            own = small_hbm.at[small_hbm.shape[0] - SMALL :, :]
            pltpu.make_async_copy(own, all_small.at[s[0]], small_sem).start()
            for piece, (_, sources, mate) in zip(pieces[len(used) :], group.pieces):
                if not mate:
                    pltpu.make_async_copy(
                        piece.at[group.height : group.height + SMALL, :], all_small.at[s[sources[0]]], small_sem
                    ).start()
        else:
            pltpu.make_async_copy(small_hbm, all_small, small_sem).start()
        pltpu.make_async_copy(all_small, all_small, small_sem).wait()
        rows = [all_small[f].astype(F32) for f in range(fsdp)]
        for v in range(8):
            vec_ref[v : v + 1, :] = jnp.concatenate([r[0:1, v * part : (v + 1) * part] for r in rows], axis=1)
        bias_ref[...] = jnp.zeros_like(bias_ref)
        bias_ref[0:1, :] = jnp.concatenate([r[1:2, :wide] for r in rows], axis=1)
        copies.start(vec_ref, outs[3])
        copies.start(bias_ref, outs[4])
        copies.wait(tokens_in)
        for n, weight in enumerate(weights):
            group.wait_one(n, weights, weight_sems)
            copies.start(weight, outs[5 + n])
            result = dot(x_ref[...], weight[...])
            if n == 0:
                result = (result + vec_ref[0:1, :]).astype(BF) * jnp.asarray(1.0 / math.sqrt(DH), BF)
            if n == 2:
                result = result + vec_ref[1:2, :]
            res_ref[n] = result.astype(BF)
            copies.start(res_ref.at[n], outs[n])
        copies.end()

    return pallas(
        body,
        "project",
        table,
        [tokens, small] + extra,
        [struct((tok, d), BF)] * 3
        + [struct((8, d), F32), struct((8, 4 * d), F32)]
        + [struct(group.full(k), BF) for k in used],
        [vmem(tok, d), vmem(3, tok, d), vmem(8, d, dtype=F32), vmem(8, 4 * d, dtype=F32)]
        + [vmem(fsdp, SMALL, d), pltpu.SemaphoreType.DMA]
        + group.scratch(used),
        6 * tok * d * d,
    )


SMALL = 16


def forward_block(table, inner, outer, context, tokens, out_grad, vectors, bias_inner):
    tok, d = tokens.shape
    ff = inner.full(1)[1]
    extra_inner, extra_outer = inner.operands((0, 1)), outer.operands((0,))
    count = len(extra_inner)
    extra = extra_inner + extra_outer
    rows, wide = struct((tok, d), BF), struct((tok, ff), BF)
    half, part = d // 2, ff // OWNERS
    outs = [rows, struct((tok, d), F32), rows, wide, struct((tok, d), F32), rows, struct((SUMS, d), F32)]
    outs += [struct((OWNERS, half, part), BF)] * 2
    outs += [struct(inner.full(0), BF), struct(inner.full(1), BF), struct(outer.full(0), BF)]

    def body(s, ctx_hbm, x_hbm, g_hbm, vec_hbm, bias_hbm, *refs):
        pieces, refs = refs[: len(extra)], refs[len(extra) :]
        out_hbm, hid_hbm, low_hbm, slope_hbm, second_hbm, grad_hbm, sum_hbm, mine_hbm, other_hbm = refs[:9]
        w_out_hbm, w_in_hbm, w_outer_hbm = refs[9:12]
        ctx_ref, x_ref, g_ref, vec_ref, bias_ref, hid_ref, low_ref, act_ref, slope_ref = refs[12:21]
        total, sum_ref, both, w_out, w_in, inner_sems, w_outer, outer_sems, sems = refs[21:]
        core = s[table.shape[0] - 1]
        copies = Copies(sems)
        loads = [copies.start(a, b) for a, b in ((ctx_hbm, ctx_ref), (x_hbm, x_ref), (vec_hbm, vec_ref))]
        inner.load((0, 1), s, pieces[:count], (w_out, w_in), inner_sems)
        outer.load((0,), s, pieces[count:], (w_outer,), outer_sems)
        later = [copies.start(bias_hbm, bias_ref), copies.start(g_hbm, g_ref)]
        sum_ref[...] = jnp.zeros_like(sum_ref)
        copies.wait(*loads)
        inner.wait_one(0, (w_out,), inner_sems)
        copies.start(w_out, w_out_hbm)
        hidden = x_ref[...].astype(F32) + dot(ctx_ref[...], w_out[...]) + vec_ref[2:3, :]
        hid_ref[...] = hidden
        hidden_out = copies.start(hid_ref, hid_hbm)
        normed, _ = norm(hidden)
        first = normed * vec_ref[3:4, :] + vec_ref[4:5, :]
        low_ref[...] = first.astype(BF)
        low_out = copies.start(low_ref, low_hbm)
        total[...] = first + vec_ref[5:6, :]
        inner.wait_one(1, (w_out, w_in), inner_sems)
        copies.start(w_in, w_in_hbm)
        outer.wait_one(0, (w_outer,), outer_sems)
        copies.start(w_outer, w_outer_hbm)
        copies.wait(*later)
        for c in range(0, ff, d):
            cols = slice(c, c + d)
            act, slope = gelu_parts(dot(low_ref[...], w_in[:, cols]) + bias_ref[0:1, cols])
            act = act.astype(BF)
            act_ref[:, cols] = act
            slope_ref[:, cols] = slope.astype(BF)
            copies.start(slope_ref.at[:, cols], slope_hbm.at[:, cols])
            total[...] += dot(act, w_outer[cols, :])
        normed, inverse = norm(total[...])
        gain = vec_ref[6:7, :]
        x_ref[...] = (normed * gain + vec_ref[7:8, :]).astype(BF)
        copies.start(x_ref, out_hbm)
        grad = g_ref[...].astype(F32)
        sum_ref[2:3, :] = column_sum(grad * normed)
        sum_ref[3:4, :] = column_sum(grad)
        second = norm_back(grad * gain, normed, inverse)
        low = second.astype(BF)
        ctx_ref[...] = low
        copies.start(ctx_ref, grad_hbm)
        copies.wait(hidden_out)
        hid_ref[...] = second
        copies.start(hid_ref, second_hbm)
        sum_ref[4:5, :] = column_sum(low.astype(F32))
        copies.start(sum_ref, sum_hbm)
        turned = low.T
        for i in range(0, OWNERS, 2):
            grads = dot(turned, act_ref[:, i * part : (i + 2) * part]).astype(BF)
            for k in (0, 1):
                columns = slice(k * part, (k + 1) * part)
                both[0, i + k], both[1, i + k] = grads[:half, columns], grads[half:, columns]
            pair = pl.ds(i, 2)
            copies.start(both.at[1 - core, pair], other_hbm.at[pair])
            copies.start(both.at[core, pair], mine_hbm.at[pair])
        copies.end()

    row = vmem(tok, d)
    return pallas(
        body,
        "forward_block",
        table,
        [context, tokens, out_grad, vectors, bias_inner] + extra,
        outs,
        [row, row, row, vmem(8, d, dtype=F32), vmem(8, ff, dtype=F32), vmem(tok, d, dtype=F32), row]
        + [vmem(tok, ff), vmem(tok, ff), vmem(tok, d, dtype=F32), vmem(SUMS, d, dtype=F32)]
        + [vmem(2, OWNERS, half, part)]
        + inner.scratch((0, 1))
        + outer.scratch((0,)),
        2 * tok * d * (d + 3 * ff),
        62,
    )


def active_back(choice, grad_low, slope, w_outer, first_low):
    tok, d = grad_low.shape
    ff = slope.shape[1]
    blocks = [slice(c, c + d) for c in range(0, ff, d)]
    half, rows, part = len(blocks) // 2, d // OWNERS, d // 2

    def body(s, g_hbm, slope_hbm, w_hbm, low_hbm, out_hbm, sum_hbm, mine_hbm, other_hbm, *refs):
        g_ref, slope_ref, w_ref, low_ref, out_ref, sum_ref, turned, held, sems = refs
        copies = Copies(sems)
        first = copies.start(g_hbm, g_ref)
        loads = [
            (copies.start(w_hbm.at[b, :], w_ref.at[b, :]), copies.start(slope_hbm.at[:, b], slope_ref.at[:, b]))
            for b in blocks
        ]
        left = copies.start(low_hbm, low_ref)
        sum_ref[...] = jnp.zeros_like(sum_ref)
        copies.wait(first)
        for n, b in enumerate(blocks):
            copies.wait(*loads[n])
            low = (dot_right(g_ref[...], w_ref[b, :]) * slope_ref[:, b].astype(F32)).astype(BF)
            out_ref[:, b] = low
            copies.start(out_ref.at[:, b], out_hbm.at[:, b])
            sum_ref[8 + n : 9 + n, :] = column_sum(low.astype(F32))
            if n == 0:
                copies.wait(left)
                turned[...] = low_ref[...].T
            grads = dot(turned[...], low).astype(BF)
            for k in range(0, d, part):
                at = (n % half * d + k) // part * rows
                held[n // half, :, at : at + rows, :] = grads[:, k : k + part].reshape(OWNERS, rows, part)
        copies.start(held.at[1 - s[0]], other_hbm)
        copies.start(held.at[s[0]], mine_hbm)
        copies.start(sum_ref, sum_hbm)
        copies.end()

    grad = struct((OWNERS, rows * ff // (2 * part), part), BF)
    return pallas(
        body,
        "active_back",
        choice,
        [grad_low, slope, w_outer, first_low],
        [struct((tok, ff), BF), struct((SUMS, d), F32), grad, grad],
        [vmem(tok, d), vmem(tok, ff), vmem(ff, d), vmem(tok, d), vmem(tok, ff), vmem(SUMS, d, dtype=F32)]
        + [vmem(d, tok), vmem(2, *grad.shape)],
        4 * tok * d * ff,
    )


def inner_back(choice, grad_inner, grad_second, hidden, vectors, w_out, w_in, context):
    tok, d = hidden.shape
    ff, half = grad_inner.shape[1], d // 2
    blocks = [slice(c, c + 2 * d) for c in range(0, ff, 2 * d)]

    def body(s, g_hbm, second_hbm, hid_hbm, vec_hbm, w_out_hbm, w_in_hbm, *refs):
        left_hbm, out_hbm, ctx_hbm, sum_hbm, mine_hbm, other_hbm = refs[:6]
        g_ref, second_ref, hid_ref, vec_ref, w_out, w_in, left_ref, ctx_ref, sum_ref, held, sems = refs[6:]
        copies = Copies(sems)
        loads = [
            (copies.start(g_hbm.at[:, b], g_ref.at[:, b]), copies.start(w_in_hbm.at[:, b], w_in.at[:, b]))
            for b in blocks[:1]
        ]
        first = copies.start(second_hbm, second_ref)
        loads += [
            (copies.start(g_hbm.at[:, b], g_ref.at[:, b]), copies.start(w_in_hbm.at[:, b], w_in.at[:, b]))
            for b in blocks[1:]
        ]
        later = [copies.start(a, b) for a, b in ((hid_hbm, hid_ref), (vec_hbm, vec_ref), (w_out_hbm, w_out))]
        later.append(copies.start(left_hbm, left_ref))
        sum_ref[...] = jnp.zeros_like(sum_ref)
        for n, b in enumerate(blocks):
            copies.wait(*loads[n])
            part = dot_right(g_ref[:, b], w_in[:, b])
            if n == 0:
                copies.wait(first)
            second_ref[...] += part
        copies.wait(*later)
        grad = second_ref[...]
        normed, inverse = norm(hid_ref[...])
        sum_ref[5:6, :] = column_sum(grad * normed)
        sum_ref[6:7, :] = column_sum(grad)
        hidden_grad = norm_back(grad * vec_ref[3:4, :], normed, inverse)
        second_ref[...] = hidden_grad
        copies.start(second_ref, out_hbm)
        low = hidden_grad.astype(BF)
        ctx_ref[...] = dot_right(low, w_out[...]).astype(BF)
        copies.start(ctx_ref, ctx_hbm)
        grads = dot(left_ref[...].T, low).astype(BF)
        for k in (0, 1):
            held[k] = grads[:, k * half : (k + 1) * half].reshape(OWNERS, d // OWNERS, half)
        copies.start(held.at[1 - s[0]], other_hbm)
        copies.start(held.at[s[0]], mine_hbm)
        sum_ref[7:8, :] = column_sum(low.astype(F32))
        copies.start(sum_ref, sum_hbm)
        copies.end()

    full, grad = vmem(tok, d, dtype=F32), struct((OWNERS, d // OWNERS, half), BF)
    return pallas(
        body,
        "inner_back",
        choice,
        [grad_inner, grad_second, hidden, vectors, w_out, w_in, context],
        [struct((tok, d), F32), struct((tok, d), BF), struct((SUMS, d), F32), grad, grad],
        [vmem(tok, ff), full, full, vmem(8, d, dtype=F32), vmem(d, d), vmem(d, ff), vmem(tok, d), vmem(tok, d)]
        + [vmem(SUMS, d, dtype=F32), vmem(2, *grad.shape)],
        2 * tok * d * (2 * d + ff),
    )


def tokens_back(choice, grad_hidden, mine, other, weights):
    tok, d = grad_hidden.shape
    half = d // 2

    def body(s, hid_hbm, mine_hbm, other_hbm, *refs):
        weights, out_hbm, hid_ref, grad_ref, w_ref, out_ref, sems = refs[:3], *refs[3:]
        copies = Copies(sems)
        loads = []
        for n, weight in enumerate(weights):
            loads.append([copies.start(weight, w_ref.at[n])])
            for grad, side in ((other_hbm, 1 - s[0]), (mine_hbm, s[0])):
                cols = pl.ds(pl.multiple_of(side * half, half), half)
                loads[-1].append(
                    copies.start(grad.at[:, n * half : (n + 1) * half], grad_ref.at[n, :, cols])
                )
            if n == 0:
                first = copies.start(hid_hbm, hid_ref)
        for n, load in enumerate(loads):
            copies.wait(*load)
            part = dot_right(grad_ref[n], w_ref[n])
            copies.wait(first)
            if n < 2:
                hid_ref[...] += part
            else:
                out_ref[...] = (hid_ref[...] + part).astype(BF)
        copies.start(out_ref, out_hbm)
        copies.end()

    return pallas(
        body,
        "tokens_back",
        choice,
        [grad_hidden, mine, other, *weights],
        [struct((tok, d), BF)],
        [vmem(tok, d, dtype=F32), vmem(3, tok, d), vmem(3, d, d), vmem(tok, d)],
        6 * tok * d * d,
    )[0]


def axis_step(value, axis):
    if axis == "x":
        return rep_step(value, 2)
    return lax.ppermute(value, "fsdp", [(f, f ^ 1) for f in range(8)])


def after(value, *events):
    return lax.optimization_barrier((value,) + events)[0] if events else value


def added(*terms):
    total = terms[0].astype(F32)
    for term in terms[1:]:
        total = total + term.astype(F32)
    return total.astype(BF)


def chosen(parts, bit, axis):
    return lax.dynamic_index_in_dim(parts, bit, axis, keepdims=False)


def halves(value, bit, axis):
    owners, rows, n = value.shape
    if axis == "y":
        return chosen(value.reshape(owners // 2, 2, rows, n), bit, 1)
    return chosen(value.reshape(owners, 2, rows // 2, n), bit, 1)


class Stream:
    def __init__(self, place, terms, order):
        self.place, self.terms, self.order = place, terms, order

    def move(self, axis, *events):
        bit = self.place.x if axis == "x" else self.place.y
        terms = self.terms[:-1] + [after(self.terms[-1], *events)]
        send = added(*(halves(v, 1 - bit, axis) for v in terms))
        self.terms = [added(*(halves(v, bit, axis) for v in terms)), axis_step(send, axis)]
        return [send]

    def first(self, *events):
        return self.move(self.order[0], *events)

    def second(self, *events):
        return self.move(self.order[1], *events)


class Owned:
    def __init__(self, place, mine, received):
        self.place, self.mine, self.received = place, mine, received

    def first(self, *events):
        mid, received = self.mine.shape[1] // 2, after(self.received, *events)
        self.streams = [
            Stream(self.place, [self.mine[:, :mid], received[:, :mid]], "xy"),
            Stream(self.place, [self.mine[:, mid:], received[:, mid:]], "yx"),
        ]
        return [s for stream in self.streams for s in stream.first()]

    def second(self, *events):
        return [s for stream in self.streams for s in stream.second(*events)]

    def third(self, *events):
        sums = [added(*s.terms[:-1], after(s.terms[-1], *events)) for s in self.streams]
        parts = jnp.concatenate(sums, 1)
        z = self.place.z
        sent = [chosen(parts, (z + k) % 4, 0) for k in (1, 3, 2)]
        moved = [
            lax.ppermute(v, "fsdp", [(f, (f // 2 + k) % 4 * 2 + f % 2) for f in range(8)])
            for v, k in zip(sent, (1, 3, 2))
        ]
        self.terms = [chosen(parts, z, 0)] + moved
        return sent

    def fourth(self, *events):
        self.own = added(*self.terms[:-1], after(self.terms[-1], *events))
        self.other = rep_step(self.own, 2)
        return [self.own]

    def fifth(self, *events):
        other = after(self.other, *events)
        low = jnp.where(self.place.x == 0, self.own, other)
        high = jnp.where(self.place.x == 0, other, self.own)
        mid = low.shape[0] // 2
        half = jnp.concatenate([low[:mid], high[:mid], low[mid:], high[mid:]], 0)
        self.both = (half, rep_step(half, 1))
        return [half]

    def last(self):
        mine, mate = self.both
        first = self.place.core == 0
        return jnp.where(first, mine, mate), jnp.where(first, mate, mine)


class Place:
    def __init__(self, mesh):
        f, r = lax.axis_index("fsdp"), lax.axis_index("rep")
        self.f, self.core, self.x = f, r % 2, r // 2
        self.y, self.z = f % 2, f // 2
        self.choice = jnp.stack([self.core, self.x, self.y]).astype(jnp.int32)
        if mesh.shape["fsdp"] == len(RING):
            row = lax.dynamic_index_in_dim(jnp.array(ring_table(), jnp.int32), f, 0, keepdims=False)
            self.table = jnp.concatenate([row, self.core[None].astype(jnp.int32)])
        else:
            self.table = jnp.zeros((1,), jnp.int32)


class Ring:
    def __init__(self, group, payload, last):
        self.group, self.ways, self.last, self.count = group, {1: [payload], -1: [payload]}, last, 0

    def ways_of(self, count):
        return (1, -1) if count < len(RING) // 2 else (self.last,)

    def source(self, way, count):
        return count if way == 1 or count == len(RING) // 2 else len(RING) // 2 + count

    @property
    def came(self):
        return tuple(self.ways[way][self.count] for way in self.ways_of(self.count))

    def step(self, *events):
        self.count += 1
        for way in self.ways_of(self.count):
            self.ways[way].append(ring_step(after(self.ways[way][-1], *events), way))
            self.group.pieces.append((self.ways[way][-1], (self.source(way, self.count),), False))

    def share(self, count, *events):
        shared = []
        for way in self.ways_of(count):
            shared.append(rep_step(after(self.ways[way][count], *events), 1))
            self.group.pieces.append((shared[-1], (self.source(way, count),), True))
        return shared


class Travel:
    def __init__(self, rings):
        self.rings, self.going, self.shared, self.seen = rings, (), (), ()

    def round(self, *order, events=()):
        came = tuple(v for n in self.going for v in self.rings[n].came)
        counts = [(n, self.rings[n].count) for n in self.going]
        self.seen = came + self.shared
        for n in order:
            self.rings[n].step(*events, *self.seen)
        self.shared = tuple(v for n, count in counts for v in self.rings[n].share(count, *events, *came))
        self.going = order

    def finish(self, *events):
        for n in self.going:
            self.rings[n].share(self.rings[n].count, *events)


def local(mesh, *args):
    (
        tokens, seq_ids, key_mask, weight_query, bias_query, weight_key, weight_value, bias_value,
        weight_out, bias_out, norm1_gain, norm1_bias, weight_inner, bias_inner, weight_outer, bias_outer,
        norm2_gain, norm2_bias, out_grad,
    ) = args
    place = Place(mesh)
    choice, table = place.choice, place.table
    fsdp = mesh.shape["fsdp"]
    d = tokens.shape[1]
    win = windows(seq_ids[0])
    narrow = [bias_query, bias_value, bias_out, norm1_gain, norm1_bias, bias_outer, norm2_gain, norm2_bias]
    shards = [[weight_query, weight_key, weight_value], [weight_out, weight_inner], [weight_outer]]
    fast = all(fast_path(mesh, s) for s in shards)
    if fast:
        groups = [Group(mesh, s) for s in shards]
        packed = pack(table, groups, narrow + [bias_inner])
        rings = [Ring(g, p, way) for g, p, way in zip(groups, packed, (1, -1, 1))]
        small = packed[0]
        travel = Travel(rings)
        travel.round(0, 1)
        travel.round(0, 2)
        travel.round(0, 1)
        travel.round(0, 2)
        travel.round(1, 2)
    else:
        groups = [Group(mesh, [lax.all_gather(w, "fsdp", axis=0, tiled=True) for w in s]) for s in shards]
        rows = [jnp.concatenate(narrow), bias_inner]
        rows = [jnp.concatenate([r, jnp.zeros((d - r.size,), BF)])[None] for r in rows]
        small = jnp.concatenate(rows + [jnp.zeros((SMALL - 2, d), BF)], 0)
        small = lax.all_gather(small, "fsdp", axis=0, tiled=False)
    qkv, inner_group, outer_group = groups

    q, k, v, vectors, full_bias_inner, *weights = project(table, qkv, tokens, small)
    if fast:
        travel.round(1, 2, events=(q,))
        q = after(q, *travel.seen)
    context, probs = attend(win, seq_ids, key_mask, q, k, v)
    if fast:
        travel.finish(context)
    (
        layer_out, hidden, first_low, slope, grad_second, grad_outer, sums2, outer_mine, outer_other,
        w_out, w_in, w_outer,
    ) = forward_block(
        place_table(table, choice), inner_group, outer_group, context, tokens, out_grad, vectors, full_bias_inner
    )
    if not fast:
        choice = jnp.zeros((3,), jnp.int32)
    if fast:
        outer_sum = Owned(place, outer_mine, rep_step(outer_other, 1))
    grad_inner, sums_inner, inner_mine, inner_other = active_back(choice, grad_outer, slope, w_outer, first_low)
    if fast:
        inner_sum = Owned(place, inner_mine, rep_step(inner_other, 1))
        event = outer_sum.first(inner_mine)
        grad_inner = after(grad_inner, *event)
    grad_hidden, grad_context, sums1, out_mine, out_other = inner_back(
        choice, grad_inner, grad_second, hidden, vectors, w_out, w_in, context
    )
    if fast:
        event = outer_sum.second(out_mine)
        event += inner_sum.first(out_mine)
        grad_context = after(grad_context, *event)
    place_win = jnp.concatenate([choice, win])
    grads_other, sums_other, query_other = attend_back(
        place_win, 1, q, k, v, context, grad_context, probs, tokens, out_other
    )
    if fast:
        event = inner_sum.second(grads_other)
        event += outer_sum.third(grads_other)
        query_came = rep_step(after(query_other, *event), 1)
        grad_context = after(grad_context, *event)
    grads_mine, sums_mine, query_mine = attend_back(
        place_win, 0, q, k, v, context, grad_context, probs, tokens, out_mine
    )
    sums_att = by_core(choice[0], sums_mine, sums_other, 1)
    sums = sums1 + sums2 + sums_inner + sums_att
    if fast:
        query_sum = Owned(place, query_mine, query_came)
        event = query_sum.first(query_mine)
        event += inner_sum.third(*event)
        sums = sums + after(rep_step(sums, 1), *event)
        event += outer_sum.fourth(*event)
        sums = sums + after(rep_step(sums, 2), *event)
        event = query_sum.second(sums, *event)
        sums = sums + after(axis_step(sums, "y"), *event)
        event += outer_sum.fifth(*event)
        event += inner_sum.fourth(*event)
        event = query_sum.third(sums, *event)
        grad_hidden = after(grad_hidden, *event)
    grad_tokens = tokens_back(choice, grad_hidden, grads_mine, grads_other, weights)
    if fast:
        event = query_sum.fourth(grad_tokens)
        sums = sums + after(z_step(sums, 1), *event)
        inner_sum.fifth(*event)
        low, high = outer_sum.last()
        final_outer = jnp.concatenate([low, high], 0).T.astype(F32)
        sums = sums + after(z_step(sums, 2), final_outer)
        low, high = inner_sum.last()
        rows = d // fsdp
        blocks = [v[c : c + rows] for v in (low, high) for c in range(0, v.shape[0], rows)]
        final_inner = jnp.concatenate(blocks, 1).astype(F32)
        query_sum.fifth(final_outer, final_inner)
        low, high = query_sum.last()
        final_query, final_key, final_value, final_out = (
            jnp.concatenate([low[c : c + rows], high[c : c + rows]], 1).astype(F32)
            for c in range(0, 4 * rows, rows)
        )
    else:

        def plain(*blocks):
            total = jnp.concatenate(blocks, 2)
            total = total.reshape(-1, total.shape[2])
            owned = lax.psum_scatter(total, "fsdp", scatter_dimension=0, tiled=True)
            return lax.psum(owned, "rep").astype(F32)

        sums = lax.psum(sums, ("fsdp", "rep"))
        final_outer = plain(jnp.concatenate([outer_mine, outer_other], 1).transpose(0, 2, 1))
        part = d // OWNERS
        unstack = lambda v: [v[:, c : c + part] for c in range(0, v.shape[1], part)]
        final_inner = plain(*unstack(inner_mine), *unstack(inner_other))
        final_query, final_key, final_value, final_out = (
            plain(a, b) for a, b in zip(unstack(query_mine), unstack(query_other))
        )

    narrow_sums = lax.dynamic_slice_in_dim(sums, place.f * (d // fsdp), d // fsdp, 1)
    inner_sums = lax.dynamic_slice_in_dim(sums[8:12].reshape(-1), place.f * bias_inner.size, bias_inner.size, 0)
    return (
        layer_out,
        grad_tokens,
        final_query,
        narrow_sums[0],
        final_key,
        final_value,
        narrow_sums[1],
        final_out,
        narrow_sums[7],
        narrow_sums[5],
        narrow_sums[6],
        final_inner,
        inner_sums,
        final_outer,
        narrow_sums[4],
        narrow_sums[2],
        narrow_sums[3],
    )


def by_core(core, mine, other, axis):
    return jnp.where(core == 0, jnp.concatenate([mine, other], axis), jnp.concatenate([other, mine], axis))


def z_step(value, bits):
    return lax.ppermute(value, "fsdp", [(f, f ^ (2 * bits)) for f in range(8)])


def place_table(table, choice):
    return jnp.concatenate([table[:-1], choice[:1]]) if table.shape[0] > 1 else jnp.zeros((1,), jnp.int32)


def solution(mesh):
    rows, shard, part = P(("fsdp", "rep"), None), P("fsdp", None), P("fsdp")
    return jax.shard_map(
        functools.partial(local, mesh),
        mesh=mesh,
        in_specs=(
            rows, rows, rows, shard, part, shard, shard, part, shard, part, part, part, shard, part, shard,
            part, part, part, rows,
        ),
        out_specs=(
            rows, rows, shard, part, shard, shard, part, shard, part, part, part, shard, part, shard, part,
            part, part,
        ),
        check_vma=False,
    )
```

```python
import functools
import math

import jax
import jax.numpy as jnp
from jax import lax
from jax.experimental import pallas as pl
from jax.experimental.pallas import tpu as pltpu
from jax.sharding import PartitionSpec as P

HEADS = 12
DH = 64
BF = jnp.bfloat16
F32 = jnp.float32
NEGATIVE = -1e30
EPSILON = 1e-12
QB = 128
KB = 128
SPAN = 5
ROWS = 1024
VMEM = 60 * 1024 * 1024
COST = 0.05
ANY = pl.BlockSpec(memory_space=pl.ANY)


def dot(left, right):
    return jnp.dot(left, right, preferred_element_type=F32)


def dot_right(left, right):
    return lax.dot_general(left, right, (((1,), (1,)), ((), ())), preferred_element_type=F32)


def params(steps=1):
    return pltpu.CompilerParams(
        dimension_semantics=("arbitrary",) * steps, vmem_limit_bytes=VMEM
    )


def cost(flops, size):
    return pl.CostEstimate(flops=int(flops * COST), bytes_accessed=int(size * COST), transcendentals=0)


def struct(shape, dtype):
    return jax.ShapeDtypeStruct(shape, dtype)


def whole(shape):
    return pl.BlockSpec(shape, lambda i, s: (0,) * len(shape))


def rows_of(width, height=ROWS):
    return pl.BlockSpec((height, width), lambda i, s: (i, 0))


def norm(hidden):
    center = hidden - jnp.mean(hidden, axis=-1, keepdims=True)
    inverse = lax.rsqrt(jnp.mean(center * center, axis=-1, keepdims=True) + EPSILON)
    return center * inverse, inverse


def norm_back(grad, normed, inverse):
    mean = jnp.mean(grad, axis=-1, keepdims=True)
    along = jnp.mean(grad * normed, axis=-1, keepdims=True)
    return inverse * (grad - mean - normed * along)


def gelu_parts(inner):
    phi = 0.5 + 0.5 * lax.erf(inner * 0.7071067811865476)
    density = jnp.exp((-0.5 * inner) * inner) * 0.3989422804014327
    return inner * phi, phi + inner * density


def column_sum(value):
    return jnp.sum(value, axis=0, keepdims=True)


def windows(seq_row):
    tiles = seq_row.reshape(seq_row.shape[0] // QB, QB)
    below = jnp.sum((seq_row[None] < tiles[:, :1]).astype(jnp.int32), axis=1)
    upto = jnp.sum((seq_row[None] <= tiles[:, -1:]).astype(jnp.int32), axis=1)
    low = below // KB
    return jnp.concatenate([low, (upto + KB - 1) // KB - low])


def first_half(shape):
    return lax.broadcasted_iota(jnp.int32, shape, len(shape) - 1) < DH


def stack_pair(pair):
    low = first_half(pair.shape)
    zero = jnp.zeros_like(pair)
    return jnp.concatenate([jnp.where(low, pair, zero), jnp.where(low, zero, pair)], axis=0)


def fold_pair(both):
    half = both.shape[0] // 2
    return jnp.where(first_half((half, both.shape[1])), both[:half], both[half:])


def attend(win, seq, mask, q, k, v):
    tok, d = q.shape
    tiles, pairs = tok // QB, d // (2 * DH)

    def kernel(win, seq_hbm, mask_hbm, q_hbm, k_hbm, v_hbm, ctx_hbm, p_hbm, *refs):
        seq_ref, mask_ref, q_ref, k_ref, v_ref, ctx_ref, p_ref, bias_ref, s_ref, p_sems, ctx_sems, sems = refs
        copies = Copies(sems)
        for source, target in (
            (seq_hbm, seq_ref), (mask_hbm, mask_ref), (k_hbm, k_ref), (q_hbm, q_ref), (v_hbm, v_ref)
        ):
            copies.start(source, target)
        copies.end()

        def store(i):
            rows = pl.ds(pl.multiple_of(i * QB, QB), QB)
            return (
                pltpu.make_async_copy(p_ref.at[i], p_hbm.at[i], p_sems.at[i]),
                pltpu.make_async_copy(ctx_ref.at[rows, :], ctx_hbm.at[rows, :], ctx_sems.at[i]),
            )

        def tile(i, n):
            w = n * KB
            base = pl.multiple_of(win[i] * KB, KB)
            start = pl.multiple_of(i * QB, QB)
            rows_now = pl.ds(start, QB)
            for pair in range(pairs):
                lanes = slice(pair * 2 * DH, (pair + 1) * 2 * DH)
                s_ref[pair, :, :w] = dot_right(stack_pair(q_ref[rows_now, lanes]), k_ref[pl.ds(base, w), lanes])
            own = jnp.broadcast_to(seq_ref[:, pl.ds(start, QB)], (QB, QB)).T
            rows = start + lax.broadcasted_iota(jnp.int32, (QB, KB), 0)
            for b in range(n):
                off = pl.multiple_of(base + b * KB, KB)
                cols = off + lax.broadcasted_iota(jnp.int32, (QB, KB), 1)
                visible = (mask_ref[:, pl.ds(off, KB)] == 1) | (rows == cols)
                allowed = (own == seq_ref[:, pl.ds(off, KB)]) & visible
                bias_ref[:, b * KB : (b + 1) * KB] = jnp.where(allowed, 0.0, NEGATIVE).astype(F32)
            ones = jnp.ones((w, 2 * DH), BF)
            expons = []
            for pair in range(pairs):
                bias = bias_ref[:, :w]
                scores = s_ref[pair, :, :w] + jnp.concatenate([bias, bias], axis=0)
                expons.append(jnp.exp(scores - jnp.max(scores, axis=1, keepdims=True)).astype(BF))
            for pair, expon in enumerate(expons):
                lanes = slice(pair * 2 * DH, (pair + 1) * 2 * DH)
                mixed = dot(expon, jnp.concatenate([v_ref[pl.ds(base, w), lanes], ones], axis=1))
                scale = 1.0 / mixed[:, 2 * DH :]
                ctx_ref[rows_now, lanes] = fold_pair(mixed[:, : 2 * DH] * scale).astype(BF)
                for b in range(n):
                    p_ref[i, pair, :, b * KB : (b + 1) * KB] = (
                        expon[:, b * KB : (b + 1) * KB].astype(F32) * scale
                    ).astype(BF)

        def step(i, carry):
            for n in range(1, SPAN + 1):
                pl.when(win[tiles + i] == n)(functools.partial(tile, i, n))
            for copy in store(i):
                copy.start()
            return carry

        lax.fori_loop(0, tiles, step, 0)
        for i in range(tiles):
            for copy in store(i):
                copy.wait()

    wide = (tiles, pairs, 2 * QB, SPAN * KB)
    return pallas(
        kernel,
        "attend",
        win,
        [seq, mask, q, k, v],
        [struct((tok, d), BF), struct(wide, BF)],
        [pltpu.VMEM(seq.shape, jnp.int32), pltpu.VMEM(mask.shape, jnp.int32)]
        + [vmem(tok, d), vmem(tok, d), vmem(tok, d), vmem(tok, d), vmem(*wide)]
        + [vmem(QB, SPAN * KB, dtype=F32), vmem(pairs, 2 * QB, SPAN * KB, dtype=F32)]
        + [pltpu.SemaphoreType.DMA((tiles,)), pltpu.SemaphoreType.DMA((tiles,))],
        1.4e10,
    )


def attend_back(place_win, side, q, k, v, ctx, do, p, tokens, out_grad):
    tok, d = q.shape
    half, rows = d // 2, d // OWNERS
    tiles, pairs = tok // QB, half // (2 * DH)

    def kernel(s, q_hbm, k_hbm, v_hbm, ctx_hbm, do_hbm, p_hbm, x_hbm, out_hbm, grad_hbm, sum_hbm, w_hbm, *refs):
        q_ref, k_ref, v_ref, ctx_ref, do_ref, p_ref, x_ref, out_ref, grad_ref, sum_ref, w_ref = refs[:11]
        dkt, dvt, s_ref, p_sems, sems = refs[11:]
        pick = s[0] if side == 0 else 1 - s[0]
        cols = pl.ds(pl.multiple_of(pick * half, half), half)
        chosen_pairs = pl.ds(pick * pairs, pairs)
        copies = Copies(sems)

        def load(i):
            return pltpu.make_async_copy(p_hbm.at[i, chosen_pairs], p_ref.at[i], p_sems.at[i])

        load(0).start()
        first = [
            copies.start(a.at[:, cols], b)
            for a, b in ((do_hbm, do_ref), (v_hbm, v_ref), (ctx_hbm, ctx_ref), (k_hbm, k_ref), (q_hbm, q_ref))
        ]
        for i in range(1, tiles):
            load(i).start()
        later = [copies.start(x_hbm, x_ref), copies.start(out_hbm, out_ref)]
        dkt[...] = jnp.zeros_like(dkt)
        dvt[...] = jnp.zeros_like(dvt)
        sum_ref[...] = jnp.zeros_like(sum_ref)
        copies.wait(*first)
        lanes = [slice(p * 2 * DH, (p + 1) * 2 * DH) for p in range(pairs)]

        def tile(i, n):
            w = n * KB
            base = pl.multiple_of(s[4 + i] * KB, KB)
            rows_now = pl.ds(pl.multiple_of(i * QB, QB), QB)
            for pair, ln in enumerate(lanes):
                s_ref[pair, :, :w] = dot_right(stack_pair(do_ref[rows_now, ln]), v_ref[pl.ds(base, w), ln])
            for pair, ln in enumerate(lanes):
                dvt[ln, pl.ds(base, w)] += dot(stack_pair(do_ref[rows_now, ln]).T, p_ref[i, pair, :, :w])
            scores = []
            for pair, ln in enumerate(lanes):
                along = do_ref[rows_now, ln].astype(F32) * ctx_ref[rows_now, ln].astype(F32)
                delta = jnp.sum(stack_pair(along), axis=1, keepdims=True)
                scores.append((p_ref[i, pair, :, :w].astype(F32) * (s_ref[pair, :, :w] - delta)).astype(BF))
            for pair, ln in enumerate(lanes):
                dq = fold_pair(dot(scores[pair], k_ref[pl.ds(base, w), ln])) * (1.0 / math.sqrt(DH))
                dq = dq.astype(BF)
                grad_ref[rows_now, ln] = dq
                sum_ref[0:1, ln] += column_sum(dq.astype(F32))
            for pair, ln in enumerate(lanes):
                dkt[ln, pl.ds(base, w)] += dot(stack_pair(q_ref[rows_now, ln]).T, scores[pair])

        def step(i, carry):
            load(i).wait()
            for n in range(1, SPAN + 1):
                pl.when(s[4 + tiles + i] == n)(functools.partial(tile, i, n))
            return carry

        lax.fori_loop(0, tiles, step, 0)
        for o in range(0, tok, QB):
            grad_ref[o : o + QB, half : 2 * half] = dkt[:, o : o + QB].T.astype(BF)
            dv = dvt[:, o : o + QB].T.astype(BF)
            grad_ref[o : o + QB, 2 * half :] = dv
            sum_ref[1:2, :] += column_sum(dv.astype(F32))
        copies.start(grad_ref, grad_hbm)
        copies.start(sum_ref, sum_hbm)
        copies.wait(*later)
        turned = x_ref[...].T
        for j in range(OWNERS):
            w_ref[spot(s, 0, 3, j)] = out_ref[j]
        for n in range(3):
            grads = dot(turned, grad_ref[:, n * half : (n + 1) * half]).astype(BF)
            for j in range(OWNERS):
                w_ref[spot(s, 0, n, j)] = grads[j * rows : (j + 1) * rows]
            if n == 1:
                copies.start(w_ref.at[0], w_hbm.at[0])
        copies.start(w_ref.at[1], w_hbm.at[1])
        copies.end()

    full = vmem(tok, half)
    return pallas(
        kernel,
        "attend_back",
        place_win,
        [q, k, v, ctx, do, p, tokens, out_grad],
        [struct((tok, 3 * half), BF), struct((SUMS, half), F32), struct((*PLACES, rows, half), BF)],
        [full, full, full, full, full, vmem(tiles, pairs, 2 * QB, SPAN * KB), vmem(tok, d)]
        + [vmem(*out_grad.shape), vmem(tok, 3 * half), vmem(SUMS, half, dtype=F32), vmem(*PLACES, rows, half)]
        + [vmem(half, tok, dtype=F32), vmem(half, tok, dtype=F32)]
        + [vmem(pairs, 2 * QB, SPAN * KB, dtype=F32), pltpu.SemaphoreType.DMA((tiles,))],
        2e10,
    )


class Weight:
    def __init__(self, shard, first):
        self.rows, self.width = shard.shape
        self.shard = shard
        self.first = first


class Group:
    def __init__(self, mesh, shards):
        self.fsdp = mesh.shape["fsdp"]
        self.fast = fast_path(mesh, shards)
        self.pieces = []
        self.weights = []
        first = 0
        for shard in shards:
            self.weights.append(Weight(shard, first))
            first += shard.size // (2 * PIECE)
        self.height = first

    def full(self, k):
        weight = self.weights[k]
        return (weight.rows * (self.fsdp if self.fast else 1), weight.width)

    def operands(self, used):
        if not self.fast:
            return [self.weights[k].shard for k in used]
        return [self.weights[k].shard for k in used] + [array for array, _, _ in self.pieces]

    def load(self, used, table, refs, targets, sems):
        if not self.fast:
            for n, target in enumerate(targets):
                pltpu.make_async_copy(refs[n], target, sems.at[n]).start()
            return
        core = table[self.fsdp]
        for n, k in enumerate(used):
            weight, target, sem = self.weights[k], targets[n], sems.at[n]
            half = weight.rows // 2
            base = pl.multiple_of(table[0] * weight.rows, weight.rows)
            pltpu.make_async_copy(refs[n], target.at[pl.ds(base, weight.rows), :], sem).start()
            for piece, (_, sources, mate) in zip(refs[len(used) :], self.pieces):
                side = (1 - core) if mate else core
                height = piece.shape[0] // len(sources)
                for order, source in enumerate(sources):
                    row = pl.multiple_of(table[source] * weight.rows + side * half, 16)
                    for c in range(weight.width // PIECE):
                        start = order * height + weight.first + c * half
                        pltpu.make_async_copy(
                            piece.at[start : start + half, :],
                            target.at[pl.ds(row, half), c * PIECE : (c + 1) * PIECE],
                            sem,
                        ).start()

    def wait(self, targets, sems):
        for n, target in enumerate(targets):
            pltpu.make_async_copy(target, target, sems.at[n]).wait()

    def wait_one(self, n, targets, sems):
        pltpu.make_async_copy(targets[n], targets[n], sems.at[n]).wait()

    def scratch(self, used):
        return [pltpu.VMEM(self.full(k), BF) for k in used] + [pltpu.SemaphoreType.DMA((len(used),))]


PIECE = 768
OWNERS = 8
SUMS = 16


def fast_path(mesh, shards):
    return (
        mesh.shape["fsdp"] == 8
        and mesh.shape["rep"] == 4
        and all(s.shape[0] % 32 == 0 and s.shape[1] % PIECE == 0 for s in shards)
    )


RING = (0, 2, 4, 6, 7, 5, 3, 1)


def ring_table():
    size = len(RING)
    place = {v: p for p, v in enumerate(RING)}
    steps = list(range(0, -(size // 2) - 1, -1)) + list(range(1, size - size // 2))
    return [[RING[(place[f] + s) % size] for s in steps] for f in range(size)]


def ring_step(value, step):
    size = len(RING)
    return lax.ppermute(value, "fsdp", [(RING[p], RING[(p + step) % size]) for p in range(size)])


def rep_step(value, bits):
    return lax.ppermute(value, "rep", [(r, r ^ bits) for r in range(4)])


def pallas(body, name, table, operands, outs, scratch, flops, limit=60):
    operands, outs = list(operands), list(outs)
    size = sum(o.size * o.dtype.itemsize for o in operands + outs)
    return pl.pallas_call(
        body,
        in_specs=[pl.BlockSpec(memory_space=pltpu.SMEM)] + [ANY] * len(operands),
        out_specs=[ANY] * len(outs),
        out_shape=outs,
        scratch_shapes=list(scratch) + [pltpu.SemaphoreType.DMA((COPIES,))],
        compiler_params=pltpu.CompilerParams(vmem_limit_bytes=limit << 20),
        cost_estimate=cost(flops, size),
        name=name,
    )(table, *operands)


COPIES = 48


class Copies:
    def __init__(self, sems):
        self.sems, self.started = sems, []

    def start(self, source, target):
        copy = pltpu.make_async_copy(source, target, self.sems.at[len(self.started)])
        copy.start()
        self.started.append([copy, False])
        return len(self.started) - 1

    def either(self, first, source, one, two):
        sem = self.sems.at[len(self.started)]
        copies = [pltpu.make_async_copy(source, target, sem) for target in (one, two)]
        pl.when(first)(copies[0].start)
        pl.when(jnp.logical_not(first))(copies[1].start)
        self.started.append([copies[0], False])

    def wait(self, *numbers):
        for n in numbers:
            if not self.started[n][1]:
                self.started[n][0].wait()
                self.started[n][1] = True

    def end(self):
        self.wait(*range(len(self.started)))


PLACES = (2, 2, 2, 4)


def spot(s, at, block, owner):
    flip = lambda bit, mine: mine if bit == 0 else 1 - mine
    x, y = flip(block % 2, s[at + 1]), flip(owner % 2, s[at + 2])
    z = lax.bitwise_and(owner // 2 - s[at + 3] + 4, 3)
    return (0, x, y, z) if block < 2 else (1, y, x, z)


def vmem(*shape, dtype=BF):
    return pltpu.VMEM(shape, dtype)


def pack(table, groups, vectors):
    shards = [w.shard for g in groups for w in g.weights]
    core = table.shape[0] - 1
    outs = [struct((g.height + (SMALL if g is groups[0] else 0), PIECE), BF) for g in groups]

    def body(s, *refs):
        vec_refs = refs[: len(vectors)]
        shard_refs = list(refs[len(vectors) : len(vectors) + len(shards)])
        outs, refs = refs[len(vectors) + len(shards) :][: len(groups)], refs[len(vectors) + len(shards) + len(groups) :]
        staged, held, sems = refs[: len(groups)], refs[len(groups) : -1], refs[-1]
        copies = Copies(sems)
        loads = [copies.start(r, h) for r, h in zip(vec_refs, held)]
        ready = []
        for g, group in enumerate(groups):
            ready.append([])
            for weight in group.weights:
                ref, half = shard_refs.pop(0), weight.rows // 2
                rows = pl.ds(pl.multiple_of(s[core] * half, half), half)
                for c in range(weight.width // PIECE):
                    ready[g].append(
                        copies.start(
                            ref.at[rows, c * PIECE : (c + 1) * PIECE],
                            staged[g].at[weight.first + c * half : weight.first + (c + 1) * half, :],
                        )
                    )
        copies.wait(*loads)
        used = [r[...].astype(F32).reshape(1, -1) for r in held]
        row = jnp.concatenate(used[:-1], axis=1)
        last = jnp.concatenate([used[-1], jnp.zeros((1, PIECE - used[-1].shape[1]), F32)], axis=1)
        rest = jnp.zeros((SMALL - 2, PIECE), F32)
        staged[0][groups[0].height :, :] = jnp.concatenate([row, last, rest], axis=0).astype(BF)
        for g in range(len(groups)):
            copies.wait(*ready[g])
            copies.start(staged[g], outs[g])
        copies.end()

    return pallas(
        body,
        "pack",
        table,
        vectors + shards,
        outs,
        [vmem(*o.shape) for o in outs] + [vmem(*v.shape) for v in vectors],
        1,
    )


def project(table, group, tokens, small):
    tok, d = tokens.shape
    used = (0, 1, 2)
    extra = group.operands(used)
    fsdp, part = group.fsdp, d // group.fsdp
    wide = 4 * d // fsdp

    def body(s, x_hbm, small_hbm, *refs):
        pieces, outs, refs = refs[: len(extra)], refs[len(extra) : len(extra) + 8], refs[len(extra) + 8 :]
        x_ref, res_ref, vec_ref, bias_ref, all_small, small_sem, *weights, weight_sems, sems = refs
        copies = Copies(sems)
        tokens_in = copies.start(x_hbm, x_ref)
        group.load(used, s, pieces, weights, weight_sems)
        if group.fast:
            own = small_hbm.at[small_hbm.shape[0] - SMALL :, :]
            pltpu.make_async_copy(own, all_small.at[s[0]], small_sem).start()
            for piece, (_, sources, mate) in zip(pieces[len(used) :], group.pieces):
                if not mate:
                    pltpu.make_async_copy(
                        piece.at[group.height : group.height + SMALL, :], all_small.at[s[sources[0]]], small_sem
                    ).start()
        else:
            pltpu.make_async_copy(small_hbm, all_small, small_sem).start()
        pltpu.make_async_copy(all_small, all_small, small_sem).wait()
        rows = [all_small[f].astype(F32) for f in range(fsdp)]
        for v in range(8):
            vec_ref[v : v + 1, :] = jnp.concatenate([r[0:1, v * part : (v + 1) * part] for r in rows], axis=1)
        bias_ref[...] = jnp.zeros_like(bias_ref)
        bias_ref[0:1, :] = jnp.concatenate([r[1:2, :wide] for r in rows], axis=1)
        copies.start(vec_ref, outs[3])
        copies.start(bias_ref, outs[4])
        copies.wait(tokens_in)
        for n, weight in enumerate(weights):
            group.wait_one(n, weights, weight_sems)
            copies.start(weight, outs[5 + n])
            result = dot(x_ref[...], weight[...])
            if n == 0:
                result = (result + vec_ref[0:1, :]).astype(BF) * jnp.asarray(1.0 / math.sqrt(DH), BF)
            if n == 2:
                result = result + vec_ref[1:2, :]
            res_ref[n] = result.astype(BF)
            copies.start(res_ref.at[n], outs[n])
        copies.end()

    return pallas(
        body,
        "project",
        table,
        [tokens, small] + extra,
        [struct((tok, d), BF)] * 3
        + [struct((8, d), F32), struct((8, 4 * d), F32)]
        + [struct(group.full(k), BF) for k in used],
        [vmem(tok, d), vmem(3, tok, d), vmem(8, d, dtype=F32), vmem(8, 4 * d, dtype=F32)]
        + [vmem(fsdp, SMALL, d), pltpu.SemaphoreType.DMA]
        + group.scratch(used),
        6 * tok * d * d,
    )


SMALL = 16


def forward_block(table, inner, outer, context, tokens, out_grad, vectors, bias_inner):
    tok, d = tokens.shape
    ff = inner.full(1)[1]
    extra_inner, extra_outer = inner.operands((0, 1)), outer.operands((0,))
    count = len(extra_inner)
    extra = extra_inner + extra_outer
    rows, wide = struct((tok, d), BF), struct((tok, ff), BF)
    half, part = d // 2, ff // OWNERS
    place = (*PLACES, half // 4, part)
    outs = [rows, struct((tok, d), F32), rows, wide, struct((tok, d), F32), rows, struct((SUMS, d), F32)]
    outs += [struct(place, BF)] * 2
    outs += [struct(inner.full(0), BF), struct(inner.full(1), BF), struct(outer.full(0), BF)]

    def body(s, ctx_hbm, x_hbm, g_hbm, vec_hbm, bias_hbm, *refs):
        pieces, refs = refs[: len(extra)], refs[len(extra) :]
        out_hbm, hid_hbm, low_hbm, slope_hbm, second_hbm, grad_hbm, sum_hbm, mine_hbm, other_hbm = refs[:9]
        w_out_hbm, w_in_hbm, w_outer_hbm = refs[9:12]
        ctx_ref, x_ref, g_ref, vec_ref, bias_ref, hid_ref, low_ref, act_ref, slope_ref = refs[12:21]
        total, sum_ref, both, w_out, w_in, inner_sems, w_outer, outer_sems, sems = refs[21:]
        at = table.shape[0] - 4
        core = s[at]
        copies = Copies(sems)
        loads = [copies.start(a, b) for a, b in ((ctx_hbm, ctx_ref), (x_hbm, x_ref), (vec_hbm, vec_ref))]
        inner.load((0, 1), s, pieces[:count], (w_out, w_in), inner_sems)
        outer.load((0,), s, pieces[count:], (w_outer,), outer_sems)
        later = [copies.start(bias_hbm, bias_ref), copies.start(g_hbm, g_ref)]
        sum_ref[...] = jnp.zeros_like(sum_ref)
        copies.wait(*loads)
        inner.wait_one(0, (w_out,), inner_sems)
        copies.start(w_out, w_out_hbm)
        hidden = x_ref[...].astype(F32) + dot(ctx_ref[...], w_out[...]) + vec_ref[2:3, :]
        hid_ref[...] = hidden
        hidden_out = copies.start(hid_ref, hid_hbm)
        normed, _ = norm(hidden)
        first = normed * vec_ref[3:4, :] + vec_ref[4:5, :]
        low_ref[...] = first.astype(BF)
        low_out = copies.start(low_ref, low_hbm)
        total[...] = first + vec_ref[5:6, :]
        inner.wait_one(1, (w_out, w_in), inner_sems)
        copies.start(w_in, w_in_hbm)
        outer.wait_one(0, (w_outer,), outer_sems)
        copies.start(w_outer, w_outer_hbm)
        copies.wait(*later)
        for c in range(0, ff, d):
            cols = slice(c, c + d)
            act, slope = gelu_parts(dot(low_ref[...], w_in[:, cols]) + bias_ref[0:1, cols])
            act = act.astype(BF)
            act_ref[:, cols] = act
            slope_ref[:, cols] = slope.astype(BF)
            copies.start(slope_ref.at[:, cols], slope_hbm.at[:, cols])
            total[...] += dot(act, w_outer[cols, :])
        normed, inverse = norm(total[...])
        gain = vec_ref[6:7, :]
        x_ref[...] = (normed * gain + vec_ref[7:8, :]).astype(BF)
        copies.start(x_ref, out_hbm)
        grad = g_ref[...].astype(F32)
        sum_ref[2:3, :] = column_sum(grad * normed)
        sum_ref[3:4, :] = column_sum(grad)
        second = norm_back(grad * gain, normed, inverse)
        low = second.astype(BF)
        ctx_ref[...] = low
        copies.start(ctx_ref, grad_hbm)
        copies.wait(hidden_out)
        hid_ref[...] = second
        copies.start(hid_ref, second_hbm)
        sum_ref[4:5, :] = column_sum(low.astype(F32))
        copies.start(sum_ref, sum_hbm)
        turned = low.T
        for i in range(0, OWNERS, 2):
            grads = dot(turned, act_ref[:, i * part : (i + 2) * part]).astype(BF)
            for k in (0, 1):
                for h in (0, 1):
                    for t in range(4):
                        start = h * half + t * half // 4
                        both[(h, *spot(s, at, t, i + k))] = grads[
                            start : start + half // 4, k * part : (k + 1) * part
                        ]
            z = spot(s, at, 0, i)[3]
            copies.start(both.at[1 - core, :, :, :, z], other_hbm.at[:, :, :, z])
            copies.start(both.at[core, :, :, :, z], mine_hbm.at[:, :, :, z])
        copies.end()

    row = vmem(tok, d)
    return pallas(
        body,
        "forward_block",
        table,
        [context, tokens, out_grad, vectors, bias_inner] + extra,
        outs,
        [row, row, row, vmem(8, d, dtype=F32), vmem(8, ff, dtype=F32), vmem(tok, d, dtype=F32), row]
        + [vmem(tok, ff), vmem(tok, ff), vmem(tok, d, dtype=F32), vmem(SUMS, d, dtype=F32)]
        + [vmem(2, *place)]
        + inner.scratch((0, 1))
        + outer.scratch((0,)),
        2 * tok * d * (d + 3 * ff),
        62,
    )


def active_back(choice, grad_low, slope, w_outer, first_low):
    tok, d = grad_low.shape
    ff = slope.shape[1]
    blocks = [slice(c, c + d) for c in range(0, ff, d)]
    half, rows, part = len(blocks) // 2, d // OWNERS, d // 2

    def body(s, g_hbm, slope_hbm, w_hbm, low_hbm, out_hbm, sum_hbm, mine_hbm, other_hbm, *refs):
        g_ref, slope_ref, w_ref, low_ref, out_ref, sum_ref, turned, held, sems = refs
        copies = Copies(sems)
        first = copies.start(g_hbm, g_ref)
        loads = [
            (copies.start(w_hbm.at[b, :], w_ref.at[b, :]), copies.start(slope_hbm.at[:, b], slope_ref.at[:, b]))
            for b in blocks
        ]
        left = copies.start(low_hbm, low_ref)
        sum_ref[...] = jnp.zeros_like(sum_ref)
        copies.wait(first)
        for n, b in enumerate(blocks):
            copies.wait(*loads[n])
            low = (dot_right(g_ref[...], w_ref[b, :]) * slope_ref[:, b].astype(F32)).astype(BF)
            out_ref[:, b] = low
            copies.start(out_ref.at[:, b], out_hbm.at[:, b])
            sum_ref[8 + n : 9 + n, :] = column_sum(low.astype(F32))
            if n == 0:
                copies.wait(left)
                turned[...] = low_ref[...].T
            grads = dot(turned[...], low).astype(BF)
            for k in (0, 1):
                for j in range(OWNERS):
                    held[(n // half, *spot(s, 0, n % half * 2 + k, j))] = grads[
                        j * rows : (j + 1) * rows, k * part : (k + 1) * part
                    ]
            if n % half == half - 1:
                copies.either(s[0] == n // half, held.at[n // half], mine_hbm, other_hbm)
        copies.start(sum_ref, sum_hbm)
        copies.end()

    grad = struct((*PLACES, rows, part), BF)
    return pallas(
        body,
        "active_back",
        choice,
        [grad_low, slope, w_outer, first_low],
        [struct((tok, ff), BF), struct((SUMS, d), F32), grad, grad],
        [vmem(tok, d), vmem(tok, ff), vmem(ff, d), vmem(tok, d), vmem(tok, ff), vmem(SUMS, d, dtype=F32)]
        + [vmem(d, tok), vmem(2, *grad.shape)],
        4 * tok * d * ff,
    )


def inner_back(choice, grad_inner, grad_second, hidden, vectors, w_out, w_in, context):
    tok, d = hidden.shape
    ff, half = grad_inner.shape[1], d // 2
    blocks = [slice(0, d), slice(d, 2 * d), slice(2 * d, ff)]

    def body(s, g_hbm, second_hbm, hid_hbm, vec_hbm, w_out_hbm, w_in_hbm, *refs):
        left_hbm, out_hbm, ctx_hbm, sum_hbm, mine_hbm, other_hbm = refs[:6]
        g_ref, second_ref, hid_ref, vec_ref, w_out, w_in, left_ref, ctx_ref, sum_ref, held, sems = refs[6:]
        copies = Copies(sems)
        loads = [
            (copies.start(g_hbm.at[:, b], g_ref.at[:, b]), copies.start(w_in_hbm.at[:, b], w_in.at[:, b]))
            for b in blocks[:1]
        ]
        first = copies.start(second_hbm, second_ref)
        loads += [
            (copies.start(g_hbm.at[:, b], g_ref.at[:, b]), copies.start(w_in_hbm.at[:, b], w_in.at[:, b]))
            for b in blocks[1:]
        ]
        later = [copies.start(a, b) for a, b in ((hid_hbm, hid_ref), (vec_hbm, vec_ref), (w_out_hbm, w_out))]
        later.append(copies.start(left_hbm, left_ref))
        sum_ref[...] = jnp.zeros_like(sum_ref)
        for n, b in enumerate(blocks):
            copies.wait(*loads[n])
            part = dot_right(g_ref[:, b], w_in[:, b])
            if n == 0:
                copies.wait(first)
            second_ref[...] += part
        copies.wait(*later)
        grad = second_ref[...]
        normed, inverse = norm(hid_ref[...])
        sum_ref[5:6, :] = column_sum(grad * normed)
        sum_ref[6:7, :] = column_sum(grad)
        hidden_grad = norm_back(grad * vec_ref[3:4, :], normed, inverse)
        second_ref[...] = hidden_grad
        copies.start(second_ref, out_hbm)
        low = hidden_grad.astype(BF)
        ctx_ref[...] = dot_right(low, w_out[...]).astype(BF)
        copies.start(ctx_ref, ctx_hbm)
        grads = dot(left_ref[...].T, low).astype(BF)
        for k in (0, 1):
            held[k] = grads[:, k * half : (k + 1) * half].reshape(OWNERS, d // OWNERS, half)
        copies.start(held.at[1 - s[0]], other_hbm)
        copies.start(held.at[s[0]], mine_hbm)
        sum_ref[7:8, :] = column_sum(low.astype(F32))
        copies.start(sum_ref, sum_hbm)
        copies.end()

    full, grad = vmem(tok, d, dtype=F32), struct((OWNERS, d // OWNERS, half), BF)
    return pallas(
        body,
        "inner_back",
        choice,
        [grad_inner, grad_second, hidden, vectors, w_out, w_in, context],
        [struct((tok, d), F32), struct((tok, d), BF), struct((SUMS, d), F32), grad, grad],
        [vmem(tok, ff), full, full, vmem(8, d, dtype=F32), vmem(d, d), vmem(d, ff), vmem(tok, d), vmem(tok, d)]
        + [vmem(SUMS, d, dtype=F32), vmem(2, *grad.shape)],
        2 * tok * d * (2 * d + ff),
    )


def tokens_back(choice, grad_hidden, mine, other, weights):
    tok, d = grad_hidden.shape
    half = d // 2

    def body(s, hid_hbm, mine_hbm, other_hbm, *refs):
        weights, out_hbm, hid_ref, grad_ref, w_ref, out_ref, sems = refs[:3], *refs[3:]
        copies = Copies(sems)
        loads = []
        for n, weight in enumerate(weights):
            loads.append([copies.start(weight, w_ref.at[n])])
            for grad, side in ((other_hbm, 1 - s[0]), (mine_hbm, s[0])):
                cols = pl.ds(pl.multiple_of(side * half, half), half)
                loads[-1].append(
                    copies.start(grad.at[:, n * half : (n + 1) * half], grad_ref.at[n, :, cols])
                )
            if n == 0:
                first = copies.start(hid_hbm, hid_ref)
        for n, load in enumerate(loads):
            copies.wait(*load)
            part = dot_right(grad_ref[n], w_ref[n])
            copies.wait(first)
            if n < 2:
                hid_ref[...] += part
            else:
                out_ref[...] = (hid_ref[...] + part).astype(BF)
        copies.start(out_ref, out_hbm)
        copies.end()

    return pallas(
        body,
        "tokens_back",
        choice,
        [grad_hidden, mine, other, *weights],
        [struct((tok, d), BF)],
        [vmem(tok, d, dtype=F32), vmem(3, tok, d), vmem(3, d, d), vmem(tok, d)],
        6 * tok * d * d,
    )[0]


def axis_step(value, axis):
    if axis == "x":
        return rep_step(value, 2)
    return lax.ppermute(value, "fsdp", [(f, f ^ 1) for f in range(8)])


def after(value, *events):
    return lax.optimization_barrier((value,) + events)[0] if events else value


def added(*terms):
    total = terms[0].astype(F32)
    for term in terms[1:]:
        total = total + term.astype(F32)
    return total.astype(BF)


def chosen(parts, bit, axis):
    return lax.dynamic_index_in_dim(parts, bit, axis, keepdims=False)


class Owned:
    def __init__(self, place, mine, received):
        self.place, self.mine, self.received = place, mine, received

    def first(self, *events):
        received = after(self.received, *events)
        sent = [added(self.mine[n, 1], received[n, 1]) for n in (0, 1)]
        moved = [axis_step(v, axis) for v, axis in zip(sent, "xy")]
        self.terms = [[self.mine[n, 0], received[n, 0], moved[n]] for n in (0, 1)]
        return sent

    def second(self, *events):
        terms = [t[:-1] + [after(t[-1], *events)] for t in self.terms]
        sent = [added(*(v[1] for v in t)) for t in terms]
        moved = [axis_step(v, axis) for v, axis in zip(sent, "yx")]
        self.terms = [[v[0] for v in t] + [m] for t, m in zip(terms, moved)]
        return sent

    def third(self, *events):
        sums = [added(*t[:-1], after(t[-1], *events)) for t in self.terms]
        parts = jnp.concatenate(sums, 1)
        moved = [
            lax.ppermute(parts[k], "fsdp", [(f, (f // 2 + k) % 4 * 2 + f % 2) for f in range(8)])
            for k in (1, 3, 2)
        ]
        self.terms = [parts[0]] + moved
        return [parts[k] for k in (1, 3, 2)]

    def fourth(self, *events):
        self.own = added(*self.terms[:-1], after(self.terms[-1], *events))
        self.other = rep_step(self.own, 2)
        return [self.own]

    def fifth(self, *events):
        other = after(self.other, *events)
        low = jnp.where(self.place.x == 0, self.own, other)
        high = jnp.where(self.place.x == 0, other, self.own)
        mid = low.shape[0] // 2
        half = jnp.concatenate([low[:mid], high[:mid], low[mid:], high[mid:]], 0)
        self.both = (half, rep_step(half, 1))
        return [half]

    def last(self):
        mine, mate = self.both
        first = self.place.core == 0
        return jnp.where(first, mine, mate), jnp.where(first, mate, mine)


class Place:
    def __init__(self, mesh):
        f, r = lax.axis_index("fsdp"), lax.axis_index("rep")
        self.f, self.core, self.x = f, r % 2, r // 2
        self.y, self.z = f % 2, f // 2
        self.choice = jnp.stack([self.core, self.x, self.y, self.z]).astype(jnp.int32)
        if mesh.shape["fsdp"] == len(RING):
            row = lax.dynamic_index_in_dim(jnp.array(ring_table(), jnp.int32), f, 0, keepdims=False)
            self.table = jnp.concatenate([row, self.core[None].astype(jnp.int32)])
        else:
            self.table = jnp.zeros((1,), jnp.int32)


class Ring:
    def __init__(self, group, payload, last):
        self.group, self.ways, self.last, self.count = group, {1: [payload], -1: [payload]}, last, 0

    def ways_of(self, count):
        return (1, -1) if count < len(RING) // 2 else (self.last,)

    def source(self, way, count):
        return count if way == 1 or count == len(RING) // 2 else len(RING) // 2 + count

    @property
    def came(self):
        return tuple(self.ways[way][self.count] for way in self.ways_of(self.count))

    def step(self, *events):
        self.count += 1
        for way in self.ways_of(self.count):
            self.ways[way].append(ring_step(after(self.ways[way][-1], *events), way))
            self.group.pieces.append((self.ways[way][-1], (self.source(way, self.count),), False))

    def share(self, count, *events):
        shared = []
        for way in self.ways_of(count):
            shared.append(rep_step(after(self.ways[way][count], *events), 1))
            self.group.pieces.append((shared[-1], (self.source(way, count),), True))
        return shared


class Travel:
    def __init__(self, rings):
        self.rings, self.going, self.shared, self.seen = rings, (), (), ()

    def round(self, *order, events=()):
        came = tuple(v for n in self.going for v in self.rings[n].came)
        counts = [(n, self.rings[n].count) for n in self.going]
        self.seen = came + self.shared
        for n in order:
            self.rings[n].step(*events, *self.seen)
        self.shared = tuple(v for n, count in counts for v in self.rings[n].share(count, *events, *came))
        self.going = order

    def finish(self, *events):
        for n in self.going:
            self.rings[n].share(self.rings[n].count, *events)


def local(mesh, *args):
    (
        tokens, seq_ids, key_mask, weight_query, bias_query, weight_key, weight_value, bias_value,
        weight_out, bias_out, norm1_gain, norm1_bias, weight_inner, bias_inner, weight_outer, bias_outer,
        norm2_gain, norm2_bias, out_grad,
    ) = args
    place = Place(mesh)
    choice, table = place.choice, place.table
    fsdp = mesh.shape["fsdp"]
    d = tokens.shape[1]
    win = windows(seq_ids[0])
    narrow = [bias_query, bias_value, bias_out, norm1_gain, norm1_bias, bias_outer, norm2_gain, norm2_bias]
    shards = [[weight_query, weight_key, weight_value], [weight_out, weight_inner], [weight_outer]]
    fast = all(fast_path(mesh, s) for s in shards)
    if fast:
        groups = [Group(mesh, s) for s in shards]
        packed = pack(table, groups, narrow + [bias_inner])
        rings = [Ring(g, p, way) for g, p, way in zip(groups, packed, (1, -1, 1))]
        small = packed[0]
        travel = Travel(rings)
        travel.round(0, 1)
        travel.round(0, 2)
        travel.round(0, 1)
        travel.round(0, 2)
        travel.round(1, 2)
    else:
        groups = [Group(mesh, [lax.all_gather(w, "fsdp", axis=0, tiled=True) for w in s]) for s in shards]
        rows = [jnp.concatenate(narrow), bias_inner]
        rows = [jnp.concatenate([r, jnp.zeros((d - r.size,), BF)])[None] for r in rows]
        small = jnp.concatenate(rows + [jnp.zeros((SMALL - 2, d), BF)], 0)
        small = lax.all_gather(small, "fsdp", axis=0, tiled=False)
    qkv, inner_group, outer_group = groups

    q, k, v, vectors, full_bias_inner, *weights = project(table, qkv, tokens, small)
    if fast:
        travel.round(1, 2, events=(q,))
        q = after(q, *travel.seen)
    context, probs = attend(win, seq_ids, key_mask, q, k, v)
    if fast:
        travel.finish(context)
    (
        layer_out, hidden, first_low, slope, grad_second, grad_outer, sums2, outer_mine, outer_other,
        w_out, w_in, w_outer,
    ) = forward_block(
        place_table(table, choice), inner_group, outer_group, context, tokens, out_grad, vectors, full_bias_inner
    )
    if not fast:
        choice = jnp.zeros((4,), jnp.int32)
    if fast:
        outer_sum = Owned(place, outer_mine, rep_step(outer_other, 1))
    grad_inner, sums_inner, inner_mine, inner_other = active_back(choice, grad_outer, slope, w_outer, first_low)
    if fast:
        inner_sum = Owned(place, inner_mine, rep_step(inner_other, 1))
        event = outer_sum.first(inner_mine)
        grad_inner = after(grad_inner, *event)
    grad_hidden, grad_context, sums1, out_mine, out_other = inner_back(
        choice, grad_inner, grad_second, hidden, vectors, w_out, w_in, context
    )
    if fast:
        event = outer_sum.second(out_mine)
        event += inner_sum.first(out_mine)
        grad_context = after(grad_context, *event)
    place_win = jnp.concatenate([choice, win])
    grads_other, sums_other, query_other = attend_back(
        place_win, 1, q, k, v, context, grad_context, probs, tokens, out_other
    )
    if fast:
        event = inner_sum.second(grads_other)
        event += outer_sum.third(grads_other)
        query_came = rep_step(after(query_other, *event), 1)
        grad_context = after(grad_context, *event)
    grads_mine, sums_mine, query_mine = attend_back(
        place_win, 0, q, k, v, context, grad_context, probs, tokens, out_mine
    )
    sums_att = by_core(choice[0], sums_mine, sums_other, 1)
    sums = sums1 + sums2 + sums_inner + sums_att
    if fast:
        query_sum = Owned(place, query_mine, query_came)
        event = query_sum.first(query_mine)
        event += inner_sum.third(*event)
        sums = sums + after(rep_step(sums, 1), *event)
        event += outer_sum.fourth(*event)
        event = query_sum.second(*event)
        sums = sums + after(rep_step(sums, 2), *event)
        event += outer_sum.fifth(*event)
        event += inner_sum.fourth(*event)
        event = query_sum.third(*event)
        sums = sums + after(axis_step(sums, "y"), *event)
        grad_hidden = after(grad_hidden, *event)
    grad_tokens = tokens_back(choice, grad_hidden, grads_mine, grads_other, weights)
    if fast:
        sums = sums + after(z_step(sums, 1), grad_tokens)
        sums = sums + after(z_step(sums, 2), grad_tokens)
        event = query_sum.fourth(grad_tokens)
        event += inner_sum.fifth(*event)
        low, high = outer_sum.last()
        final_outer = jnp.concatenate([low, high], 0).T.astype(F32)
        query_sum.fifth(final_outer, *event)
        low, high = inner_sum.last()
        rows = d // fsdp
        blocks = [v[c : c + rows] for v in (low, high) for c in range(0, v.shape[0], rows)]
        final_inner = jnp.concatenate(blocks, 1).astype(F32)
        low, high = query_sum.last()
        final_query, final_key, final_value, final_out = (
            jnp.concatenate([low[c : c + rows], high[c : c + rows]], 1).astype(F32)
            for c in range(0, 4 * rows, rows)
        )
    else:

        def plain(*blocks):
            total = jnp.concatenate(blocks, 2)
            total = total.reshape(-1, total.shape[2])
            owned = lax.psum_scatter(total, "fsdp", scatter_dimension=0, tiled=True)
            return lax.psum(owned, "rep").astype(F32)

        sums = lax.psum(sums, ("fsdp", "rep"))
        def straight(v):
            by_x, by_y = v[0].transpose(2, 1, 0, 3, 4), v[1].transpose(2, 0, 1, 3, 4)
            return jnp.concatenate([w.reshape(OWNERS, -1, w.shape[4]) for w in (by_x, by_y)], 1)

        outer_mine, outer_other, inner_mine, inner_other, query_mine, query_other = (
            straight(v) for v in (outer_mine, outer_other, inner_mine, inner_other, query_mine, query_other)
        )
        final_outer = plain(jnp.concatenate([outer_mine, outer_other], 1).transpose(0, 2, 1))
        part = d // OWNERS
        unstack = lambda v: [v[:, c : c + part] for c in range(0, v.shape[1], part)]
        final_inner = plain(*unstack(inner_mine), *unstack(inner_other))
        final_query, final_key, final_value, final_out = (
            plain(a, b) for a, b in zip(unstack(query_mine), unstack(query_other))
        )

    narrow_sums = lax.dynamic_slice_in_dim(sums, place.f * (d // fsdp), d // fsdp, 1)
    inner_sums = lax.dynamic_slice_in_dim(sums[8:12].reshape(-1), place.f * bias_inner.size, bias_inner.size, 0)
    return (
        layer_out,
        grad_tokens,
        final_query,
        narrow_sums[0],
        final_key,
        final_value,
        narrow_sums[1],
        final_out,
        narrow_sums[7],
        narrow_sums[5],
        narrow_sums[6],
        final_inner,
        inner_sums,
        final_outer,
        narrow_sums[4],
        narrow_sums[2],
        narrow_sums[3],
    )


def by_core(core, mine, other, axis):
    return jnp.where(core == 0, jnp.concatenate([mine, other], axis), jnp.concatenate([other, mine], axis))


def z_step(value, bits):
    return lax.ppermute(value, "fsdp", [(f, f ^ (2 * bits)) for f in range(8)])


def place_table(table, choice):
    return jnp.concatenate([table[:-1], choice]) if table.shape[0] > 1 else jnp.zeros((4,), jnp.int32)


def solution(mesh):
    rows, shard, part = P(("fsdp", "rep"), None), P("fsdp", None), P("fsdp")
    return jax.shard_map(
        functools.partial(local, mesh),
        mesh=mesh,
        in_specs=(
            rows, rows, rows, shard, part, shard, shard, part, shard, part, part, part, shard, part, shard,
            part, part, part, rows,
        ),
        out_specs=(
            rows, rows, shard, part, shard, shard, part, shard, part, part, part, shard, part, shard, part,
            part, part,
        ),
        check_vma=False,
    )
```

```python
import functools
import math

import jax
import jax.numpy as jnp
from jax import lax
from jax.experimental import pallas as pl
from jax.experimental.pallas import tpu as pltpu
from jax.sharding import PartitionSpec as P

HEADS = 12
DH = 64
BF = jnp.bfloat16
F32 = jnp.float32
NEGATIVE = -1e30
EPSILON = 1e-12
QB = 128
KB = 128
SPAN = 5
ROWS = 1024
VMEM = 60 * 1024 * 1024
COST = 0.05
ANY = pl.BlockSpec(memory_space=pl.ANY)


def dot(left, right):
    return jnp.dot(left, right, preferred_element_type=F32)


def dot_right(left, right):
    return lax.dot_general(left, right, (((1,), (1,)), ((), ())), preferred_element_type=F32)


def params(steps=1):
    return pltpu.CompilerParams(
        dimension_semantics=("arbitrary",) * steps, vmem_limit_bytes=VMEM
    )


def cost(flops, size):
    return pl.CostEstimate(flops=int(flops * COST), bytes_accessed=int(size * COST), transcendentals=0)


def struct(shape, dtype):
    return jax.ShapeDtypeStruct(shape, dtype)


def whole(shape):
    return pl.BlockSpec(shape, lambda i, s: (0,) * len(shape))


def rows_of(width, height=ROWS):
    return pl.BlockSpec((height, width), lambda i, s: (i, 0))


def norm(hidden):
    center = hidden - jnp.mean(hidden, axis=-1, keepdims=True)
    inverse = lax.rsqrt(jnp.mean(center * center, axis=-1, keepdims=True) + EPSILON)
    return center * inverse, inverse


def norm_back(grad, normed, inverse):
    mean = jnp.mean(grad, axis=-1, keepdims=True)
    along = jnp.mean(grad * normed, axis=-1, keepdims=True)
    return inverse * (grad - mean - normed * along)


def gelu_parts(inner):
    phi = 0.5 + 0.5 * lax.erf(inner * 0.7071067811865476)
    density = jnp.exp((-0.5 * inner) * inner) * 0.3989422804014327
    return inner * phi, phi + inner * density


def column_sum(value):
    return jnp.sum(value, axis=0, keepdims=True)


def windows(seq_row):
    tiles = seq_row.reshape(seq_row.shape[0] // QB, QB)
    below = jnp.sum((seq_row[None] < tiles[:, :1]).astype(jnp.int32), axis=1)
    upto = jnp.sum((seq_row[None] <= tiles[:, -1:]).astype(jnp.int32), axis=1)
    low = below // KB
    return jnp.concatenate([low, (upto + KB - 1) // KB - low])


def first_half(shape):
    return lax.broadcasted_iota(jnp.int32, shape, len(shape) - 1) < DH


def stack_pair(pair):
    low = first_half(pair.shape)
    zero = jnp.zeros_like(pair)
    return jnp.concatenate([jnp.where(low, pair, zero), jnp.where(low, zero, pair)], axis=0)


def fold_pair(both):
    half = both.shape[0] // 2
    return jnp.where(first_half((half, both.shape[1])), both[:half], both[half:])


def attend(win, seq, mask, q, k, v):
    tok, d = q.shape
    tiles, pairs = tok // QB, d // (2 * DH)

    def kernel(win, seq_hbm, mask_hbm, q_hbm, k_hbm, v_hbm, ctx_hbm, p_hbm, *refs):
        seq_ref, mask_ref, q_ref, k_ref, v_ref, ctx_ref, p_ref, bias_ref, s_ref, p_sems, ctx_sems, sems = refs
        copies = Copies(sems)
        for source, target in (
            (seq_hbm, seq_ref), (mask_hbm, mask_ref), (k_hbm, k_ref), (q_hbm, q_ref), (v_hbm, v_ref)
        ):
            copies.start(source, target)
        copies.end()

        def store(i):
            rows = pl.ds(pl.multiple_of(i * QB, QB), QB)
            return (
                pltpu.make_async_copy(p_ref.at[i], p_hbm.at[i], p_sems.at[i]),
                pltpu.make_async_copy(ctx_ref.at[rows, :], ctx_hbm.at[rows, :], ctx_sems.at[i]),
            )

        def tile(i, n):
            w = n * KB
            base = pl.multiple_of(win[i] * KB, KB)
            start = pl.multiple_of(i * QB, QB)
            rows_now = pl.ds(start, QB)
            for pair in range(pairs):
                lanes = slice(pair * 2 * DH, (pair + 1) * 2 * DH)
                s_ref[pair, :, :w] = dot_right(stack_pair(q_ref[rows_now, lanes]), k_ref[pl.ds(base, w), lanes])
            own = jnp.broadcast_to(seq_ref[:, pl.ds(start, QB)], (QB, QB)).T
            rows = start + lax.broadcasted_iota(jnp.int32, (QB, KB), 0)
            for b in range(n):
                off = pl.multiple_of(base + b * KB, KB)
                cols = off + lax.broadcasted_iota(jnp.int32, (QB, KB), 1)
                visible = (mask_ref[:, pl.ds(off, KB)] == 1) | (rows == cols)
                allowed = (own == seq_ref[:, pl.ds(off, KB)]) & visible
                bias_ref[:, b * KB : (b + 1) * KB] = jnp.where(allowed, 0.0, NEGATIVE).astype(F32)
            ones = jnp.ones((w, 2 * DH), BF)
            expons = []
            for pair in range(pairs):
                bias = bias_ref[:, :w]
                scores = s_ref[pair, :, :w] + jnp.concatenate([bias, bias], axis=0)
                expons.append(jnp.exp(scores - jnp.max(scores, axis=1, keepdims=True)).astype(BF))
            for pair, expon in enumerate(expons):
                lanes = slice(pair * 2 * DH, (pair + 1) * 2 * DH)
                mixed = dot(expon, jnp.concatenate([v_ref[pl.ds(base, w), lanes], ones], axis=1))
                scale = 1.0 / mixed[:, 2 * DH :]
                ctx_ref[rows_now, lanes] = fold_pair(mixed[:, : 2 * DH] * scale).astype(BF)
                for b in range(n):
                    p_ref[i, pair, :, b * KB : (b + 1) * KB] = (
                        expon[:, b * KB : (b + 1) * KB].astype(F32) * scale
                    ).astype(BF)

        def step(i, carry):
            for n in range(1, SPAN + 1):
                pl.when(win[tiles + i] == n)(functools.partial(tile, i, n))
            for copy in store(i):
                copy.start()
            return carry

        lax.fori_loop(0, tiles, step, 0)
        for i in range(tiles):
            for copy in store(i):
                copy.wait()

    wide = (tiles, pairs, 2 * QB, SPAN * KB)
    return pallas(
        kernel,
        "attend",
        win,
        [seq, mask, q, k, v],
        [struct((tok, d), BF), struct(wide, BF)],
        [pltpu.VMEM(seq.shape, jnp.int32), pltpu.VMEM(mask.shape, jnp.int32)]
        + [vmem(tok, d), vmem(tok, d), vmem(tok, d), vmem(tok, d), vmem(*wide)]
        + [vmem(QB, SPAN * KB, dtype=F32), vmem(pairs, 2 * QB, SPAN * KB, dtype=F32)]
        + [pltpu.SemaphoreType.DMA((tiles,)), pltpu.SemaphoreType.DMA((tiles,))],
        1.4e10,
    )


def attend_back(place_win, side, q, k, v, ctx, do, p, tokens, out_grad):
    tok, d = q.shape
    half, rows = d // 2, d // OWNERS
    tiles, pairs = tok // QB, half // (2 * DH)

    def kernel(s, q_hbm, k_hbm, v_hbm, ctx_hbm, do_hbm, p_hbm, x_hbm, out_hbm, grad_hbm, sum_hbm, w_hbm, *refs):
        q_ref, k_ref, v_ref, ctx_ref, do_ref, p_ref, x_ref, out_ref, grad_ref, sum_ref, w_ref = refs[:11]
        dkt, dvt, s_ref, p_sems, sems = refs[11:]
        pick = s[0] if side == 0 else 1 - s[0]
        cols = pl.ds(pl.multiple_of(pick * half, half), half)
        chosen_pairs = pl.ds(pick * pairs, pairs)
        copies = Copies(sems)

        def load(i):
            return pltpu.make_async_copy(p_hbm.at[i, chosen_pairs], p_ref.at[i], p_sems.at[i])

        load(0).start()
        first = [
            copies.start(a.at[:, cols], b)
            for a, b in ((do_hbm, do_ref), (v_hbm, v_ref), (ctx_hbm, ctx_ref), (k_hbm, k_ref), (q_hbm, q_ref))
        ]
        for i in range(1, tiles):
            load(i).start()
        later = [copies.start(x_hbm, x_ref), copies.start(out_hbm, out_ref)]
        dkt[...] = jnp.zeros_like(dkt)
        dvt[...] = jnp.zeros_like(dvt)
        sum_ref[...] = jnp.zeros_like(sum_ref)
        copies.wait(*first)
        lanes = [slice(p * 2 * DH, (p + 1) * 2 * DH) for p in range(pairs)]

        def tile(i, n):
            w = n * KB
            base = pl.multiple_of(s[4 + i] * KB, KB)
            rows_now = pl.ds(pl.multiple_of(i * QB, QB), QB)
            for pair, ln in enumerate(lanes):
                s_ref[pair, :, :w] = dot_right(stack_pair(do_ref[rows_now, ln]), v_ref[pl.ds(base, w), ln])
            for pair, ln in enumerate(lanes):
                dvt[ln, pl.ds(base, w)] += dot(stack_pair(do_ref[rows_now, ln]).T, p_ref[i, pair, :, :w])
            scores = []
            for pair, ln in enumerate(lanes):
                along = do_ref[rows_now, ln].astype(F32) * ctx_ref[rows_now, ln].astype(F32)
                delta = jnp.sum(stack_pair(along), axis=1, keepdims=True)
                scores.append((p_ref[i, pair, :, :w].astype(F32) * (s_ref[pair, :, :w] - delta)).astype(BF))
            for pair, ln in enumerate(lanes):
                dq = fold_pair(dot(scores[pair], k_ref[pl.ds(base, w), ln])) * (1.0 / math.sqrt(DH))
                dq = dq.astype(BF)
                grad_ref[rows_now, ln] = dq
                sum_ref[0:1, ln] += column_sum(dq.astype(F32))
            for pair, ln in enumerate(lanes):
                dkt[ln, pl.ds(base, w)] += dot(stack_pair(q_ref[rows_now, ln]).T, scores[pair])

        def step(i, carry):
            load(i).wait()
            for n in range(1, SPAN + 1):
                pl.when(s[4 + tiles + i] == n)(functools.partial(tile, i, n))
            return carry

        lax.fori_loop(0, tiles, step, 0)
        for o in range(0, tok, QB):
            grad_ref[o : o + QB, half : 2 * half] = dkt[:, o : o + QB].T.astype(BF)
            dv = dvt[:, o : o + QB].T.astype(BF)
            grad_ref[o : o + QB, 2 * half :] = dv
            sum_ref[1:2, :] += column_sum(dv.astype(F32))
        copies.start(grad_ref, grad_hbm)
        copies.start(sum_ref, sum_hbm)
        copies.wait(*later)
        turned = x_ref[...].T
        for j in range(OWNERS):
            w_ref[spot(s, 0, 3, j)] = out_ref[j]
        for n in range(3):
            grads = dot(turned, grad_ref[:, n * half : (n + 1) * half]).astype(BF)
            for j in range(OWNERS):
                w_ref[spot(s, 0, n, j)] = grads[j * rows : (j + 1) * rows]
            if n == 1:
                copies.start(w_ref.at[0], w_hbm.at[0])
        copies.start(w_ref.at[1], w_hbm.at[1])
        copies.end()

    full = vmem(tok, half)
    return pallas(
        kernel,
        "attend_back",
        place_win,
        [q, k, v, ctx, do, p, tokens, out_grad],
        [struct((tok, 3 * half), BF), struct((SUMS, half), F32), struct((*PLACES, rows, half), BF)],
        [full, full, full, full, full, vmem(tiles, pairs, 2 * QB, SPAN * KB), vmem(tok, d)]
        + [vmem(*out_grad.shape), vmem(tok, 3 * half), vmem(SUMS, half, dtype=F32), vmem(*PLACES, rows, half)]
        + [vmem(half, tok, dtype=F32), vmem(half, tok, dtype=F32)]
        + [vmem(pairs, 2 * QB, SPAN * KB, dtype=F32), pltpu.SemaphoreType.DMA((tiles,))],
        2e10,
    )


class Weight:
    def __init__(self, shard, first):
        self.rows, self.width = shard.shape
        self.shard = shard
        self.first = first


class Group:
    def __init__(self, mesh, shards):
        self.fsdp = mesh.shape["fsdp"]
        self.fast = fast_path(mesh, shards)
        self.pieces = []
        self.weights = []
        first = 0
        for shard in shards:
            self.weights.append(Weight(shard, first))
            first += shard.size // (2 * PIECE)
        self.height = first

    def full(self, k):
        weight = self.weights[k]
        return (weight.rows * (self.fsdp if self.fast else 1), weight.width)

    def operands(self, used):
        if not self.fast:
            return [self.weights[k].shard for k in used]
        return [self.weights[k].shard for k in used] + [array for array, _, _ in self.pieces]

    def load(self, used, table, refs, targets, sems):
        if not self.fast:
            for n, target in enumerate(targets):
                pltpu.make_async_copy(refs[n], target, sems.at[n]).start()
            return
        core = table[self.fsdp]
        for n, k in enumerate(used):
            weight, target, sem = self.weights[k], targets[n], sems.at[n]
            half = weight.rows // 2
            base = pl.multiple_of(table[0] * weight.rows, weight.rows)
            pltpu.make_async_copy(refs[n], target.at[pl.ds(base, weight.rows), :], sem).start()
            for piece, (_, sources, mate) in zip(refs[len(used) :], self.pieces):
                side = (1 - core) if mate else core
                height = piece.shape[0] // len(sources)
                for order, source in enumerate(sources):
                    row = pl.multiple_of(table[source] * weight.rows + side * half, 16)
                    for c in range(weight.width // PIECE):
                        start = order * height + weight.first + c * half
                        pltpu.make_async_copy(
                            piece.at[start : start + half, :],
                            target.at[pl.ds(row, half), c * PIECE : (c + 1) * PIECE],
                            sem,
                        ).start()

    def wait(self, targets, sems):
        for n, target in enumerate(targets):
            pltpu.make_async_copy(target, target, sems.at[n]).wait()

    def wait_one(self, n, targets, sems):
        pltpu.make_async_copy(targets[n], targets[n], sems.at[n]).wait()

    def scratch(self, used):
        return [pltpu.VMEM(self.full(k), BF) for k in used] + [pltpu.SemaphoreType.DMA((len(used),))]


PIECE = 768
OWNERS = 8
SUMS = 16


def fast_path(mesh, shards):
    return (
        mesh.shape["fsdp"] == 8
        and mesh.shape["rep"] == 4
        and all(s.shape[0] % 32 == 0 and s.shape[1] % PIECE == 0 for s in shards)
    )


RING = (0, 2, 4, 6, 7, 5, 3, 1)


def ring_table():
    size = len(RING)
    place = {v: p for p, v in enumerate(RING)}
    steps = list(range(0, -(size // 2) - 1, -1)) + list(range(1, size - size // 2))
    return [[RING[(place[f] + s) % size] for s in steps] for f in range(size)]


def ring_step(value, step):
    size = len(RING)
    return lax.ppermute(value, "fsdp", [(RING[p], RING[(p + step) % size]) for p in range(size)])


def rep_step(value, bits):
    return lax.ppermute(value, "rep", [(r, r ^ bits) for r in range(4)])


def pallas(body, name, table, operands, outs, scratch, flops, limit=60):
    operands, outs = list(operands), list(outs)
    size = sum(o.size * o.dtype.itemsize for o in operands + outs)
    return pl.pallas_call(
        body,
        in_specs=[pl.BlockSpec(memory_space=pltpu.SMEM)] + [ANY] * len(operands),
        out_specs=[ANY] * len(outs),
        out_shape=outs,
        scratch_shapes=list(scratch) + [pltpu.SemaphoreType.DMA((COPIES,))],
        compiler_params=pltpu.CompilerParams(vmem_limit_bytes=limit << 20),
        cost_estimate=cost(flops, size),
        name=name,
    )(table, *operands)


COPIES = 48


class Copies:
    def __init__(self, sems):
        self.sems, self.started = sems, []

    def start(self, source, target):
        copy = pltpu.make_async_copy(source, target, self.sems.at[len(self.started)])
        copy.start()
        self.started.append([copy, False])
        return len(self.started) - 1

    def either(self, first, source, one, two):
        sem = self.sems.at[len(self.started)]
        copies = [pltpu.make_async_copy(source, target, sem) for target in (one, two)]
        pl.when(first)(copies[0].start)
        pl.when(jnp.logical_not(first))(copies[1].start)
        self.started.append([copies[0], False])

    def wait(self, *numbers):
        for n in numbers:
            if not self.started[n][1]:
                self.started[n][0].wait()
                self.started[n][1] = True

    def end(self):
        self.wait(*range(len(self.started)))


PLACES = (2, 2, 2, 4)


def spot(s, at, block, owner):
    flip = lambda bit, mine: mine if bit == 0 else 1 - mine
    x, y = flip(block % 2, s[at + 1]), flip(owner % 2, s[at + 2])
    z = lax.bitwise_and(owner // 2 - s[at + 3] + 4, 3)
    return (0, x, y, z) if block < 2 else (1, y, x, z)


def vmem(*shape, dtype=BF):
    return pltpu.VMEM(shape, dtype)


def pack(table, groups, vectors):
    shards = [w.shard for g in groups for w in g.weights]
    core = 0
    outs = [struct((g.height + (SMALL if g is groups[0] else 0), PIECE), BF) for g in groups]

    def body(s, *refs):
        vec_refs = refs[: len(vectors)]
        shard_refs = list(refs[len(vectors) : len(vectors) + len(shards)])
        outs, refs = refs[len(vectors) + len(shards) :][: len(groups)], refs[len(vectors) + len(shards) + len(groups) :]
        staged, held, sems = refs[: len(groups)], refs[len(groups) : -1], refs[-1]
        copies = Copies(sems)
        loads = [copies.start(r, h) for r, h in zip(vec_refs, held)]
        ready = []
        for g, group in enumerate(groups):
            ready.append([])
            for weight in group.weights:
                ref, half = shard_refs.pop(0), weight.rows // 2
                rows = pl.ds(pl.multiple_of(s[core] * half, half), half)
                for c in range(weight.width // PIECE):
                    ready[g].append(
                        copies.start(
                            ref.at[rows, c * PIECE : (c + 1) * PIECE],
                            staged[g].at[weight.first + c * half : weight.first + (c + 1) * half, :],
                        )
                    )
        copies.wait(*loads)
        used = [r[...].astype(F32).reshape(1, -1) for r in held]
        row = jnp.concatenate(used[:-1], axis=1)
        last = jnp.concatenate([used[-1], jnp.zeros((1, PIECE - used[-1].shape[1]), F32)], axis=1)
        rest = jnp.zeros((SMALL - 2, PIECE), F32)
        staged[0][groups[0].height :, :] = jnp.concatenate([row, last, rest], axis=0).astype(BF)
        for g in range(len(groups)):
            copies.wait(*ready[g])
            copies.start(staged[g], outs[g])
        copies.end()

    return pallas(
        body,
        "pack",
        table,
        vectors + shards,
        outs,
        [vmem(*o.shape) for o in outs] + [vmem(*v.shape) for v in vectors],
        1,
    )


def project(table, group, tokens, small):
    tok, d = tokens.shape
    used = (0, 1, 2)
    extra = group.operands(used)
    fsdp, part = group.fsdp, d // group.fsdp
    wide = 4 * d // fsdp

    def body(s, x_hbm, small_hbm, *refs):
        pieces, outs, refs = refs[: len(extra)], refs[len(extra) : len(extra) + 8], refs[len(extra) + 8 :]
        x_ref, res_ref, vec_ref, bias_ref, all_small, small_sem, *weights, weight_sems, sems = refs
        copies = Copies(sems)
        tokens_in = copies.start(x_hbm, x_ref)
        group.load(used, s, pieces, weights, weight_sems)
        if group.fast:
            own = small_hbm.at[small_hbm.shape[0] - SMALL :, :]
            pltpu.make_async_copy(own, all_small.at[s[0]], small_sem).start()
            for piece, (_, sources, mate) in zip(pieces[len(used) :], group.pieces):
                if not mate:
                    pltpu.make_async_copy(
                        piece.at[group.height : group.height + SMALL, :], all_small.at[s[sources[0]]], small_sem
                    ).start()
        else:
            pltpu.make_async_copy(small_hbm, all_small, small_sem).start()
        pltpu.make_async_copy(all_small, all_small, small_sem).wait()
        rows = [all_small[f].astype(F32) for f in range(fsdp)]
        for v in range(8):
            vec_ref[v : v + 1, :] = jnp.concatenate([r[0:1, v * part : (v + 1) * part] for r in rows], axis=1)
        bias_ref[...] = jnp.zeros_like(bias_ref)
        bias_ref[0:1, :] = jnp.concatenate([r[1:2, :wide] for r in rows], axis=1)
        copies.start(vec_ref, outs[3])
        copies.start(bias_ref, outs[4])
        copies.wait(tokens_in)
        for n, weight in enumerate(weights):
            group.wait_one(n, weights, weight_sems)
            copies.start(weight, outs[5 + n])
            result = dot(x_ref[...], weight[...])
            if n == 0:
                result = (result + vec_ref[0:1, :]).astype(BF) * jnp.asarray(1.0 / math.sqrt(DH), BF)
            if n == 2:
                result = result + vec_ref[1:2, :]
            res_ref[n] = result.astype(BF)
            copies.start(res_ref.at[n], outs[n])
        copies.end()

    return pallas(
        body,
        "project",
        table,
        [tokens, small] + extra,
        [struct((tok, d), BF)] * 3
        + [struct((8, d), F32), struct((8, 4 * d), F32)]
        + [struct(group.full(k), BF) for k in used],
        [vmem(tok, d), vmem(3, tok, d), vmem(8, d, dtype=F32), vmem(8, 4 * d, dtype=F32)]
        + [vmem(fsdp, SMALL, d), pltpu.SemaphoreType.DMA]
        + group.scratch(used),
        6 * tok * d * d,
    )


SMALL = 16


def forward_block(table, inner, outer, context, tokens, out_grad, vectors, bias_inner):
    tok, d = tokens.shape
    ff = inner.full(1)[1]
    extra_inner, extra_outer = inner.operands((0, 1)), outer.operands((0,))
    count = len(extra_inner)
    extra = extra_inner + extra_outer
    rows, wide = struct((tok, d), BF), struct((tok, ff), BF)
    half, part = d // 2, ff // OWNERS
    place = (*PLACES, half // 4, part)
    outs = [rows, struct((tok, d), F32), rows, wide, struct((tok, d), F32), rows, struct((SUMS, d), F32)]
    outs += [struct(place, BF)] * 2
    outs += [struct(inner.full(0), BF), struct(inner.full(1), BF), struct(outer.full(0), BF)]

    def body(s, ctx_hbm, x_hbm, g_hbm, vec_hbm, bias_hbm, *refs):
        pieces, refs = refs[: len(extra)], refs[len(extra) :]
        out_hbm, hid_hbm, low_hbm, slope_hbm, second_hbm, grad_hbm, sum_hbm, mine_hbm, other_hbm = refs[:9]
        w_out_hbm, w_in_hbm, w_outer_hbm = refs[9:12]
        ctx_ref, x_ref, g_ref, vec_ref, bias_ref, hid_ref, low_ref, act_ref, slope_ref = refs[12:21]
        total, sum_ref, both, w_out, w_in, inner_sems, w_outer, outer_sems, sems = refs[21:]
        at = table.shape[0] - 4
        core = s[at]
        copies = Copies(sems)
        loads = [copies.start(a, b) for a, b in ((ctx_hbm, ctx_ref), (x_hbm, x_ref), (vec_hbm, vec_ref))]
        inner.load((0, 1), s, pieces[:count], (w_out, w_in), inner_sems)
        outer.load((0,), s, pieces[count:], (w_outer,), outer_sems)
        later = [copies.start(bias_hbm, bias_ref), copies.start(g_hbm, g_ref)]
        sum_ref[...] = jnp.zeros_like(sum_ref)
        copies.wait(*loads)
        inner.wait_one(0, (w_out,), inner_sems)
        copies.start(w_out, w_out_hbm)
        hidden = x_ref[...].astype(F32) + dot(ctx_ref[...], w_out[...]) + vec_ref[2:3, :]
        hid_ref[...] = hidden
        hidden_out = copies.start(hid_ref, hid_hbm)
        normed, _ = norm(hidden)
        first = normed * vec_ref[3:4, :] + vec_ref[4:5, :]
        low_ref[...] = first.astype(BF)
        low_out = copies.start(low_ref, low_hbm)
        total[...] = first + vec_ref[5:6, :]
        inner.wait_one(1, (w_out, w_in), inner_sems)
        copies.start(w_in, w_in_hbm)
        outer.wait_one(0, (w_outer,), outer_sems)
        copies.start(w_outer, w_outer_hbm)
        copies.wait(*later)
        for c in range(0, ff, d):
            cols = slice(c, c + d)
            act, slope = gelu_parts(dot(low_ref[...], w_in[:, cols]) + bias_ref[0:1, cols])
            act = act.astype(BF)
            act_ref[:, cols] = act
            slope_ref[:, cols] = slope.astype(BF)
            copies.start(slope_ref.at[:, cols], slope_hbm.at[:, cols])
            total[...] += dot(act, w_outer[cols, :])
        normed, inverse = norm(total[...])
        gain = vec_ref[6:7, :]
        x_ref[...] = (normed * gain + vec_ref[7:8, :]).astype(BF)
        copies.start(x_ref, out_hbm)
        grad = g_ref[...].astype(F32)
        sum_ref[2:3, :] = column_sum(grad * normed)
        sum_ref[3:4, :] = column_sum(grad)
        second = norm_back(grad * gain, normed, inverse)
        low = second.astype(BF)
        ctx_ref[...] = low
        copies.start(ctx_ref, grad_hbm)
        copies.wait(hidden_out)
        hid_ref[...] = second
        copies.start(hid_ref, second_hbm)
        sum_ref[4:5, :] = column_sum(low.astype(F32))
        copies.start(sum_ref, sum_hbm)
        turned = low.T
        for i in range(0, OWNERS, 2):
            grads = dot(turned, act_ref[:, i * part : (i + 2) * part]).astype(BF)
            for k in (0, 1):
                for h in (0, 1):
                    for t in range(4):
                        start = h * half + t * half // 4
                        both[(h, *spot(s, at, t, i + k))] = grads[
                            start : start + half // 4, k * part : (k + 1) * part
                        ]
            z = spot(s, at, 0, i)[3]
            copies.start(both.at[1 - core, :, :, :, z], other_hbm.at[:, :, :, z])
            copies.start(both.at[core, :, :, :, z], mine_hbm.at[:, :, :, z])
        copies.end()

    row = vmem(tok, d)
    return pallas(
        body,
        "forward_block",
        table,
        [context, tokens, out_grad, vectors, bias_inner] + extra,
        outs,
        [row, row, row, vmem(8, d, dtype=F32), vmem(8, ff, dtype=F32), vmem(tok, d, dtype=F32), row]
        + [vmem(tok, ff), vmem(tok, ff), vmem(tok, d, dtype=F32), vmem(SUMS, d, dtype=F32)]
        + [vmem(2, *place)]
        + inner.scratch((0, 1))
        + outer.scratch((0,)),
        2 * tok * d * (d + 3 * ff),
        62,
    )


def active_back(choice, grad_low, slope, w_outer, first_low):
    tok, d = grad_low.shape
    ff = slope.shape[1]
    blocks = [slice(c, c + d) for c in range(0, ff, d)]
    half, rows, part = len(blocks) // 2, d // OWNERS, d // 2

    def body(s, g_hbm, slope_hbm, w_hbm, low_hbm, out_hbm, sum_hbm, mine_hbm, other_hbm, *refs):
        g_ref, slope_ref, w_ref, low_ref, out_ref, sum_ref, turned, held, sems = refs
        copies = Copies(sems)
        first = copies.start(g_hbm, g_ref)
        loads = [
            (copies.start(w_hbm.at[b, :], w_ref.at[b, :]), copies.start(slope_hbm.at[:, b], slope_ref.at[:, b]))
            for b in blocks
        ]
        left = copies.start(low_hbm, low_ref)
        sum_ref[...] = jnp.zeros_like(sum_ref)
        copies.wait(first)
        for n, b in enumerate(blocks):
            copies.wait(*loads[n])
            low = (dot_right(g_ref[...], w_ref[b, :]) * slope_ref[:, b].astype(F32)).astype(BF)
            out_ref[:, b] = low
            copies.start(out_ref.at[:, b], out_hbm.at[:, b])
            sum_ref[8 + n : 9 + n, :] = column_sum(low.astype(F32))
            if n == 0:
                copies.wait(left)
                turned[...] = low_ref[...].T
            grads = dot(turned[...], low).astype(BF)
            for k in (0, 1):
                for j in range(OWNERS):
                    held[(n // half, *spot(s, 0, n % half * 2 + k, j))] = grads[
                        j * rows : (j + 1) * rows, k * part : (k + 1) * part
                    ]
            if n % half == half - 1:
                copies.either(s[0] == n // half, held.at[n // half], mine_hbm, other_hbm)
        copies.start(sum_ref, sum_hbm)
        copies.end()

    grad = struct((*PLACES, rows, part), BF)
    return pallas(
        body,
        "active_back",
        choice,
        [grad_low, slope, w_outer, first_low],
        [struct((tok, ff), BF), struct((SUMS, d), F32), grad, grad],
        [vmem(tok, d), vmem(tok, ff), vmem(ff, d), vmem(tok, d), vmem(tok, ff), vmem(SUMS, d, dtype=F32)]
        + [vmem(d, tok), vmem(2, *grad.shape)],
        4 * tok * d * ff,
    )


def inner_back(choice, grad_inner, grad_second, hidden, vectors, w_out, w_in, context):
    tok, d = hidden.shape
    ff, half = grad_inner.shape[1], d // 2
    blocks = [slice(0, d), slice(d, 2 * d), slice(2 * d, ff)]

    def body(s, g_hbm, second_hbm, hid_hbm, vec_hbm, w_out_hbm, w_in_hbm, *refs):
        left_hbm, out_hbm, ctx_hbm, sum_hbm, mine_hbm, other_hbm = refs[:6]
        g_ref, second_ref, hid_ref, vec_ref, w_out, w_in, left_ref, ctx_ref, sum_ref, held, sems = refs[6:]
        copies = Copies(sems)
        loads = [
            (copies.start(g_hbm.at[:, b], g_ref.at[:, b]), copies.start(w_in_hbm.at[:, b], w_in.at[:, b]))
            for b in blocks[:1]
        ]
        first = copies.start(second_hbm, second_ref)
        loads += [
            (copies.start(g_hbm.at[:, b], g_ref.at[:, b]), copies.start(w_in_hbm.at[:, b], w_in.at[:, b]))
            for b in blocks[1:]
        ]
        later = [copies.start(a, b) for a, b in ((hid_hbm, hid_ref), (vec_hbm, vec_ref), (w_out_hbm, w_out))]
        later.append(copies.start(left_hbm, left_ref))
        sum_ref[...] = jnp.zeros_like(sum_ref)
        for n, b in enumerate(blocks):
            copies.wait(*loads[n])
            part = dot_right(g_ref[:, b], w_in[:, b])
            if n == 0:
                copies.wait(first)
            second_ref[...] += part
        copies.wait(*later)
        grad = second_ref[...]
        normed, inverse = norm(hid_ref[...])
        sum_ref[5:6, :] = column_sum(grad * normed)
        sum_ref[6:7, :] = column_sum(grad)
        hidden_grad = norm_back(grad * vec_ref[3:4, :], normed, inverse)
        second_ref[...] = hidden_grad
        copies.start(second_ref, out_hbm)
        low = hidden_grad.astype(BF)
        ctx_ref[...] = dot_right(low, w_out[...]).astype(BF)
        copies.start(ctx_ref, ctx_hbm)
        grads = dot(left_ref[...].T, low).astype(BF)
        for k in (0, 1):
            held[k] = grads[:, k * half : (k + 1) * half].reshape(OWNERS, d // OWNERS, half)
        copies.start(held.at[1 - s[0]], other_hbm)
        copies.start(held.at[s[0]], mine_hbm)
        sum_ref[7:8, :] = column_sum(low.astype(F32))
        copies.start(sum_ref, sum_hbm)
        copies.end()

    full, grad = vmem(tok, d, dtype=F32), struct((OWNERS, d // OWNERS, half), BF)
    return pallas(
        body,
        "inner_back",
        choice,
        [grad_inner, grad_second, hidden, vectors, w_out, w_in, context],
        [struct((tok, d), F32), struct((tok, d), BF), struct((SUMS, d), F32), grad, grad],
        [vmem(tok, ff), full, full, vmem(8, d, dtype=F32), vmem(d, d), vmem(d, ff), vmem(tok, d), vmem(tok, d)]
        + [vmem(SUMS, d, dtype=F32), vmem(2, *grad.shape)],
        2 * tok * d * (2 * d + ff),
    )


def tokens_back(choice, grad_hidden, mine, other, weights):
    tok, d = grad_hidden.shape
    half = d // 2

    def body(s, hid_hbm, mine_hbm, other_hbm, *refs):
        weights, out_hbm, hid_ref, grad_ref, w_ref, out_ref, sems = refs[:3], *refs[3:]
        copies = Copies(sems)
        loads = []
        for n, weight in enumerate(weights):
            loads.append([copies.start(weight, w_ref.at[n])])
            for grad, side in ((other_hbm, 1 - s[0]), (mine_hbm, s[0])):
                cols = pl.ds(pl.multiple_of(side * half, half), half)
                loads[-1].append(
                    copies.start(grad.at[:, n * half : (n + 1) * half], grad_ref.at[n, :, cols])
                )
            if n == 0:
                first = copies.start(hid_hbm, hid_ref)
        for n, load in enumerate(loads):
            copies.wait(*load)
            part = dot_right(grad_ref[n], w_ref[n])
            copies.wait(first)
            if n < 2:
                hid_ref[...] += part
            else:
                out_ref[...] = (hid_ref[...] + part).astype(BF)
        copies.start(out_ref, out_hbm)
        copies.end()

    return pallas(
        body,
        "tokens_back",
        choice,
        [grad_hidden, mine, other, *weights],
        [struct((tok, d), BF)],
        [vmem(tok, d, dtype=F32), vmem(3, tok, d), vmem(3, d, d), vmem(tok, d)],
        6 * tok * d * d,
    )[0]


def join(choice, mine, mate):
    rows, half = mine.shape[0] // 4, mine.shape[1]

    def body(s, mine_hbm, mate_hbm, *refs):
        outs, (both, held, sems) = refs[:4], refs[4:]
        copies = Copies(sems)
        copies.start(mine_hbm, both.at[s[0]])
        copies.start(mate_hbm, both.at[1 - s[0]])
        copies.end()
        for n, out in enumerate(outs):
            for k in (0, 1):
                held[n, :, k * half : (k + 1) * half] = both[k, n * rows : (n + 1) * rows, :].astype(F32)
            copies.start(held.at[n], out)
        copies.end()

    return pallas(
        body,
        "join",
        choice,
        [mine, mate],
        [struct((rows, 2 * half), F32)] * 4,
        [vmem(2, *mine.shape), vmem(4, rows, 2 * half, dtype=F32)],
        1,
    )


def axis_step(value, axis):
    if axis == "x":
        return rep_step(value, 2)
    return lax.ppermute(value, "fsdp", [(f, f ^ 1) for f in range(8)])


def after(value, *events):
    return lax.optimization_barrier((value,) + events)[0] if events else value


def added(*terms):
    total = terms[0].astype(F32)
    for term in terms[1:]:
        total = total + term.astype(F32)
    return total.astype(BF)


def chosen(parts, bit, axis):
    return lax.dynamic_index_in_dim(parts, bit, axis, keepdims=False)


class Owned:
    def __init__(self, place, mine, received):
        self.place, self.mine, self.received = place, mine, received

    def first(self, *events):
        received = after(self.received, *events)
        sent = [added(self.mine[n, 1], received[n, 1]) for n in (0, 1)]
        moved = [axis_step(v, axis) for v, axis in zip(sent, "xy")]
        self.terms = [[self.mine[n, 0], received[n, 0], moved[n]] for n in (0, 1)]
        return sent

    def second(self, *events):
        terms = [t[:-1] + [after(t[-1], *events)] for t in self.terms]
        sent = [added(*(v[1] for v in t)) for t in terms]
        moved = [axis_step(v, axis) for v, axis in zip(sent, "yx")]
        self.terms = [[v[0] for v in t] + [m] for t, m in zip(terms, moved)]
        return sent

    def third(self, *events):
        sums = [added(*t[:-1], after(t[-1], *events)) for t in self.terms]
        parts = jnp.concatenate(sums, 1)
        moved = [
            lax.ppermute(parts[k], "fsdp", [(f, (f // 2 + k) % 4 * 2 + f % 2) for f in range(8)])
            for k in (1, 3, 2)
        ]
        self.terms = [parts[0]] + moved
        return [parts[k] for k in (1, 3, 2)]

    def fourth(self, *events):
        self.own = added(*self.terms[:-1], after(self.terms[-1], *events))
        self.other = rep_step(self.own, 2)
        return [self.own]

    def fifth(self, *events):
        other = after(self.other, *events)
        low = jnp.where(self.place.x == 0, self.own, other)
        high = jnp.where(self.place.x == 0, other, self.own)
        mid = low.shape[0] // 2
        half = jnp.concatenate([low[:mid], high[:mid], low[mid:], high[mid:]], 0)
        self.both = (half, rep_step(half, 1))
        return [half]

    def last(self):
        mine, mate = self.both
        first = self.place.core == 0
        return jnp.where(first, mine, mate), jnp.where(first, mate, mine)


class Place:
    def __init__(self, mesh):
        f, r = lax.axis_index("fsdp"), lax.axis_index("rep")
        self.f, self.core, self.x = f, r % 2, r // 2
        self.y, self.z = f % 2, f // 2
        self.choice = jnp.stack([self.core, self.x, self.y, self.z]).astype(jnp.int32)
        if mesh.shape["fsdp"] == len(RING):
            row = lax.dynamic_index_in_dim(jnp.array(ring_table(), jnp.int32), f, 0, keepdims=False)
            self.table = jnp.concatenate([row, self.core[None].astype(jnp.int32)])
        else:
            self.table = jnp.zeros((1,), jnp.int32)


class Ring:
    def __init__(self, group, payload, last):
        self.group, self.ways, self.last, self.count = group, {1: [payload], -1: [payload]}, last, 0

    def ways_of(self, count):
        return (1, -1) if count < len(RING) // 2 else (self.last,)

    def source(self, way, count):
        return count if way == 1 or count == len(RING) // 2 else len(RING) // 2 + count

    @property
    def came(self):
        return tuple(self.ways[way][self.count] for way in self.ways_of(self.count))

    def step(self, *events):
        self.count += 1
        for way in self.ways_of(self.count):
            self.ways[way].append(ring_step(after(self.ways[way][-1], *events), way))
            self.group.pieces.append((self.ways[way][-1], (self.source(way, self.count),), False))

    def share(self, count, *events):
        shared = []
        for way in self.ways_of(count):
            shared.append(rep_step(after(self.ways[way][count], *events), 1))
            self.group.pieces.append((shared[-1], (self.source(way, count),), True))
        return shared


class Travel:
    def __init__(self, rings):
        self.rings, self.going, self.shared, self.seen = rings, (), (), ()

    def round(self, *order, events=()):
        came = tuple(v for n in self.going for v in self.rings[n].came)
        counts = [(n, self.rings[n].count) for n in self.going]
        self.seen = came + self.shared
        for n in order:
            self.rings[n].step(*events, *self.seen)
        self.shared = tuple(v for n, count in counts for v in self.rings[n].share(count, *events, *came))
        self.going = order

    def finish(self, *events):
        for n in self.going:
            self.rings[n].share(self.rings[n].count, *events)


def local(mesh, *args):
    (
        tokens, seq_ids, key_mask, weight_query, bias_query, weight_key, weight_value, bias_value,
        weight_out, bias_out, norm1_gain, norm1_bias, weight_inner, bias_inner, weight_outer, bias_outer,
        norm2_gain, norm2_bias, out_grad,
    ) = args
    place = Place(mesh)
    choice, table = place.choice, place.table
    fsdp = mesh.shape["fsdp"]
    d = tokens.shape[1]
    win = windows(seq_ids[0])
    narrow = [bias_query, bias_value, bias_out, norm1_gain, norm1_bias, bias_outer, norm2_gain, norm2_bias]
    shards = [[weight_query, weight_key, weight_value], [weight_out, weight_inner], [weight_outer]]
    fast = all(fast_path(mesh, s) for s in shards)
    if fast:
        groups = [Group(mesh, s) for s in shards]
        packed = pack(choice, groups, narrow + [bias_inner])
        rings = [Ring(g, p, way) for g, p, way in zip(groups, packed, (1, -1, 1))]
        small = packed[0]
        travel = Travel(rings)
        travel.round(0, 1)
        travel.round(0, 2)
        travel.round(0, 1)
        travel.round(0, 2)
        travel.round(1, 2)
    else:
        groups = [Group(mesh, [lax.all_gather(w, "fsdp", axis=0, tiled=True) for w in s]) for s in shards]
        rows = [jnp.concatenate(narrow), bias_inner]
        rows = [jnp.concatenate([r, jnp.zeros((d - r.size,), BF)])[None] for r in rows]
        small = jnp.concatenate(rows + [jnp.zeros((SMALL - 2, d), BF)], 0)
        small = lax.all_gather(small, "fsdp", axis=0, tiled=False)
    qkv, inner_group, outer_group = groups

    q, k, v, vectors, full_bias_inner, *weights = project(table, qkv, tokens, small)
    if fast:
        travel.round(1, 2, events=(q,))
        q = after(q, *travel.seen)
    context, probs = attend(win, seq_ids, key_mask, q, k, v)
    if fast:
        travel.finish(context)
    (
        layer_out, hidden, first_low, slope, grad_second, grad_outer, sums2, outer_mine, outer_other,
        w_out, w_in, w_outer,
    ) = forward_block(
        place_table(table, choice), inner_group, outer_group, context, tokens, out_grad, vectors, full_bias_inner
    )
    if not fast:
        choice = jnp.zeros((4,), jnp.int32)
    if fast:
        outer_sum = Owned(place, outer_mine, rep_step(outer_other, 1))
    grad_inner, sums_inner, inner_mine, inner_other = active_back(choice, grad_outer, slope, w_outer, first_low)
    if fast:
        inner_sum = Owned(place, inner_mine, rep_step(inner_other, 1))
        event = outer_sum.first(inner_mine)
        grad_inner = after(grad_inner, *event)
    grad_hidden, grad_context, sums1, out_mine, out_other = inner_back(
        choice, grad_inner, grad_second, hidden, vectors, w_out, w_in, context
    )
    if fast:
        event = outer_sum.second(out_mine)
        event += inner_sum.first(out_mine)
        grad_context = after(grad_context, *event)
    place_win = jnp.concatenate([choice, win])
    grads_other, sums_other, query_other = attend_back(
        place_win, 1, q, k, v, context, grad_context, probs, tokens, out_other
    )
    if fast:
        event = inner_sum.second(grads_other)
        event += outer_sum.third(grads_other)
        query_came = rep_step(after(query_other, *event), 1)
        grad_context = after(grad_context, *event)
    grads_mine, sums_mine, query_mine = attend_back(
        place_win, 0, q, k, v, context, grad_context, probs, tokens, out_mine
    )
    sums_att = by_core(choice[0], sums_mine, sums_other, 1)
    sums = sums1 + sums2 + sums_inner + sums_att
    if fast:
        query_sum = Owned(place, query_mine, query_came)
        event = query_sum.first(query_mine)
        event += inner_sum.third(*event)
        sums = sums + after(rep_step(sums, 1), *event)
        event += outer_sum.fourth(*event)
        event = query_sum.second(*event)
        sums = sums + after(rep_step(sums, 2), *event)
        event += outer_sum.fifth(*event)
        event += inner_sum.fourth(*event)
        event = query_sum.third(*event)
        sums = sums + after(axis_step(sums, "y"), *event)
        grad_hidden = after(grad_hidden, *event)
    grad_tokens = tokens_back(choice, grad_hidden, grads_mine, grads_other, weights)
    if fast:
        sums = sums + after(z_step(sums, 1), grad_tokens)
        sums = sums + after(z_step(sums, 2), grad_tokens)
        event = query_sum.fourth(grad_tokens)
        event += inner_sum.fifth(*event)
        low, high = outer_sum.last()
        final_outer = jnp.concatenate([low, high], 0).T.astype(F32)
        query_sum.fifth(final_outer, *event)
        low, high = inner_sum.last()
        rows = d // fsdp
        blocks = [v[c : c + rows] for v in (low, high) for c in range(0, v.shape[0], rows)]
        final_inner = jnp.concatenate(blocks, 1).astype(F32)
        final_query, final_key, final_value, final_out = join(choice, *query_sum.both)
    else:

        def plain(*blocks):
            total = jnp.concatenate(blocks, 2)
            total = total.reshape(-1, total.shape[2])
            owned = lax.psum_scatter(total, "fsdp", scatter_dimension=0, tiled=True)
            return lax.psum(owned, "rep").astype(F32)

        sums = lax.psum(sums, ("fsdp", "rep"))
        def straight(v):
            by_x, by_y = v[0].transpose(2, 1, 0, 3, 4), v[1].transpose(2, 0, 1, 3, 4)
            return jnp.concatenate([w.reshape(OWNERS, -1, w.shape[4]) for w in (by_x, by_y)], 1)

        outer_mine, outer_other, inner_mine, inner_other, query_mine, query_other = (
            straight(v) for v in (outer_mine, outer_other, inner_mine, inner_other, query_mine, query_other)
        )
        final_outer = plain(jnp.concatenate([outer_mine, outer_other], 1).transpose(0, 2, 1))
        part = d // OWNERS
        unstack = lambda v: [v[:, c : c + part] for c in range(0, v.shape[1], part)]
        final_inner = plain(*unstack(inner_mine), *unstack(inner_other))
        final_query, final_key, final_value, final_out = (
            plain(a, b) for a, b in zip(unstack(query_mine), unstack(query_other))
        )

    narrow_sums = lax.dynamic_slice_in_dim(sums, place.f * (d // fsdp), d // fsdp, 1)
    inner_sums = lax.dynamic_slice_in_dim(sums[8:12].reshape(-1), place.f * bias_inner.size, bias_inner.size, 0)
    return (
        layer_out,
        grad_tokens,
        final_query,
        narrow_sums[0],
        final_key,
        final_value,
        narrow_sums[1],
        final_out,
        narrow_sums[7],
        narrow_sums[5],
        narrow_sums[6],
        final_inner,
        inner_sums,
        final_outer,
        narrow_sums[4],
        narrow_sums[2],
        narrow_sums[3],
    )


def by_core(core, mine, other, axis):
    return jnp.where(core == 0, jnp.concatenate([mine, other], axis), jnp.concatenate([other, mine], axis))


def z_step(value, bits):
    return lax.ppermute(value, "fsdp", [(f, f ^ (2 * bits)) for f in range(8)])


def place_table(table, choice):
    return jnp.concatenate([table[:-1], choice]) if table.shape[0] > 1 else jnp.zeros((4,), jnp.int32)


def solution(mesh):
    rows, shard, part = P(("fsdp", "rep"), None), P("fsdp", None), P("fsdp")
    return jax.shard_map(
        functools.partial(local, mesh),
        mesh=mesh,
        in_specs=(
            rows, rows, rows, shard, part, shard, shard, part, shard, part, part, part, shard, part, shard,
            part, part, part, rows,
        ),
        out_specs=(
            rows, rows, shard, part, shard, shard, part, shard, part, part, part, shard, part, shard, part,
            part, part,
        ),
        check_vma=False,
    )
```
